128 devices in a mesh: ctx: 16 (over y, z_hi, core), fsdp: 8 (over x, z_lo).
Axes of the slice: x: 4, y: 4, z: 4 (z_hi: 2, z_lo: 2; z = z_hi * 2 + z_lo), core: 2. Of those that a mesh axis runs over, the one named last changes fastest.
Arguments:
- tokens: bfloat16 [8, 2048, 7168], P('fsdp', 'ctx'), may hold values from -16 to 16
- kv_weight: bfloat16 [7168, 576], P('fsdp'), may hold values from -0.0625 to 0.0625
- latent_gain: float32 [512], replicated, may hold values from 0.1 to 1.9
- queries: bfloat16 [8, 2048, 32, 576], P('fsdp', 'ctx'), may hold values from -40 to 40
- out_grad: bfloat16 [8, 2048, 32, 512], P('fsdp', 'ctx'), may hold values from -6 to 6
- segment_ids: int32 [8, 2048], P('fsdp', 'ctx'), may hold values from 0 to 7, never falling along the last dimension, each value on 1 to 1024 neighbouring positions
Outputs:
- attended: bfloat16 [8, 2048, 32, 512], P('fsdp', 'ctx')
- logit_max: float32 [32], replicated
- update: float32 [7168, 576], P(('ctx', 'fsdp'))
The draws below stay inside these ranges and needn't reach their ends.
Inputs may be any that keep to these rules, and one draw needn't show every extreme that they name: `segment_ids`: within each rollout the document numbers never fall; each document holds 1 to 1024 positions, and one holds exactly 1024.
All inputs are finite; a program needn't handle non-finite values.
Results may differ from the reference program's by a relative error of at most 0.022.
Values may be sent and summed in bfloat16 or wider, within the bound.
A program may use at most 320 MiB of HBM per device.

```python
import math
import jax
import jax.numpy as jnp
import numpy as np
from jax import lax

D = 7168
LAT = 512
ROPE = 64
HEADS = 32
DOCS = 8
NS_ITERS = 5
SEQ_LEN = 2048
SEQS = 8


def draw_tokens(key, part):
    key = jax.random.fold_in(key, 23)
    shape = (SEQS, SEQ_LEN, D)
    along = jnp.arange(D, dtype=jnp.float32) / (D - 1)
    ramp = 1.0 + 1.5 * along
    values = jax.random.normal(key, shape, jnp.float32) * ramp[None, None, :]
    return jnp.clip(values, -16.0, 16.0).astype(jnp.bfloat16)


def draw_queries(key, part):
    key = jax.random.fold_in(key, 11)
    shape = (SEQS, SEQ_LEN, HEADS, LAT + ROPE)
    along = jnp.arange(SEQ_LEN, dtype=jnp.float32) / SEQ_LEN
    across = jnp.arange(SEQS, dtype=jnp.float32) / max(SEQS - 1, 1)
    ramp = 0.3 * (1.0 + 2.0 * along)[None, :, None, None] * (1.0 + 2.0 * across)[:, None, None, None]
    values = jax.random.normal(key, shape, jnp.float32) * ramp
    return jnp.clip(values, -40.0, 40.0).astype(jnp.bfloat16)


def levels(own_key, extent, cuts, low, high):
    factor_of = 1.0
    for position, parts in cuts:
        draws = jax.random.uniform(jax.random.fold_in(jax.random.fold_in(own_key, 6), position), (parts,), jnp.float32, low / len(cuts), high / len(cuts))
        factor_of = factor_of * jnp.repeat(jnp.exp(draws), extent[position] // parts).reshape((-1,) + (1,) * (len(extent) - 1 - position))
    return factor_of


def split_up(count, total, bound, slope):
    weights = [(1 << 20) // math.isqrt(standing ** slope) + 1 for standing in range(2, count + 1)]
    spare, holding = total - bound - (count - 1), [1] * (count - 1)
    while spare > 0:
        candidates = [i for i in range(count - 1) if holding[i] < bound]
        pool, remaining = sum([weights[i] for i in candidates]), spare
        for i in candidates:
            extra = min(bound - holding[i], max(1, remaining * weights[i] // pool), spare)
            holding[i] = holding[i] + extra
            spare = spare - extra
    return np.array([bound] + holding)


def ragged_sizes(rng, count, total, limit, slope):
    if count == 2:
        one = jax.random.randint(rng, (), max(1, total - limit), min(limit, total - 1) + 1)
        return jnp.stack([one, total - one])
    tallies = jnp.asarray(split_up(count, total, limit, slope), jnp.int32)
    pairs = (count - 1) // 2
    giver, taker = tallies[1:1 + 2 * pairs:2], tallies[2:2 + 2 * pairs:2]
    slack = jnp.minimum(giver - 1, limit - taker)
    moved = jax.random.randint(jax.random.fold_in(rng, 1), (pairs,), 0, 1 << 20) % (slack + 1)
    tallies = tallies.at[1:1 + 2 * pairs:2].set(giver - moved).at[2:2 + 2 * pairs:2].set(taker + moved)
    return tallies[jax.random.permutation(jax.random.fold_in(rng, 2), count)]


def scatter_about(rng, extent, deviation, limit, pieces=(), kind=jnp.bfloat16):
    array = jax.random.normal(rng, extent, jnp.float32) * deviation
    if len(pieces) > 0:
        array = levels(rng, extent, pieces, -0.22, 0.18) * array
    return jnp.clip(array, min=-limit, max=limit).astype(kind)


def setup_inputs(seed: int = 0) -> dict:
    key_list = jax.random.split(jax.random.key(seed), 7)
    tokens = draw_tokens(jax.random.fold_in(key_list[6], 71), 0)
    kv_weight = scatter_about(key_list[1], (D, LAT + ROPE), D ** -0.5, 0.0625, ((0, 8),))
    latent_gain = jnp.clip(1.0 + 0.18 * jax.random.normal(key_list[2], (LAT,), jnp.float32), 0.1, 1.9)
    queries = draw_queries(jax.random.fold_in(key_list[6], 71), 0)
    out_grad = scatter_about(key_list[4], (SEQS, SEQ_LEN, HEADS, LAT), 1.0, 6.0, ((0, 8), (1, 16)))
    segment_ids = jax.vmap(lambda own: jnp.searchsorted(jnp.cumsum(ragged_sizes(own, DOCS, SEQ_LEN, SEQ_LEN // 2, 2)), jnp.arange(SEQ_LEN), side="right"))(jax.random.split(key_list[5], SEQS)).reshape((SEQS, SEQ_LEN)).astype(jnp.int32)
    return {"tokens": tokens, "kv_weight": kv_weight, "latent_gain": latent_gain, "queries": queries, "out_grad": out_grad, "segment_ids": segment_ids}


attn_scale = 192.0 ** (-0.5)
masked_score = -1e+30
rope_base = 50000.0
quintic_a = 3.4445
quintic_b = -4.775
quintic_c = 2.0315

def rope_tables(positions):
    ladder = jnp.arange(ROPE // 2, dtype=jnp.float32)
    freqs = jnp.power(rope_base, -2.0 * ladder / ROPE)
    angles = positions.astype(jnp.float32)[:, None] * freqs[None, :]
    return (jnp.cos(angles), jnp.sin(angles))

def one_sequence(rows_x, kv_weight, latent_gain, query_rows, grad_out, doc_ids):
    half_rope = ROPE // 2
    projected = jnp.dot(rows_x, kv_weight, preferred_element_type=jnp.float32)
    compressed = projected[:, :LAT]
    inverse = lax.rsqrt(lax.optimization_barrier(jnp.mean(compressed * compressed, axis=1)) + 1e-06)
    latent = compressed * inverse[:, None] * latent_gain[None, :]
    rope_cos, rope_sin = rope_tables(jnp.arange(SEQ_LEN, dtype=jnp.int32))
    rope_first = projected[:, LAT:LAT + half_rope]
    rope_second = projected[:, LAT + half_rope:]
    keys = jnp.concatenate([latent, rope_first * rope_cos - rope_second * rope_sin, rope_second * rope_cos + rope_first * rope_sin], axis=1).astype(jnp.bfloat16)
    block_rows = math.gcd(SEQ_LEN, 512)
    key_grad = jnp.zeros((SEQ_LEN, LAT + ROPE), jnp.float32)
    attended_parts = []
    peak_parts = []
    for index in range(SEQ_LEN // block_rows):
        low = index * block_rows
        high = low + block_rows
        query_part = query_rows[low:high].astype(jnp.float32)
        keys_part = keys[:high].astype(jnp.float32)
        raw_scores = jnp.einsum('ihe,je->hij', query_part, keys_part, precision=lax.Precision.HIGHEST) * attn_scale
        query_pos = jnp.arange(low, high, dtype=jnp.int32)
        key_pos = jnp.arange(high, dtype=jnp.int32)
        allowed = (key_pos[None, :] <= query_pos[:, None]) & (doc_ids[:high][None, :] == doc_ids[low:high][:, None])
        scores = jnp.where(allowed[None], raw_scores, masked_score)
        row_peak = lax.optimization_barrier(jnp.max(scores, axis=2))
        exps = jnp.exp(scores - row_peak[:, :, None])
        row_total = lax.optimization_barrier(jnp.sum(exps, axis=2))
        weights = exps / row_total[:, :, None]
        rounded = lax.optimization_barrier(weights.astype(jnp.bfloat16)).astype(jnp.float32)
        attended_part = jnp.einsum('hij,je->ihe', rounded, keys_part[:, :LAT], precision=lax.Precision.HIGHEST).astype(jnp.bfloat16)
        grad_part = grad_out[low:high].astype(jnp.float32)
        row_delta = lax.optimization_barrier(jnp.sum(grad_part * attended_part.astype(jnp.float32), axis=2)).T
        dprob = jnp.einsum('ihe,je->hij', grad_part, keys_part[:, :LAT], precision=lax.Precision.HIGHEST)
        dscore = (weights * (dprob - row_delta[:, :, None]) * attn_scale).astype(jnp.bfloat16)
        dscore = lax.optimization_barrier(dscore).astype(jnp.float32)
        from_scores = jnp.einsum('hij,ihe->je', dscore, query_part, precision=lax.Precision.HIGHEST)
        from_values = jnp.einsum('hij,ihe->je', rounded, grad_part, precision=lax.Precision.HIGHEST)
        grads = from_scores + jnp.concatenate([from_values, jnp.zeros((high, ROPE), jnp.float32)], axis=1)
        key_grad = key_grad.at[:high].add(grads)
        attended_parts.append(attended_part)
        peak_parts.append(lax.optimization_barrier(jnp.max(row_peak, axis=1)))
    grad_first = key_grad[:, LAT:LAT + half_rope]
    grad_second = key_grad[:, LAT + half_rope:]
    d_first = grad_first * rope_cos + grad_second * rope_sin
    d_second = -grad_first * rope_sin + grad_second * rope_cos
    scaled = key_grad[:, :LAT] * latent_gain[None, :]
    inner = lax.optimization_barrier(jnp.mean(compressed * scaled, axis=1))
    d_comp = inverse[:, None] * (scaled - compressed * (inverse * inverse * inner)[:, None])
    kv_grad = jnp.concatenate([d_comp, d_first, d_second], axis=1).astype(jnp.bfloat16)
    weight_grad = jnp.dot(rows_x.T, kv_grad, preferred_element_type=jnp.float32)
    attended = jnp.concatenate(attended_parts, axis=0)
    peak = lax.optimization_barrier(jnp.max(jnp.stack(peak_parts, axis=0), axis=0))
    return (attended, peak, weight_grad)

def reference(tokens, kv_weight, latent_gain, queries, out_grad, segment_ids):
    attended_all = []
    peaks = []
    weight_grad = jnp.zeros((D, LAT + ROPE), jnp.float32)
    for seq in range(SEQS):
        attended, peak, partial_grad = one_sequence(tokens[seq], kv_weight, latent_gain, queries[seq], out_grad[seq], segment_ids[seq])
        attended_all.append(attended)
        peaks.append(peak)
        weight_grad = weight_grad + partial_grad
    logit_max = lax.optimization_barrier(jnp.max(jnp.stack(peaks, axis=0), axis=0))
    frob_norm = jnp.sqrt(jnp.sum(weight_grad * weight_grad)) + 1e-07
    iterate = weight_grad / frob_norm
    for iteration in range(NS_ITERS):
        gram_matrix = jnp.dot(iterate.T, iterate, precision=lax.Precision.HIGHEST)
        mixing = quintic_b * gram_matrix + quintic_c * jnp.dot(gram_matrix, gram_matrix, precision=lax.Precision.HIGHEST)
        iterate = quintic_a * iterate + jnp.dot(iterate, mixing, precision=lax.Precision.HIGHEST)
    update = 0.2 * math.sqrt(D) * iterate
    return (jnp.stack(attended_all, axis=0), logit_max, update)
```

```python
import functools
import math

import jax
import jax.numpy as jnp
from jax import lax
from jax.experimental import pallas as pl
from jax.experimental.pallas import tpu as pltpu
from jax.sharding import PartitionSpec as P

D = 7168
LAT = 512
ROPE = 64
HEADS = 32
NS_ITERS = 5
KV = LAT + ROPE
PAD = 640
HALF = ROPE // 2
BLOCK = 128
REACH = 8
SLOTS = REACH + 2
WINDOW = SLOTS * BLOCK
CHUNK = 256
CHUNKS = WINDOW // CHUNK
CTX = 16
FSDP = 8
SHARD = D // FSDP
PIECE = SHARD // CTX
TILE_Q = 16
ROWS = TILE_Q * HEADS
TILES = BLOCK // TILE_Q

attn_scale = 192.0 ** (-0.5)
rope_base = 50000.0
quintic_a = 3.4445
quintic_b = -4.775
quintic_c = 2.0315
BIG = -1e30
MiB = 1 << 20

MESH = pl.DeviceIdType.MESH
VMEM = pl.BlockSpec(memory_space=pltpu.VMEM)
f32, bf16 = jnp.float32, jnp.bfloat16


def rope_tables(positions):
    ladder = jnp.arange(HALF, dtype=f32)
    freqs = jnp.power(rope_base, -2.0 * ladder / ROPE)
    angles = positions.astype(f32)[:, None] * freqs[None, :]
    return (jnp.cos(angles), jnp.sin(angles))


def nn(a, b, **kw):
    return lax.dot_general(a, b, (((1,), (0,)), ((), ())), preferred_element_type=f32, **kw)


def nt(a, b, **kw):
    return lax.dot_general(a, b, (((1,), (1,)), ((), ())), preferred_element_type=f32, **kw)


def tn(a, b, **kw):
    return lax.dot_general(a, b, (((0,), (0,)), ((), ())), preferred_element_type=f32, **kw)


class Place:
    def __init__(self):
        self.c, self.f = lax.axis_index("ctx"), lax.axis_index("fsdp")
        self.y, self.zh, self.k = self.c // 4, (self.c // 2) % 2, self.c % 2
        self.x, self.zl = self.f // 2, self.f % 2

    def at(self, x=None, y=None, zh=None, zl=None, k=None):
        x = self.x if x is None else x
        y = self.y if y is None else y
        zh = self.zh if zh is None else zh
        zl = self.zl if zl is None else zl
        k = self.k if k is None else k
        return ((y * 2 + zh) * 2 + k, x * 2 + zl)

    def ctx(self, c):
        return (c, self.f)

    def fsdp(self, f):
        return (self.c, f)


def greet(devices, others=0):
    barrier = pltpu.get_barrier_semaphore()
    for device in devices:
        pl.semaphore_signal(barrier, inc=1, device_id=device, device_id_type=MESH)
    pl.semaphore_wait(barrier, len(devices) + others)


def send(src, dst, send_sem, recv_sem, device):
    return pltpu.make_async_remote_copy(
        src_ref=src,
        dst_ref=dst,
        send_sem=send_sem,
        recv_sem=recv_sem,
        device_id=device,
        device_id_type=MESH,
    )


def keys_kernel(tok, w, gain, hot, cos, sin, keys_out, proj_out, wall, win, ws, wr, ks, kr):
    me = Place()
    c, k, x = me.c, me.k, me.x
    sibling = me.at(k=1 - k)
    z_same, z_other = me.at(zl=1 - me.zl), me.at(zl=1 - me.zl, zh=1 - me.zh)
    x_up, x_down = me.at(x=(x + 1) % 4), me.at(x=(x + 3) % 4)
    later = [me.ctx((c + 2 * j) % CTX) for j in range(1, 5)]
    earlier = [me.ctx((c - 2 * j + CTX) % CTX) for j in range(1, 5)]
    greet([sibling, z_same, z_other, x_up, x_down] + later + earlier[:3])

    half = SHARD // 2
    quarter = half // 2
    counter = [0]

    def rows(core, q=None):
        if q is None:
            return pl.ds(pl.multiple_of(core * half, 16), half)
        return pl.ds(pl.multiple_of(core * half + q * quarter, 16), quarter)

    def post(src_f, src, core, q, device):
        i = counter[0]
        counter[0] += 1
        where = rows(core, q)
        source = w.at[where] if src is None else src.at[src_f, where]
        copy = send(source, wall.at[src_f, where], ws.at[i], wr.at[i], device)
        copy.start()
        return copy

    def shard_of(xx, zl):
        return (xx % 4) * 2 + zl

    own = me.f
    copies = []
    up = post(own, None, k, None, x_up)
    down = post(own, None, k, None, x_down)
    own_a = post(own, None, k, 0, z_same)
    own_b = post(own, None, k, 1, z_other)
    copies += [up, down, own_a, own_b]
    acc = nn(tok[:, pl.ds(pl.multiple_of(own * SHARD, 128), SHARD)], w[...])

    def forward_half(shard):
        return [
            post(shard, wall, k, 0, z_same),
            post(shard, wall, k, 1, z_other),
            post(shard, wall, k, None, sibling),
        ]

    f_prev, f_next, f_far = shard_of(x + 3, me.zl), shard_of(x + 1, me.zl), shard_of(x + 2, me.zl)
    up.wait_recv()
    relay_up = post(f_prev, wall, k, 0, x_up)
    fw_prev = forward_half(f_prev)
    down.wait_recv()
    relay_down = post(f_next, wall, k, 1, x_down)
    fw_next = forward_half(f_next)
    other = 1 - me.zl
    oz = shard_of(x, other)

    def pass_on(pair, shard):
        pair[0].wait_recv()
        a = post(shard, wall, k, 0, sibling)
        pair[1].wait_recv()
        b = post(shard, wall, k, 1, sibling)
        return [a, b]

    on_own = pass_on([own_a, own_b], oz)
    relay_up.wait_recv()
    far_a = post(f_far, wall, k, 0, z_same)
    far_sa = post(f_far, wall, k, 0, sibling)
    relay_down.wait_recv()
    far_b = post(f_far, wall, k, 1, z_other)
    far_sb = post(f_far, wall, k, 1, sibling)
    on_prev = pass_on(fw_prev[:2], shard_of(x + 3, other))
    on_next = pass_on(fw_next[:2], shard_of(x + 1, other))

    def add(total, shard):
        return total + nn(
            tok[:, pl.ds(pl.multiple_of(shard * SHARD, 128), SHARD)], wall[shard]
        )

    fw_prev[2].wait_recv()
    acc = add(acc, f_prev)
    fw_next[2].wait_recv()
    acc = add(acc, f_next)
    for copy in on_own:
        copy.wait_recv()
    acc = add(acc, oz)
    far_sa.wait_recv()
    far_sb.wait_recv()
    acc = add(acc, f_far)
    for copy in on_prev:
        copy.wait_recv()
    acc = add(acc, shard_of(x + 3, other))
    on_far = pass_on([far_a, far_b], shard_of(x + 2, other))
    for copy in on_next:
        copy.wait_recv()
    acc = add(acc, shard_of(x + 1, other))
    for copy in on_far:
        copy.wait_recv()
    acc = add(acc, shard_of(x + 2, other))

    compressed = acc[:, :LAT]
    inverse = lax.rsqrt(jnp.mean(compressed * compressed, axis=1, keepdims=True) + 1e-06)
    latent = compressed * inverse * gain[...]
    first, second = acc[:, LAT : LAT + HALF], acc[:, LAT + HALF :]
    mine = win.at[SLOTS - 1]
    mine[:, :LAT] = latent.astype(bf16)
    tail = jnp.concatenate(
        [
            first * cos[...] - second * sin[...],
            second * cos[...] + first * sin[...],
            hot[...],
        ],
        axis=1,
    )
    mine[:, LAT:] = tail.astype(bf16)
    proj_out[...] = acc

    def slot(distance):
        return SLOTS - 1 - distance

    spread = []
    for j in range(1, 5):
        copy = send(mine, win.at[slot(2 * j)], ks.at[j - 1], kr.at[j - 1], later[j - 1])
        copy.start()
        spread.append(copy)
    to_sibling = []

    def give(n):
        copy = send(
            win.at[slot(2 * n + 2 * k)], win.at[slot(2 * n + 1)], ks.at[4 + n], kr.at[4 + n], sibling
        )
        copy.start()
        to_sibling.append(copy)

    spread[0].wait_recv()
    give(0)
    give_next = 1
    for j in range(1, 4):
        spread[j].wait_recv()
        give(give_next)
        give_next += 1
    for copy in to_sibling:
        copy.wait_recv()
    lane = lax.broadcasted_iota(jnp.int32, (BLOCK, 128), 1)
    flag = jnp.where(lane == ROPE + 8, 1.0, 0.0)
    for d in range(REACH + 1):
        keys_out[slot(d)] = win[slot(d)]
        if d > 0:

            @pl.when(c < d)
            def _(d=d):
                keys_out[slot(d), :, LAT:] = flag.astype(bf16)

    keys_out[0] = jnp.zeros((BLOCK, PAD), bf16)
    keys_out[0, :, LAT:] = flag.astype(bf16)
    for copy in (
        copies
        + [relay_up, relay_down, far_a, far_b, far_sa, far_sb]
        + fw_prev
        + fw_next
        + on_own
        + on_prev
        + on_next
        + on_far
        + spread
        + to_sibling
    ):
        copy.wait_send()


N_W = 4 + 1 + 3 + 1 + 3 + 2 + 2 + 2 + 2 + 2 + 2


def make_keys(tok, w, gain, hot, cos, sin):
    return pl.pallas_call(
        keys_kernel,
        out_shape=(
            jax.ShapeDtypeStruct((SLOTS, BLOCK, PAD), bf16),
            jax.ShapeDtypeStruct((BLOCK, KV), f32),
        ),
        in_specs=[VMEM] * 6,
        out_specs=(VMEM, VMEM),
        scratch_shapes=[
            pltpu.VMEM((FSDP, SHARD, KV), bf16),
            pltpu.VMEM((SLOTS, BLOCK, PAD), bf16),
            pltpu.SemaphoreType.DMA((N_W,)),
            pltpu.SemaphoreType.DMA((N_W,)),
            pltpu.SemaphoreType.DMA((8,)),
            pltpu.SemaphoreType.DMA((8,)),
        ],
        compiler_params=pltpu.CompilerParams(
            collective_id=0, has_side_effects=True, vmem_limit_bytes=48 * MiB
        ),
        name="keys",
    )(tok, w, gain, hot, cos, sin)


def attention_kernel(
    low, q, dout, qmask, keys, att_out, grad_out, peak_out, vt, qr, s_scr, p_scr, att_t
):
    t = pl.program_id(0)
    start = low[t]

    @pl.when(t == 0)
    def _():
        grad_out[...] = jnp.zeros_like(grad_out)
        peak_out[...] = jnp.full_like(peak_out, BIG)
        for j in range(CHUNKS):
            vt[:, j * CHUNK : (j + 1) * CHUNK] = keys[j * CHUNK : (j + 1) * CHUNK, :LAT].T

    qr[:, :ROPE] = q[:, LAT:]
    spread = jnp.broadcast_to(qmask[...][:, None, :], (TILE_Q, HEADS, ROPE))
    qr[:, ROPE:] = spread.reshape(ROWS, ROPE).astype(bf16)

    def at(j):
        return pl.ds(pl.multiple_of(j * CHUNK, CHUNK), CHUNK)

    def raw(j):
        return nt(keys[at(j), :LAT], q[:, :LAT]) + nt(keys[at(j), LAT:], qr[...])

    last = CHUNKS - 1

    def score(j, peak):
        s = raw(j)
        s_scr[at(j), :] = s
        return jnp.maximum(peak, jnp.max(s, axis=0, keepdims=True))

    s = raw(last)
    key = lax.broadcasted_iota(jnp.int32, (CHUNK, ROWS), 0) - (CHUNK - BLOCK)
    query = t * TILE_Q + lax.broadcasted_iota(jnp.int32, (CHUNK, ROWS), 1) // HEADS
    s = jnp.where(key <= query, s, BIG)
    s_scr[at(last), :] = s
    peak = lax.fori_loop(start, last, score, jnp.max(s, axis=0, keepdims=True))
    peak_out[...] = jnp.maximum(peak_out[...], peak * attn_scale)

    def exps(j, total):
        e = jnp.exp((s_scr[at(j), :] - peak) * attn_scale)
        s_scr[at(j), :] = e
        return total + jnp.sum(e, axis=0, keepdims=True)

    total = lax.fori_loop(start, CHUNKS, exps, jnp.zeros((1, ROWS), f32))
    share = 1.0 / total
    att_t[...] = jnp.zeros_like(att_t)

    def values(j, _):
        w = s_scr[at(j), :] * share
        s_scr[at(j), :] = w
        rounded = w.astype(bf16)
        p_scr[at(j), :] = rounded
        att_t[...] += nn(vt[:, at(j)], rounded)
        return 0

    lax.fori_loop(start, CHUNKS, values, 0)
    attended = att_t[...].T.astype(bf16)
    att_out[...] = attended
    delta = jnp.sum(dout[...].astype(f32) * attended.astype(f32), axis=1, keepdims=True)
    delta = jnp.broadcast_to(delta, (ROWS, 128)).T[:1, :]

    def grads(j, _):
        dprob = nt(keys[at(j), :LAT], dout[...])
        ds = (s_scr[at(j), :] * (dprob - delta) * attn_scale).astype(bf16)
        grad_out[at(j), :] += nn(ds, q[...])
        grad_out[at(j), :LAT] += nn(p_scr[at(j), :], dout[...])
        return 0

    lax.fori_loop(start, CHUNKS, grads, 0)


def attention(low, q, dout, qmask, keys):
    per_tile = lambda width: pl.BlockSpec((ROWS, width), lambda t, low: (t, 0))
    whole = lambda *shape: pl.BlockSpec(shape, lambda t, low: (0, 0))
    flops = 2 * BLOCK * HEADS * WINDOW // 2 * (2 * KV + 3 * LAT)
    return pl.pallas_call(
        attention_kernel,
        grid_spec=pltpu.PrefetchScalarGridSpec(
            num_scalar_prefetch=1,
            grid=(TILES,),
            in_specs=[
                per_tile(KV),
                per_tile(LAT),
                pl.BlockSpec((TILE_Q, ROPE), lambda t, low: (t, 0)),
                whole(WINDOW, PAD),
            ],
            out_specs=[per_tile(LAT), whole(WINDOW, KV), whole(1, ROWS)],
            scratch_shapes=[
                pltpu.VMEM((LAT, WINDOW), bf16),
                pltpu.VMEM((ROWS, 128), bf16),
                pltpu.VMEM((WINDOW, ROWS), f32),
                pltpu.VMEM((WINDOW, ROWS), bf16),
                pltpu.VMEM((LAT, ROWS), f32),
            ],
        ),
        out_shape=(
            jax.ShapeDtypeStruct((BLOCK * HEADS, LAT), bf16),
            jax.ShapeDtypeStruct((WINDOW, KV), f32),
            jax.ShapeDtypeStruct((1, ROWS), f32),
        ),
        compiler_params=pltpu.CompilerParams(
            dimension_semantics=("arbitrary",), vmem_limit_bytes=48 * MiB
        ),
        cost_estimate=pl.CostEstimate(
            flops=flops, bytes_accessed=16 << 20, transcendentals=BLOCK * HEADS * WINDOW
        ),
        name="attention",
    )(low, q, dout, qmask, keys)


def grads_kernel(
    kg, proj, gain, cos, sin, tok, peak, rows_out, peak_out,
    near, far, kvg, peaks, tok_t, part, part_in, sums, sums_in,
    ns, nr, fs, fr, gs, gr, ps, pr, ss, sr, ts, tr,
):
    me = Place()
    c, k, f = me.c, me.k, me.f
    sibling = me.at(k=1 - k)
    back = [me.ctx((c - 2 * j + CTX) % CTX) for j in range(1, 8)]
    peers = [me.fsdp((f + s) % FSDP) for s in range(1, FSDP)]
    greet([sibling] + back + peers)

    def slot(distance):
        return SLOTS - 1 - distance

    swaps = []
    for n in range(4):
        copy = send(kg.at[slot(2 * n + 1)], near.at[n], ns.at[n], nr.at[n], sibling)
        copy.start()
        swaps.append(copy)
    gathers = []
    for s in range(1, FSDP):
        copy = send(peak, peaks.at[s], ps.at[s - 1], pr.at[s - 1], peers[s - 1])
        copy.start()
        gathers.append(copy)
    sends = []
    own = kg[slot(0)]
    for n in range(4):
        swaps[n].wait_recv()
        j = n + 1

        @pl.when(k == 1)
        def _(n=n):
            near[n] = near[n] + kg[slot(2 * n + 2)]

    own = own + jnp.where(k == 0, near[0], jnp.zeros_like(own))

    @pl.when(k == 0)
    def _():
        for n in range(3):
            near[4 + n] = near[n + 1] + kg[slot(2 * n + 2)]
        near[7] = kg[slot(8)]

    base = (1 - k) * 4
    for n in range(4):
        copy = send(near.at[base + n], far.at[n], fs.at[n], fr.at[n], back[n])
        copy.start()
        sends.append(copy)
    for s in range(FSDP):
        tok_t[:, s * BLOCK : (s + 1) * BLOCK] = tok[s].T
    for copy in sends:
        copy.wait_recv()
    key_grad = own + far[0] + far[1] + far[2] + far[3]

    compressed = proj[:, :LAT]
    inverse = lax.rsqrt(jnp.mean(compressed * compressed, axis=1, keepdims=True) + 1e-06)
    first, second = key_grad[:, LAT : LAT + HALF], key_grad[:, LAT + HALF :]
    d_first = first * cos[...] + second * sin[...]
    d_second = -first * sin[...] + second * cos[...]
    scaled = key_grad[:, :LAT] * gain[...]
    inner = jnp.mean(compressed * scaled, axis=1, keepdims=True)
    d_comp = inverse * (scaled - compressed * (inverse * inverse * inner))
    kvg[0, :, :LAT] = d_comp.astype(bf16)
    kvg[0, :, LAT:] = jnp.concatenate([d_first, d_second], axis=1).astype(bf16)
    spread = []
    for s in range(1, FSDP):
        copy = send(kvg.at[0], kvg.at[s], gs.at[s - 1], gr.at[s - 1], peers[s - 1])
        copy.start()
        spread.append(copy)
    top = peak[...]
    for s in range(1, FSDP):
        gathers[s - 1].wait_recv()
        top = jnp.maximum(top, peaks[s])
    for copy in spread:
        copy.wait_recv()

    everything = kvg[...].reshape(FSDP * BLOCK, KV)

    def multiply(n, core):
        p = 2 * n + core
        rows = pl.ds(pl.multiple_of(p * PIECE, 8), PIECE)
        return nn(tok_t[rows, :], everything)

    whole = nn(tok_t[...], everything)
    for p in range(CTX):
        part[p, :, :KV] = whole[p * PIECE : (p + 1) * PIECE]
        part[p, :8, KV:] = top[:, :ROPE]
    halves = []
    for n in range(CTX // 2):
        copy = send(part.at[2 * n + 1 - k], part_in.at[n], ss.at[n], sr.at[n], sibling)
        copy.start()
        halves.append(copy)
    totals = []
    me_n = c // 2
    for n in range(CTX // 2):
        halves[n].wait_recv()
        here = part.at[2 * n + k]
        sums[n, :, :KV] = here[:, :KV] + part_in[n, :, :KV]
        sums[n, :8, KV:] = jnp.maximum(here[:8, KV:], part_in[n, :8, KV:])
    for s in range(1, CTX // 2):
        to = (me_n - s + 8) % 8
        copy = send(sums.at[to], sums_in.at[s], ts.at[s], tr.at[s], back[s - 1])
        copy.start()
        totals.append(copy)
    rows = sums[me_n, :, :KV]
    top = sums[me_n, :8, KV:]
    for s in range(1, CTX // 2):
        totals[s - 1].wait_recv()
        rows = rows + sums_in[s, :, :KV]
        top = jnp.maximum(top, sums_in[s, :8, KV:])
    rows_out[...] = rows
    peak_out[...] = top
    for copy in swaps + gathers + sends + spread + halves + totals:
        copy.wait_send()


def weight_grad(kg, proj, gain, cos, sin, tok, peak):
    sems = [4, 4, 4, 4, 7, 7, 7, 7, 8, 8, 8, 8]
    return pl.pallas_call(
        grads_kernel,
        out_shape=(
            jax.ShapeDtypeStruct((PIECE, KV), f32),
            jax.ShapeDtypeStruct((8, ROPE), f32),
        ),
        in_specs=[VMEM] * 7,
        out_specs=(VMEM, VMEM),
        scratch_shapes=[
            pltpu.VMEM((8, BLOCK, KV), f32),
            pltpu.VMEM((4, BLOCK, KV), f32),
            pltpu.VMEM((FSDP, BLOCK, KV), bf16),
            pltpu.VMEM((FSDP, 8, 128), f32),
            pltpu.VMEM((SHARD, FSDP * BLOCK), bf16),
            pltpu.VMEM((CTX, PIECE, PAD), f32),
            pltpu.VMEM((CTX // 2, PIECE, PAD), f32),
            pltpu.VMEM((CTX // 2, PIECE, PAD), f32),
            pltpu.VMEM((CTX // 2, PIECE, PAD), f32),
        ]
        + [pltpu.SemaphoreType.DMA((n,)) for n in sems],
        compiler_params=pltpu.CompilerParams(
            collective_id=1, has_side_effects=True, vmem_limit_bytes=56 * MiB
        ),
        name="weight_grad",
    )(kg, proj, gain, cos, sin, tok, peak)


TRI = [(r, s) for r in range(5) for s in range(r, 5)]
PACKED = 2048
HIGH = lax.Precision.HIGHEST


def muon_kernel(
    g, out, pack, core_in, yz_in, x_in, acc, gram, rows_in, ms, mr, cs, cr, ys, yr, xs, xr, xs2, xr2, ys2, yr2, cs2, cr2
):
    me = Place()
    k, x, y = me.k, me.x, me.y
    z = me.zh * 2 + me.zl
    sibling = me.at(k=1 - k)

    def plane(n):
        yy, zz = (y + n // 4) % 4, (z + n % 4) % 4
        return me.at(y=yy, zh=zz // 2, zl=zz % 2), yy * 4 + zz

    planes = [plane(n) for n in range(16)]
    line = [me.at(x=(x + s) % 4) for s in range(4)]
    give = me.f * CTX + me.c
    take = me.c * FSDP + me.f
    moving = give != take
    barrier = pltpu.get_barrier_semaphore()

    @pl.when(moving)
    def _():
        pl.semaphore_signal(
            barrier, inc=1, device_id=(take % CTX, take // CTX), device_id_type=MESH
        )

    friends = [sibling] + [p[0] for p in planes[1:]] + line[1:]
    greet(friends, jnp.where(moving, 1, 0))
    move = send(g, rows_in, ms.at[0], mr.at[0], (give // FSDP, give % FSDP))

    grad = g[...]
    wide = jnp.concatenate([grad, jnp.zeros((PIECE, PAD - KV), f32)], axis=1)
    for i, (r, s) in enumerate(TRI):
        if i < 14:
            block = tn(wide[:, r * 128 : r * 128 + 128], wide[:, s * 128 : s * 128 + 128], precision=HIGH)
            pack[i * 128 : i * 128 + 128, :] = block
    corner = tn(wide[:, 512:576], wide[:, 512:], precision=HIGH)
    pack[1792:1856, :] = corner
    pack[1856:, :] = jnp.zeros((PACKED - 1856, 128), f32)

    half = PACKED // 2
    unit = half // 16
    small = unit // 4

    def rows(start, size):
        return pl.ds(pl.multiple_of(start, 8), size)

    copies = []
    swap = send(pack.at[rows((1 - k) * half, half)], core_in, cs.at[0], cr.at[0], sibling)
    swap.start()

    @pl.when(moving)
    def _():
        move.start()

    @pl.when(jnp.logical_not(moving))
    def _():
        rows_in[...] = grad

    swap.wait_recv()
    acc[...] = pack[rows(k * half, half), :] + core_in[...]
    copies.append(swap)
    mine = y * 4 + z
    first = []
    for n in range(1, 16):
        device, index = planes[n]
        copy = send(acc.at[rows(index * unit, unit)], yz_in.at[n], ys.at[n], yr.at[n], device)
        copy.start()
        first.append(copy)
    total = acc[rows(mine * unit, unit), :]
    for n in range(1, 16):
        first[n - 1].wait_recv()
        total = total + yz_in[n]
    yz_in[0] = total
    second = []
    for s in range(1, 4):
        to = (x + s) % 4
        copy = send(yz_in.at[0, rows(to * small, small)], x_in.at[s], xs.at[s], xr.at[s], line[s])
        copy.start()
        second.append(copy)
    total = yz_in[0, rows(x * small, small), :]
    for s in range(1, 4):
        second[s - 1].wait_recv()
        total = total + x_in[s]
    base = k * half + mine * unit
    gram[rows(base + x * small, small), :] = total
    third = []
    for s in range(1, 4):
        there = gram.at[rows(base + x * small, small)]
        copy = send(there, there, xs2.at[s], xr2.at[s], line[s])
        copy.start()
        third.append(copy)
    for copy in third:
        copy.wait_recv()
    fourth = []
    for n in range(1, 16):
        there = gram.at[rows(base, unit)]
        copy = send(there, there, ys2.at[n], yr2.at[n], planes[n][0])
        copy.start()
        fourth.append(copy)
    for copy in fourth:
        copy.wait_recv()
    there = gram.at[rows(k * half, half)]
    last = send(there, there, cs2.at[0], cr2.at[0], sibling)
    last.start()
    last.wait_recv()
    copies += first + second + third + fourth + [last]

    blocks = {}
    for i, (r, s) in enumerate(TRI):
        if i < 14:
            blocks[r, s] = gram[i * 128 : i * 128 + 128, :]
            if r != s:
                blocks[s, r] = blocks[r, s].T
    edge = gram[1792:1856, :]
    lines = []
    for r in range(4):
        lines.append(jnp.concatenate([blocks[r, s] for s in range(5)], axis=1)[:, :KV])
    bottom = [blocks[4, s][:64] for s in range(4)] + [edge]
    lines.append(jnp.concatenate(bottom, axis=1)[:, :KV])
    full = jnp.concatenate(lines, axis=0)
    row = lax.broadcasted_iota(jnp.int32, (KV, KV), 0)
    col = lax.broadcasted_iota(jnp.int32, (KV, KV), 1)
    diagonal = row == col
    squares = jnp.sum(jnp.where(diagonal, full, 0.0))
    norm = jnp.sqrt(jnp.full((1, 1), squares, f32)) + 1e-07
    inv = 1.0 / norm
    a = full * inv * inv

    @pl.when(moving)
    def _():
        move.wait_recv()

    iterate = rows_in[...] * inv
    for step in range(NS_ITERS):
        a2 = nn(a, a, precision=HIGH)
        mixing = quintic_b * a + quintic_c * a2
        iterate = quintic_a * iterate + nn(iterate, mixing, precision=HIGH)
        if step < NS_ITERS - 1:
            b = quintic_a * a + nn(a, mixing, precision=HIGH)
            a = quintic_a * b + nn(b, mixing, precision=HIGH)
    out[...] = iterate * (0.2 * math.sqrt(D))

    @pl.when(moving)
    def _():
        move.wait_send()

    for copy in copies:
        copy.wait_send()


def muon(g):
    half = PACKED // 2
    sems = [1, 1, 16, 16, 4, 4, 4, 4, 16, 16, 1, 1]
    return pl.pallas_call(
        muon_kernel,
        out_shape=jax.ShapeDtypeStruct((PIECE, KV), f32),
        in_specs=[VMEM],
        out_specs=VMEM,
        scratch_shapes=[
            pltpu.VMEM((PACKED, 128), f32),
            pltpu.VMEM((half, 128), f32),
            pltpu.VMEM((16, half // 16, 128), f32),
            pltpu.VMEM((4, half // 64, 128), f32),
            pltpu.VMEM((half, 128), f32),
            pltpu.VMEM((PACKED, 128), f32),
            pltpu.VMEM((PIECE, KV), f32),
            pltpu.SemaphoreType.DMA((1,)),
            pltpu.SemaphoreType.DMA((1,)),
        ]
        + [pltpu.SemaphoreType.DMA((n,)) for n in sems],
        compiler_params=pltpu.CompilerParams(
            collective_id=2, has_side_effects=True, vmem_limit_bytes=56 * MiB
        ),
        name="muon",
    )(g)


def per_device(tokens, kv_weight, latent_gain, queries, out_grad, segment_ids):
    tok = tokens[0]
    c = lax.axis_index("ctx")
    positions = c * BLOCK + jnp.arange(BLOCK, dtype=jnp.int32)
    cos, sin = rope_tables(positions)
    gain = latent_gain[None]
    docs = segment_ids[0]
    lanes = jnp.arange(ROPE, dtype=jnp.int32)
    hot = (docs[:, None] == lanes[None]).astype(f32)
    qmask = jnp.where((lanes[None] < 9) & (docs[:, None] != lanes[None]), BIG, 0.0)

    keys, proj = make_keys(tok, kv_weight, gain, hot, cos, sin)
    keys = keys.reshape(WINDOW, PAD)

    tok_after, keys = lax.optimization_barrier((tok, keys))
    f = lax.axis_index("fsdp")
    moved = []
    for s in range(FSDP):
        piece = lax.dynamic_slice_in_dim(tok_after, ((f + s) % FSDP) * SHARD, SHARD, 1)
        if s > 0:
            piece = lax.ppermute(piece, "fsdp", [(i, (i + s) % FSDP) for i in range(FSDP)])
        moved.append(piece)

    codes = keys[:, KV : KV + 9].astype(f32)
    window_docs = jnp.sum(codes * jnp.array([0, 1, 2, 3, 4, 5, 6, 7, -1], f32), axis=1)
    heads = docs[::TILE_Q].astype(f32)
    begin = jnp.sum((window_docs[None] < heads[:, None]).astype(jnp.int32), axis=1)
    low = begin // CHUNK

    q = queries[0].reshape(BLOCK * HEADS, KV)
    dout = out_grad[0].reshape(BLOCK * HEADS, LAT)
    attended, kg, peak = attention(low, q, dout, qmask, keys)
    moved = jnp.stack(moved)
    peak = jnp.max(peak.reshape(TILE_Q, HEADS), axis=0)
    peak = jnp.broadcast_to(jnp.pad(peak, (0, 128 - HEADS))[None], (8, 128))
    rows, top = weight_grad(
        kg.reshape(SLOTS, BLOCK, KV), proj, gain, cos, sin, moved, peak
    )
    update = muon(rows)
    return (attended.reshape(1, BLOCK, HEADS, LAT), top[0, :HEADS], update)


def solution(mesh):
    return jax.shard_map(
        per_device,
        mesh=mesh,
        in_specs=(
            P("fsdp", "ctx", None),
            P("fsdp", None),
            P(),
            P("fsdp", "ctx", None, None),
            P("fsdp", "ctx", None, None),
            P("fsdp", "ctx"),
        ),
        out_specs=(P("fsdp", "ctx", None, None), P(), P(("ctx", "fsdp"), None)),
        check_vma=False,
    )
```

```python
import functools
import math

import jax
import jax.numpy as jnp
from jax import lax
from jax.experimental import pallas as pl
from jax.experimental.pallas import tpu as pltpu
from jax.sharding import PartitionSpec as P

D = 7168
LAT = 512
ROPE = 64
HEADS = 32
NS_ITERS = 5
KV = LAT + ROPE
PAD = 640
HALF = ROPE // 2
BLOCK = 128
REACH = 8
SLOTS = REACH + 2
WINDOW = SLOTS * BLOCK
CHUNK = 256
CHUNKS = WINDOW // CHUNK
CTX = 16
FSDP = 8
SHARD = D // FSDP
PIECE = SHARD // CTX
TILE_Q = 16
ROWS = TILE_Q * HEADS
TILES = BLOCK // TILE_Q

attn_scale = 192.0 ** (-0.5)
rope_base = 50000.0
quintic_a = 3.4445
quintic_b = -4.775
quintic_c = 2.0315
BIG = -1e30
MiB = 1 << 20

MESH = pl.DeviceIdType.MESH
VMEM = pl.BlockSpec(memory_space=pltpu.VMEM)
f32, bf16 = jnp.float32, jnp.bfloat16


def rope_tables(positions):
    ladder = jnp.arange(HALF, dtype=f32)
    freqs = jnp.power(rope_base, -2.0 * ladder / ROPE)
    angles = positions.astype(f32)[:, None] * freqs[None, :]
    return (jnp.cos(angles), jnp.sin(angles))


def nn(a, b, **kw):
    return lax.dot_general(a, b, (((1,), (0,)), ((), ())), preferred_element_type=f32, **kw)


def nt(a, b, **kw):
    return lax.dot_general(a, b, (((1,), (1,)), ((), ())), preferred_element_type=f32, **kw)


def tn(a, b, **kw):
    return lax.dot_general(a, b, (((0,), (0,)), ((), ())), preferred_element_type=f32, **kw)


class Place:
    def __init__(self):
        self.c, self.f = lax.axis_index("ctx"), lax.axis_index("fsdp")
        self.y, self.zh, self.k = self.c // 4, (self.c // 2) % 2, self.c % 2
        self.x, self.zl = self.f // 2, self.f % 2

    def at(self, x=None, y=None, zh=None, zl=None, k=None):
        x = self.x if x is None else x
        y = self.y if y is None else y
        zh = self.zh if zh is None else zh
        zl = self.zl if zl is None else zl
        k = self.k if k is None else k
        return ((y * 2 + zh) * 2 + k, x * 2 + zl)

    def ctx(self, c):
        return (c, self.f)

    def fsdp(self, f):
        return (self.c, f)


def greet(devices, others=0):
    barrier = pltpu.get_barrier_semaphore()
    for device in devices:
        pl.semaphore_signal(barrier, inc=1, device_id=device, device_id_type=MESH)
    pl.semaphore_wait(barrier, len(devices) + others)


def send(src, dst, send_sem, recv_sem, device):
    return pltpu.make_async_remote_copy(
        src_ref=src,
        dst_ref=dst,
        send_sem=send_sem,
        recv_sem=recv_sem,
        device_id=device,
        device_id_type=MESH,
    )


def keys_kernel(
    tok, w, gain, hot, cos, sin, heads, qt, keys_out, proj_out, low_out, q_out, wall, win, qin, qrow, qs, ws, wr, ks, kr
):
    me = Place()
    c, k, x = me.c, me.k, me.x
    sibling = me.at(k=1 - k)
    z_same, z_other = me.at(zl=1 - me.zl), me.at(zl=1 - me.zl, zh=1 - me.zh)
    x_up, x_down = me.at(x=(x + 1) % 4), me.at(x=(x + 3) % 4)
    later = [me.ctx((c + 2 * j) % CTX) for j in range(1, 5)]
    earlier = [me.ctx((c - 2 * j + CTX) % CTX) for j in range(1, 5)]
    greet([sibling, z_same, z_other, x_up, x_down] + later + earlier[:3])

    half = KV // 2
    quarter = half // 2
    counter = [0]

    def rows(core, q=None):
        if q is None:
            return pl.ds(pl.multiple_of(core * half, 16), half)
        return pl.ds(pl.multiple_of(core * half + q * quarter, 16), quarter)

    def post(src_f, src, core, q, device):
        i = counter[0]
        counter[0] += 1
        where = rows(core, q)
        source = w.at[where] if src is None else src.at[src_f, where]
        copy = send(source, wall.at[src_f, where], ws.at[i], wr.at[i], device)
        copy.start()
        return copy

    def shard_of(xx, zl):
        return (xx % 4) * 2 + zl

    own = me.f
    up = [post(own, None, k, 0, x_up), post(own, None, k, 1, x_up)]
    down = [post(own, None, k, 1, x_down), post(own, None, k, 0, x_down)]
    own_z = [post(own, None, k, 0, z_same), post(own, None, k, 1, z_other)]
    fetch = pltpu.make_async_copy(qt, qin, qs.at[0])
    fetch.start()
    posted = up + down + own_z

    def forward(copy, shard, q):
        copy.wait_recv()
        z = post(shard, wall, k, q, (z_same, z_other)[q])
        s = post(shard, wall, k, q, sibling)
        posted.extend([z, s])
        return z, s

    def pass_on(copy, shard, q):
        copy.wait_recv()
        s = post(shard, wall, k, q, sibling)
        posted.append(s)
        return s

    other = 1 - me.zl
    f_prev, f_next, f_far = shard_of(x + 3, me.zl), shard_of(x + 1, me.zl), shard_of(x + 2, me.zl)
    o_own, o_prev, o_next, o_far = (shard_of(x + i, other) for i in (0, 3, 1, 2))

    def add(total, shard):
        return total + nt(
            tok[:, pl.ds(pl.multiple_of(shard * SHARD, 128), SHARD)], wall[shard]
        )

    fetch.wait()

    def turn(h, _):
        for lanes in range(PAD // 128):
            width = min(128, KV - lanes * 128)
            block = qin[h, lanes * 128 : lanes * 128 + width, :].astype(f32)
            if width < 128:
                block = jnp.concatenate([block, jnp.zeros((128 - width, BLOCK), f32)], axis=0)
            qrow[lanes, pl.ds(h, BLOCK, stride=HEADS), :] = block.T
        return 0

    lax.fori_loop(0, HEADS // 2, turn, 0)

    prev0 = forward(up[0], f_prev, 0)
    relay_up = post(f_prev, wall, k, 0, x_up)
    next1 = forward(down[0], f_next, 1)
    relay_down = post(f_next, wall, k, 1, x_down)
    posted.extend([relay_up, relay_down])
    s_own = [pass_on(own_z[q], o_own, q) for q in range(2)]
    lax.fori_loop(HEADS // 2, HEADS, turn, 0)
    acc = nt(tok[:, pl.ds(pl.multiple_of(own * SHARD, 128), SHARD)], w[...])
    prev1 = forward(up[1], f_prev, 1)
    next0 = forward(down[1], f_next, 0)
    s_prev0 = pass_on(prev0[0], o_prev, 0)
    s_next1 = pass_on(next1[0], o_next, 1)

    def narrow(i, _):
        rows = pl.ds(pl.multiple_of(i * ROWS, ROWS), ROWS)
        for lanes in range(PAD // 128):
            width = min(128, KV - lanes * 128)
            q_out[rows, lanes * 128 : lanes * 128 + width] = qrow[lanes, rows, :width].astype(bf16)
        return 0

    lax.fori_loop(0, TILES, narrow, 0)
    for copy in s_own:
        copy.wait_recv()
    acc = add(acc, o_own)
    far0 = forward(relay_up, f_far, 0)
    far1 = forward(relay_down, f_far, 1)
    prev0[1].wait_recv()
    prev1[1].wait_recv()
    acc = add(acc, f_prev)
    next0[1].wait_recv()
    next1[1].wait_recv()
    acc = add(acc, f_next)
    s_prev1 = pass_on(prev1[0], o_prev, 1)
    s_next0 = pass_on(next0[0], o_next, 0)
    far0[1].wait_recv()
    far1[1].wait_recv()
    acc = add(acc, f_far)
    s_far0 = pass_on(far0[0], o_far, 0)
    s_far1 = pass_on(far1[0], o_far, 1)
    for shard, pair in ((o_prev, (s_prev0, s_prev1)), (o_next, (s_next0, s_next1)), (o_far, (s_far0, s_far1))):
        for copy in pair:
            copy.wait_recv()
        acc = add(acc, shard)

    compressed = acc[:, :LAT]
    inverse = lax.rsqrt(jnp.mean(compressed * compressed, axis=1, keepdims=True) + 1e-06)
    latent = compressed * inverse * gain[...]
    first, second = acc[:, LAT : LAT + HALF], acc[:, LAT + HALF :]
    mine = win.at[SLOTS - 1]
    mine[:, :LAT] = latent.astype(bf16)
    tail = jnp.concatenate(
        [
            first * cos[...] - second * sin[...],
            second * cos[...] + first * sin[...],
            hot[...],
        ],
        axis=1,
    )
    mine[:, LAT:] = tail.astype(bf16)
    proj_out[...] = acc

    def slot(distance):
        return SLOTS - 1 - distance

    spread = []
    for j in range(1, 5):
        copy = send(mine, win.at[slot(2 * j)], ks.at[j - 1], kr.at[j - 1], later[j - 1])
        copy.start()
        spread.append(copy)
    to_sibling = []

    def give(n):
        copy = send(
            win.at[slot(2 * n + 2 * k)], win.at[slot(2 * n + 1)], ks.at[4 + n], kr.at[4 + n], sibling
        )
        copy.start()
        to_sibling.append(copy)

    spread[0].wait_recv()
    give(0)
    give_next = 1
    for j in range(1, 4):
        spread[j].wait_recv()
        give(give_next)
        give_next += 1
    for copy in to_sibling:
        copy.wait_recv()
    lane = lax.broadcasted_iota(jnp.int32, (BLOCK, 128), 1)
    flag = jnp.where(lane == ROPE + 8, 1.0, 0.0)
    for d in range(REACH + 1):
        keys_out[slot(d)] = win[slot(d)]
        if d > 0:

            @pl.when(c < d)
            def _(d=d):
                keys_out[slot(d), :, LAT:] = flag.astype(bf16)

    keys_out[0] = jnp.zeros((BLOCK, PAD), bf16)
    keys_out[0, :, LAT:] = flag.astype(bf16)
    before = jnp.zeros((1, 128), f32)
    weight = jnp.where(
        lane < ROPE, 0.0, jnp.where(lane < ROPE + 8, (lane - ROPE).astype(f32), jnp.where(lane == ROPE + 8, -1.0, 0.0))
    )
    for d in range(SLOTS):
        code = keys_out[d, :, LAT:].astype(f32)
        document = jnp.sum(code * weight, axis=1, keepdims=True)
        before = before + jnp.sum(jnp.where(document < heads[...], 1.0, 0.0), axis=0, keepdims=True)
    low_out[...] = (before * (1.0 / CHUNK)).astype(jnp.int32)
    for copy in posted + spread + to_sibling:
        copy.wait_send()


N_W = 6 + 2 + 6 * 2 + 8


def make_keys(tok, w, gain, hot, cos, sin, heads, qt):
    return pl.pallas_call(
        keys_kernel,
        out_shape=(
            jax.ShapeDtypeStruct((SLOTS, BLOCK, PAD), bf16),
            jax.ShapeDtypeStruct((BLOCK, KV), f32),
            jax.ShapeDtypeStruct((1, 128), jnp.int32),
            jax.ShapeDtypeStruct((BLOCK * HEADS, KV), bf16),
        ),
        in_specs=[VMEM] * 7 + [pl.BlockSpec(memory_space=pl.ANY)],
        out_specs=(VMEM,) * 4,
        scratch_shapes=[
            pltpu.VMEM((FSDP, KV, SHARD), bf16),
            pltpu.VMEM((SLOTS, BLOCK, PAD), bf16),
            pltpu.VMEM((HEADS, KV, BLOCK), bf16),
            pltpu.VMEM((PAD // 128, BLOCK * HEADS, 128), f32),
            pltpu.SemaphoreType.DMA((1,)),
            pltpu.SemaphoreType.DMA((N_W,)),
            pltpu.SemaphoreType.DMA((N_W,)),
            pltpu.SemaphoreType.DMA((8,)),
            pltpu.SemaphoreType.DMA((8,)),
        ],
        compiler_params=pltpu.CompilerParams(
            collective_id=0, has_side_effects=True, vmem_limit_bytes=48 * MiB
        ),
        name="keys",
    )(tok, w, gain, hot, cos, sin, heads, qt)


def attention_kernel(
    low, q, dout, hot, keys, att_out, grad_out, peak_out, vt, qr, s_scr, p_scr, att_t
):
    t = pl.program_id(0)
    start = low[t]

    @pl.when(t == 0)
    def _():
        grad_out[...] = jnp.zeros_like(grad_out)
        peak_out[...] = jnp.full_like(peak_out, BIG)
        for j in range(CHUNKS):
            vt[:, j * CHUNK : (j + 1) * CHUNK] = keys[j * CHUNK : (j + 1) * CHUNK, :LAT].T

    qr[:, :ROPE] = q[:, LAT:]
    lane = lax.broadcasted_iota(jnp.int32, (TILE_Q, ROPE), 1)
    qmask = jnp.where((lane < 9) & (hot[...] == 0.0), BIG, 0.0)
    spread = jnp.broadcast_to(qmask[:, None, :], (TILE_Q, HEADS, ROPE))
    qr[:, ROPE:] = spread.reshape(ROWS, ROPE).astype(bf16)

    def at(j):
        return pl.ds(pl.multiple_of(j * CHUNK, CHUNK), CHUNK)

    def raw(j):
        return nt(keys[at(j), :LAT], q[:, :LAT]) + nt(keys[at(j), LAT:], qr[...])

    last = CHUNKS - 1

    def score(j, peak):
        s = raw(j)
        s_scr[at(j), :] = s
        return jnp.maximum(peak, jnp.max(s, axis=0, keepdims=True))

    s = raw(last)
    key = lax.broadcasted_iota(jnp.int32, (CHUNK, ROWS), 0) - (CHUNK - BLOCK)
    query = t * TILE_Q + lax.broadcasted_iota(jnp.int32, (CHUNK, ROWS), 1) // HEADS
    s = jnp.where(key <= query, s, BIG)
    s_scr[at(last), :] = s
    peak = lax.fori_loop(start, last, score, jnp.max(s, axis=0, keepdims=True))
    peak_out[...] = jnp.maximum(peak_out[...], peak * attn_scale)

    def exps(j, total):
        e = jnp.exp((s_scr[at(j), :] - peak) * attn_scale)
        s_scr[at(j), :] = e
        return total + jnp.sum(e, axis=0, keepdims=True)

    total = lax.fori_loop(start, CHUNKS, exps, jnp.zeros((1, ROWS), f32))
    share = 1.0 / total
    att_t[...] = jnp.zeros_like(att_t)

    def values(j, _):
        w = s_scr[at(j), :] * share
        s_scr[at(j), :] = w
        rounded = w.astype(bf16)
        p_scr[at(j), :] = rounded
        att_t[...] += nn(vt[:, at(j)], rounded)
        return 0

    lax.fori_loop(start, CHUNKS, values, 0)
    attended = att_t[...].T.astype(bf16)
    att_out[...] = attended
    delta = jnp.sum(dout[...].astype(f32) * attended.astype(f32), axis=1, keepdims=True)
    delta = jnp.broadcast_to(delta, (ROWS, 128)).T[:1, :]

    def grads(j, _):
        dprob = nt(keys[at(j), :LAT], dout[...])
        ds = (s_scr[at(j), :] * (dprob - delta) * attn_scale).astype(bf16)
        grad_out[at(j), :] += nn(ds, q[...])
        grad_out[at(j), :LAT] += nn(p_scr[at(j), :], dout[...])
        return 0

    lax.fori_loop(start, CHUNKS, grads, 0)


def attention(low, q, dout, hot, keys):
    per_tile = lambda width: pl.BlockSpec((ROWS, width), lambda t, low: (t, 0))
    whole = lambda *shape: pl.BlockSpec(shape, lambda t, low: (0, 0))
    flops = 2 * BLOCK * HEADS * WINDOW // 2 * (2 * KV + 3 * LAT)
    return pl.pallas_call(
        attention_kernel,
        grid_spec=pltpu.PrefetchScalarGridSpec(
            num_scalar_prefetch=1,
            grid=(TILES,),
            in_specs=[
                per_tile(KV),
                per_tile(LAT),
                pl.BlockSpec((TILE_Q, ROPE), lambda t, low: (t, 0)),
                whole(WINDOW, PAD),
            ],
            out_specs=[per_tile(LAT), whole(WINDOW, KV), whole(8, ROWS)],
            scratch_shapes=[
                pltpu.VMEM((LAT, WINDOW), bf16),
                pltpu.VMEM((ROWS, 128), bf16),
                pltpu.VMEM((WINDOW, ROWS), f32),
                pltpu.VMEM((WINDOW, ROWS), bf16),
                pltpu.VMEM((LAT, ROWS), f32),
            ],
        ),
        out_shape=(
            jax.ShapeDtypeStruct((BLOCK * HEADS, LAT), bf16),
            jax.ShapeDtypeStruct((WINDOW, KV), f32),
            jax.ShapeDtypeStruct((8, ROWS), f32),
        ),
        compiler_params=pltpu.CompilerParams(
            dimension_semantics=("arbitrary",), vmem_limit_bytes=32 * MiB
        ),
        cost_estimate=pl.CostEstimate(
            flops=flops, bytes_accessed=16 << 20, transcendentals=BLOCK * HEADS * WINDOW
        ),
        name="attention",
    )(low, q, dout, hot, keys)


def grads_kernel(
    kg, proj, gain, cos, sin, tok, peak, rows_out, peak_out,
    near, far, kvg, peaks, tok_in, tok_t, part, part_in, sums, sums_in,
    ns, nr, fs, fr, gs, gr, ps, pr, ss, sr, ts, tr, as_, ar,
):
    me = Place()
    c, k, f = me.c, me.k, me.f
    sibling = me.at(k=1 - k)
    back = [me.ctx((c - 2 * j + CTX) % CTX) for j in range(1, 8)]
    peers = [me.fsdp((f + s) % FSDP) for s in range(1, FSDP)]
    greet([sibling] + back + peers)

    def slot(distance):
        return SLOTS - 1 - distance

    swaps = []
    for n in range(4):
        copy = send(kg.at[slot(2 * n + 1)], near.at[n], ns.at[n], nr.at[n], sibling)
        copy.start()
        swaps.append(copy)
    tokens = []
    for s in range(1, FSDP):
        columns = pl.ds(pl.multiple_of(((f + s) % FSDP) * SHARD, 128), SHARD)
        copy = send(tok.at[:, columns], tok_in.at[s], as_.at[s - 1], ar.at[s - 1], peers[s - 1])
        copy.start()
        tokens.append(copy)
    gathers = []
    for s in range(1, FSDP):
        copy = send(peak, peaks.at[s], ps.at[s - 1], pr.at[s - 1], peers[s - 1])
        copy.start()
        gathers.append(copy)
    sends = []
    own = kg[slot(0)]
    for n in range(4):
        swaps[n].wait_recv()
        j = n + 1

        @pl.when(k == 1)
        def _(n=n):
            near[n] = near[n] + kg[slot(2 * n + 2)]

    own = own + jnp.where(k == 0, near[0], jnp.zeros_like(own))

    @pl.when(k == 0)
    def _():
        for n in range(3):
            near[4 + n] = near[n + 1] + kg[slot(2 * n + 2)]
        near[7] = kg[slot(8)]

    base = (1 - k) * 4
    for n in range(4):
        copy = send(near.at[base + n], far.at[n], fs.at[n], fr.at[n], back[n])
        copy.start()
        sends.append(copy)
    tok_t[:, :BLOCK] = tok[:, pl.ds(pl.multiple_of(f * SHARD, 128), SHARD)].T
    for s in range(1, FSDP):
        tokens[s - 1].wait_recv()
        tok_t[:, s * BLOCK : (s + 1) * BLOCK] = tok_in[s].T
    for copy in sends:
        copy.wait_recv()
    key_grad = own + far[0] + far[1] + far[2] + far[3]

    compressed = proj[:, :LAT]
    inverse = lax.rsqrt(jnp.mean(compressed * compressed, axis=1, keepdims=True) + 1e-06)
    first, second = key_grad[:, LAT : LAT + HALF], key_grad[:, LAT + HALF :]
    d_first = first * cos[...] + second * sin[...]
    d_second = -first * sin[...] + second * cos[...]
    scaled = key_grad[:, :LAT] * gain[...]
    inner = jnp.mean(compressed * scaled, axis=1, keepdims=True)
    d_comp = inverse * (scaled - compressed * (inverse * inverse * inner))
    kvg[0, :, :LAT] = d_comp.astype(bf16)
    kvg[0, :, LAT:] = jnp.concatenate([d_first, d_second], axis=1).astype(bf16)
    spread = []
    for s in range(1, FSDP):
        copy = send(kvg.at[0], kvg.at[s], gs.at[s - 1], gr.at[s - 1], peers[s - 1])
        copy.start()
        spread.append(copy)
    top = peak[...]
    for s in range(1, FSDP):
        gathers[s - 1].wait_recv()
        top = jnp.maximum(top, peaks[s])
    for copy in spread:
        copy.wait_recv()

    everything = kvg[...].reshape(FSDP * BLOCK, KV)

    def multiply(n, core):
        p = 2 * n + core
        rows = pl.ds(pl.multiple_of(p * PIECE, 8), PIECE)
        return nn(tok_t[rows, :], everything)

    whole = nn(tok_t[...], everything)
    for p in range(CTX):
        part[p, :, :KV] = whole[p * PIECE : (p + 1) * PIECE]
        for r in range(8):
            part[p, r : r + 1, KV:] = top[r : r + 1, r * ROPE : (r + 1) * ROPE]
    halves = []
    for n in range(CTX // 2):
        copy = send(part.at[2 * n + 1 - k], part_in.at[n], ss.at[n], sr.at[n], sibling)
        copy.start()
        halves.append(copy)
    totals = []
    me_n = c // 2
    for n in range(CTX // 2):
        halves[n].wait_recv()
        here = part.at[2 * n + k]
        sums[n, :, :KV] = here[:, :KV] + part_in[n, :, :KV]
        sums[n, :8, KV:] = jnp.maximum(here[:8, KV:], part_in[n, :8, KV:])
    for s in range(1, CTX // 2):
        to = (me_n - s + 8) % 8
        copy = send(sums.at[to], sums_in.at[s], ts.at[s], tr.at[s], back[s - 1])
        copy.start()
        totals.append(copy)
    rows = sums[me_n, :, :KV]
    top = sums[me_n, :8, KV:]
    for s in range(1, CTX // 2):
        totals[s - 1].wait_recv()
        rows = rows + sums_in[s, :, :KV]
        top = jnp.maximum(top, sums_in[s, :8, KV:])
    rows_out[...] = rows
    peak_out[...] = top
    for copy in swaps + tokens + gathers + sends + spread + halves + totals:
        copy.wait_send()


def weight_grad(kg, proj, gain, cos, sin, tok, peak):
    sems = [4, 4, 4, 4, 7, 7, 7, 7, 8, 8, 8, 8, 7, 7]
    return pl.pallas_call(
        grads_kernel,
        out_shape=(
            jax.ShapeDtypeStruct((PIECE, KV), f32),
            jax.ShapeDtypeStruct((8, ROPE), f32),
        ),
        in_specs=[VMEM] * 7,
        out_specs=(VMEM, VMEM),
        scratch_shapes=[
            pltpu.VMEM((8, BLOCK, KV), f32),
            pltpu.VMEM((4, BLOCK, KV), f32),
            pltpu.VMEM((FSDP, BLOCK, KV), bf16),
            pltpu.VMEM((FSDP, 8, ROWS), f32),
            pltpu.VMEM((FSDP, BLOCK, SHARD), bf16),
            pltpu.VMEM((SHARD, FSDP * BLOCK), bf16),
            pltpu.VMEM((CTX, PIECE, PAD), f32),
            pltpu.VMEM((CTX // 2, PIECE, PAD), f32),
            pltpu.VMEM((CTX // 2, PIECE, PAD), f32),
            pltpu.VMEM((CTX // 2, PIECE, PAD), f32),
        ]
        + [pltpu.SemaphoreType.DMA((n,)) for n in sems],
        compiler_params=pltpu.CompilerParams(
            collective_id=1, has_side_effects=True, vmem_limit_bytes=32 * MiB
        ),
        name="weight_grad",
    )(kg, proj, gain, cos, sin, tok, peak)


TRI = [(r, s) for r in range(5) for s in range(r, 5)]
PACKED = 2048
PAIRS = {3: [(0, 0), (0, 1), (1, 0)], 6: [(0, 0), (0, 1), (1, 0), (0, 2), (2, 0), (1, 1)]}


def split(value, count):
    parts = []
    for _ in range(count):
        part = value.astype(bf16)
        parts.append(part)
        value = value - part.astype(f32)
    return parts


def muon_kernel(
    g, out, pack, core_in, yz_in, x_in, acc, gram, rows_in, a_scr, left_scr, thin_scr, right_scr, ms, mr, cs, cr, ys, yr, xs, xr, xs2, xr2, ys2, yr2, cs2, cr2
):
    me = Place()
    k, x, y = me.k, me.x, me.y
    z = me.zh * 2 + me.zl
    sibling = me.at(k=1 - k)

    def plane(n):
        yy, zz = (y + n // 4) % 4, (z + n % 4) % 4
        return me.at(y=yy, zh=zz // 2, zl=zz % 2), yy * 4 + zz

    planes = [plane(n) for n in range(16)]
    line = [me.at(x=(x + s) % 4) for s in range(4)]
    give = me.f * CTX + me.c
    take = me.c * FSDP + me.f
    moving = give != take
    barrier = pltpu.get_barrier_semaphore()

    @pl.when(moving)
    def _():
        pl.semaphore_signal(
            barrier, inc=1, device_id=(take % CTX, take // CTX), device_id_type=MESH
        )

    friends = [sibling] + [p[0] for p in planes[1:]] + line[1:]
    greet(friends, jnp.where(moving, 1, 0))
    move = send(g, rows_in, ms.at[0], mr.at[0], (give // FSDP, give % FSDP))

    grad = g[...]
    parts = [
        jnp.concatenate([p.astype(f32), jnp.zeros((8, KV), f32)], axis=0).astype(bf16)
        for p in split(grad, 3)
    ]
    left = jnp.concatenate([parts[i] for i, _ in PAIRS[6]], axis=0)
    right = jnp.concatenate([parts[j] for _, j in PAIRS[6]], axis=0)
    local = tn(left, right)
    for i, (r, s) in enumerate(TRI[:14]):
        width = min(128, KV - s * 128)
        pack[i * 128 : i * 128 + 128, :width] = local[r * 128 : r * 128 + 128, s * 128 : s * 128 + width]
    pack[1792:1856, :64] = local[512:, 512:]
    pack[1856:, :] = jnp.zeros((PACKED - 1856, 128), f32)

    half = PACKED // 2
    unit = half // 16
    small = unit // 4

    def rows(start, size):
        return pl.ds(pl.multiple_of(start, 8), size)

    copies = []
    swap = send(pack.at[rows((1 - k) * half, half)], core_in, cs.at[0], cr.at[0], sibling)
    swap.start()

    @pl.when(moving)
    def _():
        move.start()

    @pl.when(jnp.logical_not(moving))
    def _():
        rows_in[...] = grad

    swap.wait_recv()
    acc[...] = pack[rows(k * half, half), :] + core_in[...]
    copies.append(swap)
    mine = y * 4 + z
    first = []
    for n in range(1, 16):
        device, index = planes[n]
        copy = send(acc.at[rows(index * unit, unit)], yz_in.at[n], ys.at[n], yr.at[n], device)
        copy.start()
        first.append(copy)
    total = acc[rows(mine * unit, unit), :]
    for n in range(1, 16):
        first[n - 1].wait_recv()
        total = total + yz_in[n]
    yz_in[0] = total
    second = []
    for s in range(1, 4):
        to = (x + s) % 4
        copy = send(yz_in.at[0, rows(to * small, small)], x_in.at[s], xs.at[s], xr.at[s], line[s])
        copy.start()
        second.append(copy)
    total = yz_in[0, rows(x * small, small), :]
    for s in range(1, 4):
        second[s - 1].wait_recv()
        total = total + x_in[s]
    base = k * half + mine * unit
    gram[rows(base + x * small, small), :] = total
    third = []
    for s in range(1, 4):
        there = gram.at[rows(base + x * small, small)]
        copy = send(there, there, xs2.at[s], xr2.at[s], line[s])
        copy.start()
        third.append(copy)
    for copy in third:
        copy.wait_recv()
    fourth = []
    for n in range(1, 16):
        there = gram.at[rows(base, unit)]
        copy = send(there, there, ys2.at[n], yr2.at[n], planes[n][0])
        copy.start()
        fourth.append(copy)
    for copy in fourth:
        copy.wait_recv()
    there = gram.at[rows(k * half, half)]
    last = send(there, there, cs2.at[0], cr2.at[0], sibling)
    last.start()
    last.wait_recv()
    copies += first + second + third + fourth + [last]

    blocks = {}
    for i, (r, s) in enumerate(TRI):
        if i < 14:
            blocks[r, s] = gram[i * 128 : i * 128 + 128, :]
            if r != s:
                blocks[s, r] = blocks[r, s].T
    edge = gram[1792:1856, :]
    lines = []
    for r in range(4):
        lines.append(jnp.concatenate([blocks[r, s] for s in range(5)], axis=1)[:, :KV])
    bottom = [blocks[4, s][:64] for s in range(4)] + [edge]
    lines.append(jnp.concatenate(bottom, axis=1)[:, :KV])
    full = jnp.concatenate(lines, axis=0)
    row = lax.broadcasted_iota(jnp.int32, (KV, KV), 0)
    col = lax.broadcasted_iota(jnp.int32, (KV, KV), 1)
    diagonal = row == col
    squares = jnp.sum(jnp.where(diagonal, full, 0.0))
    norm = jnp.sqrt(jnp.full((1, 1), squares, f32)) + 1e-07
    inv = 1.0 / norm
    a_scr[...] = full * inv * inv

    @pl.when(moving)
    def _():
        move.wait_recv()

    out[...] = rows_in[...] * inv

    def lay_left(ref, value, terms):
        parts = split(value, 3 if terms == 6 else 2)
        for t, (i, _) in enumerate(PAIRS[terms]):
            ref[:, t * LAT : (t + 1) * LAT] = parts[i][:, :LAT]
            at = terms * LAT + t * ROPE
            ref[:, at : at + ROPE] = parts[i][:, LAT:]

    def lay_right(value, terms):
        parts = split(value, 3 if terms == 6 else 2)
        for t, (_, j) in enumerate(PAIRS[terms]):
            right_scr[t * LAT : (t + 1) * LAT, :] = parts[j][:LAT]
            at = terms * LAT + t * ROPE
            right_scr[at : at + ROPE, :] = parts[j][LAT:]

    def symmetric(terms):
        size = terms * KV
        wide = nn(left_scr[:, :size], right_scr[:size, :LAT])
        corner = nn(left_scr[LAT:, :size], right_scr[:size, LAT:])
        return jnp.concatenate([wide, jnp.concatenate([wide[LAT:].T, corner], axis=0)], axis=1)

    def mix(terms):
        a = a_scr[...]
        lay_left(left_scr, a, terms)
        lay_right(a, terms)
        mixing = quintic_b * a + quintic_c * symmetric(terms)
        lay_right(mixing, terms)
        lay_left(thin_scr, out[...], terms)
        size = terms * KV
        out[...] = quintic_a * out[...] + nn(thin_scr[:, :size], right_scr[:size, :])

    def advance(terms):
        b = quintic_a * a_scr[...] + symmetric(terms)
        lay_left(left_scr, b, terms)
        a_scr[...] = quintic_a * b + symmetric(terms)

    mix(6)
    advance(6)

    def iteration(step, _):
        mix(3)
        advance(3)
        return 0

    lax.fori_loop(1, NS_ITERS - 1, iteration, 0)
    mix(3)
    iterate = out[...]
    out[...] = iterate * (0.2 * math.sqrt(D))

    @pl.when(moving)
    def _():
        move.wait_send()

    for copy in copies:
        copy.wait_send()


def muon(g):
    half = PACKED // 2
    sems = [1, 1, 16, 16, 4, 4, 4, 4, 16, 16, 1, 1]
    return pl.pallas_call(
        muon_kernel,
        out_shape=jax.ShapeDtypeStruct((PIECE, KV), f32),
        in_specs=[VMEM],
        out_specs=VMEM,
        scratch_shapes=[
            pltpu.VMEM((PACKED, 128), f32),
            pltpu.VMEM((half, 128), f32),
            pltpu.VMEM((16, half // 16, 128), f32),
            pltpu.VMEM((4, half // 64, 128), f32),
            pltpu.VMEM((half, 128), f32),
            pltpu.VMEM((PACKED, 128), f32),
            pltpu.VMEM((PIECE, KV), f32),
            pltpu.VMEM((KV, KV), f32),
            pltpu.VMEM((KV, 6 * KV), bf16),
            pltpu.VMEM((PIECE, 6 * KV), bf16),
            pltpu.VMEM((6 * KV, KV), bf16),
            pltpu.SemaphoreType.DMA((1,)),
            pltpu.SemaphoreType.DMA((1,)),
        ]
        + [pltpu.SemaphoreType.DMA((n,)) for n in sems],
        compiler_params=pltpu.CompilerParams(
            collective_id=2, has_side_effects=True, vmem_limit_bytes=32 * MiB
        ),
        name="muon",
    )(g)


def per_device(tokens, kv_weight, latent_gain, queries, out_grad, segment_ids):
    tok = tokens[0]
    c = lax.axis_index("ctx")
    positions = c * BLOCK + jnp.arange(BLOCK, dtype=jnp.int32)
    cos, sin = rope_tables(positions)
    gain = latent_gain[None]
    docs = segment_ids[0]
    lanes = jnp.arange(ROPE, dtype=jnp.int32)
    hot = (docs[:, None] == lanes[None]).astype(f32)
    heads = jnp.pad(docs[::TILE_Q].astype(f32), (0, 128 - TILES))[None]
    qt = jnp.transpose(queries[0], (1, 2, 0))
    keys, proj, low, q = make_keys(tok, kv_weight.T, gain, hot, cos, sin, heads, qt)
    keys = keys.reshape(WINDOW, PAD)
    dout = out_grad[0].reshape(BLOCK * HEADS, LAT)
    attended, kg, peak = attention(low.reshape(128), q, dout, hot, keys)
    rows, top = weight_grad(
        kg.reshape(SLOTS, BLOCK, KV), proj, gain, cos, sin, tok, peak
    )
    update = muon(rows)
    return (attended.reshape(1, BLOCK, HEADS, LAT), jnp.max(top.reshape(TILE_Q, HEADS), axis=0), update)


def solution(mesh):
    return jax.shard_map(
        per_device,
        mesh=mesh,
        in_specs=(
            P("fsdp", "ctx", None),
            P("fsdp", None),
            P(),
            P("fsdp", "ctx", None, None),
            P("fsdp", "ctx", None, None),
            P("fsdp", "ctx"),
        ),
        out_specs=(P("fsdp", "ctx", None, None), P(), P(("ctx", "fsdp"), None)),
        check_vma=False,
    )
```

```python
import functools
import math

import jax
import jax.numpy as jnp
from jax import lax
from jax.experimental import pallas as pl
from jax.experimental.pallas import tpu as pltpu
from jax.sharding import PartitionSpec as P

D = 7168
LAT = 512
ROPE = 64
HEADS = 32
NS_ITERS = 5
KV = LAT + ROPE
PAD = 640
HALF = ROPE // 2
BLOCK = 128
REACH = 8
SLOTS = REACH + 1
WINDOW = SLOTS * BLOCK
CTX = 16
FSDP = 8
SHARD = D // FSDP
PIECE = SHARD // CTX
TILE_Q = 16
ROWS = TILE_Q * HEADS
TILES = BLOCK // TILE_Q

attn_scale = 192.0 ** (-0.5)
rope_base = 50000.0
quintic_a = 3.4445
quintic_b = -4.775
quintic_c = 2.0315
BIG = -1e30
MiB = 1 << 20

MESH = pl.DeviceIdType.MESH
VMEM = pl.BlockSpec(memory_space=pltpu.VMEM)
f32, bf16 = jnp.float32, jnp.bfloat16


def rope_tables(positions):
    ladder = jnp.arange(HALF, dtype=f32)
    freqs = jnp.power(rope_base, -2.0 * ladder / ROPE)
    angles = positions.astype(f32)[:, None] * freqs[None, :]
    return (jnp.cos(angles), jnp.sin(angles))


def nn(a, b, **kw):
    return lax.dot_general(a, b, (((1,), (0,)), ((), ())), preferred_element_type=f32, **kw)


def nt(a, b, **kw):
    return lax.dot_general(a, b, (((1,), (1,)), ((), ())), preferred_element_type=f32, **kw)


def tn(a, b, **kw):
    return lax.dot_general(a, b, (((0,), (0,)), ((), ())), preferred_element_type=f32, **kw)


class Place:
    def __init__(self):
        self.c, self.f = lax.axis_index("ctx"), lax.axis_index("fsdp")
        self.y, self.zh, self.k = self.c // 4, (self.c // 2) % 2, self.c % 2
        self.x, self.zl = self.f // 2, self.f % 2

    def at(self, x=None, y=None, zh=None, zl=None, k=None):
        x = self.x if x is None else x
        y = self.y if y is None else y
        zh = self.zh if zh is None else zh
        zl = self.zl if zl is None else zl
        k = self.k if k is None else k
        return ((y * 2 + zh) * 2 + k, x * 2 + zl)

    def ctx(self, c):
        return (c, self.f)

    def fsdp(self, f):
        return (self.c, f)


def greet(devices, others=0):
    barrier = pltpu.get_barrier_semaphore()
    for device in devices:
        pl.semaphore_signal(barrier, inc=1, device_id=device, device_id_type=MESH)
    pl.semaphore_wait(barrier, len(devices) + others)


def send(src, dst, send_sem, recv_sem, device):
    return pltpu.make_async_remote_copy(
        src_ref=src,
        dst_ref=dst,
        send_sem=send_sem,
        recv_sem=recv_sem,
        device_id=device,
        device_id_type=MESH,
    )


def keys_kernel(
    tok, w, gain, hot, cos, sin, heads, qt, keys_out, proj_out, low_out, q_out, wall, win, qin, qrow, qs, ws, wr, ks, kr
):
    me = Place()
    c, k, x = me.c, me.k, me.x
    sibling = me.at(k=1 - k)
    z_same, z_other = me.at(zl=1 - me.zl), me.at(zl=1 - me.zl, zh=1 - me.zh)
    x_up, x_down = me.at(x=(x + 1) % 4), me.at(x=(x + 3) % 4)
    later = [me.ctx((c + 2 * j) % CTX) for j in range(1, 5)]
    earlier = [me.ctx((c - 2 * j + CTX) % CTX) for j in range(1, 5)]
    greet([sibling, z_same, z_other, x_up, x_down] + later + earlier[:3])

    half = KV // 2
    quarter = half // 2
    counter = [0]

    def rows(core, q=None):
        if q is None:
            return pl.ds(pl.multiple_of(core * half, 16), half)
        return pl.ds(pl.multiple_of(core * half + q * quarter, 16), quarter)

    def post(src_f, src, core, q, device):
        i = counter[0]
        counter[0] += 1
        where = rows(core, q)
        source = w.at[where] if src is None else src.at[src_f, where]
        copy = send(source, wall.at[src_f, where], ws.at[i], wr.at[i], device)
        copy.start()
        return copy

    def shard_of(xx, zl):
        return (xx % 4) * 2 + zl

    own = me.f
    up = [post(own, None, k, 0, x_up), post(own, None, k, 1, x_up)]
    down = [post(own, None, k, 1, x_down), post(own, None, k, 0, x_down)]
    own_z = [post(own, None, k, 0, z_same), post(own, None, k, 1, z_other)]
    fetch = pltpu.make_async_copy(qt, qin, qs.at[0])
    fetch.start()
    posted = up + down + own_z

    def forward(copy, shard, q):
        copy.wait_recv()
        z = post(shard, wall, k, q, (z_same, z_other)[q])
        s = post(shard, wall, k, q, sibling)
        posted.extend([z, s])
        return z, s

    def pass_on(copy, shard, q):
        copy.wait_recv()
        s = post(shard, wall, k, q, sibling)
        posted.append(s)
        return s

    other = 1 - me.zl
    f_prev, f_next, f_far = shard_of(x + 3, me.zl), shard_of(x + 1, me.zl), shard_of(x + 2, me.zl)
    o_own, o_prev, o_next, o_far = (shard_of(x + i, other) for i in (0, 3, 1, 2))

    def add(total, shard):
        return total + nt(
            tok[:, pl.ds(pl.multiple_of(shard * SHARD, 128), SHARD)], wall[shard]
        )

    fetch.wait()

    def turn(h, _):
        for lanes in range(PAD // 128):
            width = min(128, KV - lanes * 128)
            block = qin[h, lanes * 128 : lanes * 128 + width, :].astype(f32)
            if width < 128:
                block = jnp.concatenate([block, jnp.zeros((128 - width, BLOCK), f32)], axis=0)
            qrow[lanes, pl.ds(h, BLOCK, stride=HEADS), :] = block.T
        return 0

    lax.fori_loop(0, HEADS // 2, turn, 0)

    prev0 = forward(up[0], f_prev, 0)
    relay_up = post(f_prev, wall, k, 0, x_up)
    next1 = forward(down[0], f_next, 1)
    relay_down = post(f_next, wall, k, 1, x_down)
    posted.extend([relay_up, relay_down])
    s_own = [pass_on(own_z[q], o_own, q) for q in range(2)]
    lax.fori_loop(HEADS // 2, HEADS, turn, 0)
    acc = nt(tok[:, pl.ds(pl.multiple_of(own * SHARD, 128), SHARD)], w[...])
    prev1 = forward(up[1], f_prev, 1)
    next0 = forward(down[1], f_next, 0)
    s_prev0 = pass_on(prev0[0], o_prev, 0)
    s_next1 = pass_on(next1[0], o_next, 1)

    def narrow(i, _):
        rows = pl.ds(pl.multiple_of(i * ROWS, ROWS), ROWS)
        for lanes in range(PAD // 128):
            width = min(128, KV - lanes * 128)
            q_out[rows, lanes * 128 : lanes * 128 + width] = qrow[lanes, rows, :width].astype(bf16)
        return 0

    lax.fori_loop(0, TILES, narrow, 0)
    for copy in s_own:
        copy.wait_recv()
    acc = add(acc, o_own)
    far0 = forward(relay_up, f_far, 0)
    far1 = forward(relay_down, f_far, 1)
    prev0[1].wait_recv()
    prev1[1].wait_recv()
    acc = add(acc, f_prev)
    next0[1].wait_recv()
    next1[1].wait_recv()
    acc = add(acc, f_next)
    s_prev1 = pass_on(prev1[0], o_prev, 1)
    s_next0 = pass_on(next0[0], o_next, 0)
    far0[1].wait_recv()
    far1[1].wait_recv()
    acc = add(acc, f_far)
    s_far0 = pass_on(far0[0], o_far, 0)
    s_far1 = pass_on(far1[0], o_far, 1)
    for shard, pair in ((o_prev, (s_prev0, s_prev1)), (o_next, (s_next0, s_next1)), (o_far, (s_far0, s_far1))):
        for copy in pair:
            copy.wait_recv()
        acc = add(acc, shard)

    compressed = acc[:, :LAT]
    inverse = lax.rsqrt(jnp.mean(compressed * compressed, axis=1, keepdims=True) + 1e-06)
    latent = compressed * inverse * gain[...]
    first, second = acc[:, LAT : LAT + HALF], acc[:, LAT + HALF :]
    mine = win.at[SLOTS - 1]
    mine[:, :LAT] = latent.astype(bf16)
    tail = jnp.concatenate(
        [
            first * cos[...] - second * sin[...],
            second * cos[...] + first * sin[...],
            hot[...],
        ],
        axis=1,
    )
    mine[:, LAT:] = tail.astype(bf16)
    proj_out[...] = acc

    def slot(distance):
        return SLOTS - 1 - distance

    spread = []
    for j in range(1, 5):
        copy = send(mine, win.at[slot(2 * j)], ks.at[j - 1], kr.at[j - 1], later[j - 1])
        copy.start()
        spread.append(copy)
    to_sibling = []

    def give(n):
        copy = send(
            win.at[slot(2 * n + 2 * k)], win.at[slot(2 * n + 1)], ks.at[4 + n], kr.at[4 + n], sibling
        )
        copy.start()
        to_sibling.append(copy)

    spread[0].wait_recv()
    give(0)
    give_next = 1
    for j in range(1, 4):
        spread[j].wait_recv()
        give(give_next)
        give_next += 1
    for copy in to_sibling:
        copy.wait_recv()
    lane = lax.broadcasted_iota(jnp.int32, (BLOCK, 128), 1)
    flag = jnp.where(lane == ROPE + 8, 1.0, 0.0)
    for d in range(REACH + 1):
        keys_out[slot(d)] = win[slot(d)]
        if d > 0:

            @pl.when(c < d)
            def _(d=d):
                keys_out[slot(d), :, LAT:] = flag.astype(bf16)

    before = jnp.zeros((1, 128), f32)
    weight = jnp.where(
        lane < ROPE, 0.0, jnp.where(lane < ROPE + 8, (lane - ROPE).astype(f32), jnp.where(lane == ROPE + 8, -1.0, 0.0))
    )
    for d in range(SLOTS):
        code = keys_out[d, :, LAT:].astype(f32)
        document = jnp.sum(code * weight, axis=1, keepdims=True)
        before = before + jnp.sum(jnp.where(document < heads[...], 1.0, 0.0), axis=0, keepdims=True)
    low_out[...] = (before * (1.0 / BLOCK)).astype(jnp.int32)
    for copy in posted + spread + to_sibling:
        copy.wait_send()


N_W = 6 + 2 + 6 * 2 + 8


def make_keys(tok, w, gain, hot, cos, sin, heads, qt):
    return pl.pallas_call(
        keys_kernel,
        out_shape=(
            jax.ShapeDtypeStruct((SLOTS, BLOCK, PAD), bf16),
            jax.ShapeDtypeStruct((BLOCK, KV), f32),
            jax.ShapeDtypeStruct((1, 128), jnp.int32),
            jax.ShapeDtypeStruct((BLOCK * HEADS, KV), bf16),
        ),
        in_specs=[VMEM] * 7 + [pl.BlockSpec(memory_space=pl.ANY)],
        out_specs=(VMEM,) * 4,
        scratch_shapes=[
            pltpu.VMEM((FSDP, KV, SHARD), bf16),
            pltpu.VMEM((SLOTS, BLOCK, PAD), bf16),
            pltpu.VMEM((HEADS, KV, BLOCK), bf16),
            pltpu.VMEM((PAD // 128, BLOCK * HEADS, 128), f32),
            pltpu.SemaphoreType.DMA((1,)),
            pltpu.SemaphoreType.DMA((N_W,)),
            pltpu.SemaphoreType.DMA((N_W,)),
            pltpu.SemaphoreType.DMA((8,)),
            pltpu.SemaphoreType.DMA((8,)),
        ],
        compiler_params=pltpu.CompilerParams(
            collective_id=0, has_side_effects=True, vmem_limit_bytes=48 * MiB
        ),
        name="keys",
    )(tok, w, gain, hot, cos, sin, heads, qt)


def attention_kernel(
    low, q, dout, hot, keys, att_out, grad_out, peak_out, vt, qr, s_scr, d_scr, p_scr
):
    t = pl.program_id(0)

    @pl.when(t == 0)
    def _():
        grad_out[...] = jnp.zeros_like(grad_out)
        peak_out[...] = jnp.full_like(peak_out, BIG)
        for j in range(SLOTS):
            vt[:, j * BLOCK : (j + 1) * BLOCK] = keys[j * BLOCK : (j + 1) * BLOCK, :LAT].T

    qr[:, :ROPE] = q[:, LAT:]
    lane = lax.broadcasted_iota(jnp.int32, (TILE_Q, ROPE), 1)
    qmask = jnp.where((lane < 9) & (hot[...] == 0.0), BIG, 0.0)
    spread = jnp.broadcast_to(qmask[:, None, :], (TILE_Q, HEADS, ROPE))
    qr[:, ROPE:] = spread.reshape(ROWS, ROPE).astype(bf16)

    def run(first):
        here = slice(first * BLOCK, WINDOW)
        own = slice(WINDOW - BLOCK, WINDOW)
        s_scr[here, :] = nt(keys[here, :LAT], q[:, :LAT]) + nt(keys[here, LAT:], qr[...])
        d_scr[here, :] = nt(keys[here, :LAT], dout[...])
        key = lax.broadcasted_iota(jnp.int32, (BLOCK, ROWS), 0)
        query = t * TILE_Q + lax.broadcasted_iota(jnp.int32, (BLOCK, ROWS), 1) // HEADS
        s_scr[own, :] = jnp.where(key <= query, s_scr[own, :], BIG)
        peak = jnp.max(s_scr[here, :], axis=0, keepdims=True)
        peak_out[...] = jnp.maximum(peak_out[...], peak * attn_scale)
        total = jnp.zeros((1, ROWS), f32)
        for j in range(first, SLOTS):
            at = slice(j * BLOCK, (j + 1) * BLOCK)
            e = jnp.exp((s_scr[at, :] - peak) * attn_scale)
            s_scr[at, :] = e
            total = total + jnp.sum(e, axis=0, keepdims=True)
        share = 1.0 / total
        for j in range(first, SLOTS):
            at = slice(j * BLOCK, (j + 1) * BLOCK)
            p_scr[at, :] = (s_scr[at, :] * share).astype(bf16)
        attended = nn(vt[:, here], p_scr[here, :]).T.astype(bf16)
        grad_out[here, :LAT] += nn(p_scr[here, :], dout[...])
        att_out[...] = attended
        delta = jnp.sum(dout[...].astype(f32) * attended.astype(f32), axis=1, keepdims=True)
        delta = jnp.broadcast_to(delta, (ROWS, 128)).T[:1, :]
        share = share * attn_scale
        for j in range(first, SLOTS):
            at = slice(j * BLOCK, (j + 1) * BLOCK)
            p_scr[at, :] = (s_scr[at, :] * share * (d_scr[at, :] - delta)).astype(bf16)
        grad_out[here, :] += nn(p_scr[here, :], q[...])

    for first in range(SLOTS):

        @pl.when(low[t] == first)
        def _(first=first):
            run(first)


def attention(low, q, dout, hot, keys):
    per_tile = lambda width: pl.BlockSpec((ROWS, width), lambda t, low: (t, 0))
    whole = lambda *shape: pl.BlockSpec(shape, lambda t, low: (0, 0))
    flops = 2 * BLOCK * HEADS * WINDOW // 2 * (2 * KV + 3 * LAT)
    return pl.pallas_call(
        attention_kernel,
        grid_spec=pltpu.PrefetchScalarGridSpec(
            num_scalar_prefetch=1,
            grid=(TILES,),
            in_specs=[
                per_tile(KV),
                per_tile(LAT),
                pl.BlockSpec((TILE_Q, ROPE), lambda t, low: (t, 0)),
                whole(WINDOW, PAD),
            ],
            out_specs=[per_tile(LAT), whole(WINDOW, KV), whole(8, ROWS)],
            scratch_shapes=[
                pltpu.VMEM((LAT, WINDOW), bf16),
                pltpu.VMEM((ROWS, 128), bf16),
                pltpu.VMEM((WINDOW, ROWS), f32),
                pltpu.VMEM((WINDOW, ROWS), f32),
                pltpu.VMEM((WINDOW, ROWS), bf16),
            ],
        ),
        out_shape=(
            jax.ShapeDtypeStruct((BLOCK * HEADS, LAT), bf16),
            jax.ShapeDtypeStruct((WINDOW, KV), f32),
            jax.ShapeDtypeStruct((8, ROWS), f32),
        ),
        compiler_params=pltpu.CompilerParams(
            dimension_semantics=("arbitrary",), vmem_limit_bytes=32 * MiB
        ),
        cost_estimate=pl.CostEstimate(
            flops=flops, bytes_accessed=16 << 20, transcendentals=BLOCK * HEADS * WINDOW
        ),
        name="attention",
    )(low, q, dout, hot, keys)


def grads_kernel(
    kg, proj, gain, cos, sin, tok, peak, rows_out, peak_out,
    near, outbox, far, kvg, peaks, tok_in, tok_t, part, part_in, sums, sums_in,
    ns, nr, fs, fr, gs, gr, ps, pr, ss, sr, ts, tr, as_, ar,
):
    me = Place()
    c, k, f = me.c, me.k, me.f
    sibling = me.at(k=1 - k)
    back = [me.ctx((c - 2 * j + CTX) % CTX) for j in range(1, 8)]
    peers = [me.fsdp((f + s) % FSDP) for s in range(1, FSDP)]
    greet([sibling] + back + peers)

    def slot(distance):
        return SLOTS - 1 - distance

    swaps = []
    for n in range(4):
        copy = send(kg.at[slot(2 * n + 1)], near.at[n], ns.at[n], nr.at[n], sibling)
        copy.start()
        swaps.append(copy)
    tokens = []
    for s in range(1, FSDP):
        columns = pl.ds(pl.multiple_of(((f + s) % FSDP) * SHARD, 128), SHARD)
        copy = send(tok.at[:, columns], tok_in.at[s], as_.at[s - 1], ar.at[s - 1], peers[s - 1])
        copy.start()
        tokens.append(copy)
    gathers = []
    for s in range(1, FSDP):
        copy = send(peak, peaks.at[s], ps.at[s - 1], pr.at[s - 1], peers[s - 1])
        copy.start()
        gathers.append(copy)
    sends = []
    own = kg[slot(0)]
    for copy in swaps:
        copy.wait_recv()

    @pl.when(k == 1)
    def _():
        for n in range(4):
            outbox[n] = near[n] + kg[slot(2 * n + 2)]

    @pl.when(k == 0)
    def _():
        for n in range(3):
            outbox[n] = near[n + 1] + kg[slot(2 * n + 2)]
        outbox[3] = kg[slot(8)]

    own = own + jnp.where(k == 0, near[0], jnp.zeros_like(own))
    for n in range(4):
        copy = send(outbox.at[n], far.at[n], fs.at[n], fr.at[n], back[n])
        copy.start()
        sends.append(copy)
    tok_t[:, :BLOCK] = tok[:, pl.ds(pl.multiple_of(f * SHARD, 128), SHARD)].T
    for s in range(1, FSDP):
        tokens[s - 1].wait_recv()
        tok_t[:, s * BLOCK : (s + 1) * BLOCK] = tok_in[s].T
    for copy in sends:
        copy.wait_recv()
    key_grad = own
    for n in range(4):
        key_grad = key_grad + far[n]

    compressed = proj[:, :LAT]
    inverse = lax.rsqrt(jnp.mean(compressed * compressed, axis=1, keepdims=True) + 1e-06)
    first, second = key_grad[:, LAT : LAT + HALF], key_grad[:, LAT + HALF :]
    d_first = first * cos[...] + second * sin[...]
    d_second = -first * sin[...] + second * cos[...]
    scaled = key_grad[:, :LAT] * gain[...]
    inner = jnp.mean(compressed * scaled, axis=1, keepdims=True)
    d_comp = inverse * (scaled - compressed * (inverse * inverse * inner))
    kvg[0, :, :LAT] = d_comp.astype(bf16)
    kvg[0, :, LAT:] = jnp.concatenate([d_first, d_second], axis=1).astype(bf16)
    spread = []
    for s in range(1, FSDP):
        copy = send(kvg.at[0], kvg.at[s], gs.at[s - 1], gr.at[s - 1], peers[s - 1])
        copy.start()
        spread.append(copy)
    top = peak[...]
    for s in range(1, FSDP):
        gathers[s - 1].wait_recv()
        top = jnp.maximum(top, peaks[s])
    for copy in spread:
        copy.wait_recv()

    everything = kvg[...].reshape(FSDP * BLOCK, KV)

    def multiply(n, core):
        p = 2 * n + core
        rows = pl.ds(pl.multiple_of(p * PIECE, 8), PIECE)
        return nn(tok_t[rows, :], everything)

    whole = nn(tok_t[...], everything)
    for p in range(CTX):
        part[p, :, :KV] = whole[p * PIECE : (p + 1) * PIECE]
        for r in range(8):
            part[p, r : r + 1, KV:] = top[r : r + 1, r * ROPE : (r + 1) * ROPE]
    halves = []
    for n in range(CTX // 2):
        copy = send(part.at[2 * n + 1 - k], part_in.at[n], ss.at[n], sr.at[n], sibling)
        copy.start()
        halves.append(copy)
    totals = []
    me_n = c // 2
    for n in range(CTX // 2):
        halves[n].wait_recv()
        here = part.at[2 * n + k]
        sums[n, :, :KV] = here[:, :KV] + part_in[n, :, :KV]
        sums[n, :8, KV:] = jnp.maximum(here[:8, KV:], part_in[n, :8, KV:])
    for s in range(1, CTX // 2):
        to = (me_n - s + 8) % 8
        copy = send(sums.at[to], sums_in.at[s], ts.at[s], tr.at[s], back[s - 1])
        copy.start()
        totals.append(copy)
    rows = sums[me_n, :, :KV]
    top = sums[me_n, :8, KV:]
    for s in range(1, CTX // 2):
        totals[s - 1].wait_recv()
        rows = rows + sums_in[s, :, :KV]
        top = jnp.maximum(top, sums_in[s, :8, KV:])
    rows_out[...] = rows
    peak_out[...] = top
    for copy in swaps + tokens + gathers + sends + spread + halves + totals:
        copy.wait_send()


def weight_grad(kg, proj, gain, cos, sin, tok, peak):
    sems = [4, 4, 4, 4, 7, 7, 7, 7, 8, 8, 8, 8, 7, 7]
    return pl.pallas_call(
        grads_kernel,
        out_shape=(
            jax.ShapeDtypeStruct((PIECE, KV), f32),
            jax.ShapeDtypeStruct((8, ROPE), f32),
        ),
        in_specs=[VMEM] * 7,
        out_specs=(VMEM, VMEM),
        scratch_shapes=[
            pltpu.VMEM((4, BLOCK, KV), f32),
            pltpu.VMEM((4, BLOCK, KV), f32),
            pltpu.VMEM((4, BLOCK, KV), f32),
            pltpu.VMEM((FSDP, BLOCK, KV), bf16),
            pltpu.VMEM((FSDP, 8, ROWS), f32),
            pltpu.VMEM((FSDP, BLOCK, SHARD), bf16),
            pltpu.VMEM((SHARD, FSDP * BLOCK), bf16),
            pltpu.VMEM((CTX, PIECE, PAD), f32),
            pltpu.VMEM((CTX // 2, PIECE, PAD), f32),
            pltpu.VMEM((CTX // 2, PIECE, PAD), f32),
            pltpu.VMEM((CTX // 2, PIECE, PAD), f32),
        ]
        + [pltpu.SemaphoreType.DMA((n,)) for n in sems],
        compiler_params=pltpu.CompilerParams(
            collective_id=1, has_side_effects=True, vmem_limit_bytes=32 * MiB
        ),
        name="weight_grad",
    )(kg, proj, gain, cos, sin, tok, peak)


TRI = [(r, s) for r in range(5) for s in range(r, 5)]
PACKED = 2048
PAIRS = {3: [(0, 0), (0, 1), (1, 0)], 6: [(0, 0), (0, 1), (1, 0), (0, 2), (2, 0), (1, 1)]}


def split(value, count):
    parts = []
    for _ in range(count):
        part = value.astype(bf16)
        parts.append(part)
        value = value - part.astype(f32)
    return parts


def muon_kernel(
    g, out, pack, core_in, yz_in, x_in, acc, gram, rows_in, a_scr, left_scr, thin_scr, right_scr, ms, mr, cs, cr, ys, yr, xs, xr, xs2, xr2, ys2, yr2, cs2, cr2
):
    me = Place()
    k, x, y = me.k, me.x, me.y
    z = me.zh * 2 + me.zl
    sibling = me.at(k=1 - k)

    def plane(n):
        yy, zz = (y + n // 4) % 4, (z + n % 4) % 4
        return me.at(y=yy, zh=zz // 2, zl=zz % 2), yy * 4 + zz

    planes = [plane(n) for n in range(16)]
    line = [me.at(x=(x + s) % 4) for s in range(4)]
    give = me.f * CTX + me.c
    take = me.c * FSDP + me.f
    moving = give != take
    barrier = pltpu.get_barrier_semaphore()

    @pl.when(moving)
    def _():
        pl.semaphore_signal(
            barrier, inc=1, device_id=(take % CTX, take // CTX), device_id_type=MESH
        )

    friends = [sibling] + [p[0] for p in planes[1:]] + line[1:]
    greet(friends, jnp.where(moving, 1, 0))
    move = send(g, rows_in, ms.at[0], mr.at[0], (give // FSDP, give % FSDP))

    grad = g[...]
    parts = [
        jnp.concatenate([p.astype(f32), jnp.zeros((8, KV), f32)], axis=0).astype(bf16)
        for p in split(grad, 3)
    ]
    left = jnp.concatenate([parts[i] for i, _ in PAIRS[6]], axis=0)
    right = jnp.concatenate([parts[j] for _, j in PAIRS[6]], axis=0)
    local = tn(left, right)
    for i, (r, s) in enumerate(TRI[:14]):
        width = min(128, KV - s * 128)
        pack[i * 128 : i * 128 + 128, :width] = local[r * 128 : r * 128 + 128, s * 128 : s * 128 + width]
    pack[1792:1856, :64] = local[512:, 512:]
    pack[1856:, :] = jnp.zeros((PACKED - 1856, 128), f32)

    half = PACKED // 2
    unit = half // 16
    small = unit // 4

    def rows(start, size):
        return pl.ds(pl.multiple_of(start, 8), size)

    copies = []
    swap = send(pack.at[rows((1 - k) * half, half)], core_in, cs.at[0], cr.at[0], sibling)
    swap.start()

    @pl.when(moving)
    def _():
        move.start()

    @pl.when(jnp.logical_not(moving))
    def _():
        rows_in[...] = grad

    swap.wait_recv()
    acc[...] = pack[rows(k * half, half), :] + core_in[...]
    copies.append(swap)
    mine = y * 4 + z
    first = []
    for n in range(1, 16):
        device, index = planes[n]
        copy = send(acc.at[rows(index * unit, unit)], yz_in.at[n], ys.at[n], yr.at[n], device)
        copy.start()
        first.append(copy)
    total = acc[rows(mine * unit, unit), :]
    for n in range(1, 16):
        first[n - 1].wait_recv()
        total = total + yz_in[n]
    yz_in[0] = total
    second = []
    for s in range(1, 4):
        to = (x + s) % 4
        copy = send(yz_in.at[0, rows(to * small, small)], x_in.at[s], xs.at[s], xr.at[s], line[s])
        copy.start()
        second.append(copy)
    total = yz_in[0, rows(x * small, small), :]
    for s in range(1, 4):
        second[s - 1].wait_recv()
        total = total + x_in[s]
    base = k * half + mine * unit
    gram[rows(base + x * small, small), :] = total
    third = []
    for s in range(1, 4):
        there = gram.at[rows(base + x * small, small)]
        copy = send(there, there, xs2.at[s], xr2.at[s], line[s])
        copy.start()
        third.append(copy)
    for copy in third:
        copy.wait_recv()
    fourth = []
    for n in range(1, 16):
        there = gram.at[rows(base, unit)]
        copy = send(there, there, ys2.at[n], yr2.at[n], planes[n][0])
        copy.start()
        fourth.append(copy)
    for copy in fourth:
        copy.wait_recv()
    there = gram.at[rows(k * half, half)]
    last = send(there, there, cs2.at[0], cr2.at[0], sibling)
    last.start()
    last.wait_recv()
    copies += first + second + third + fourth + [last]

    blocks = {}
    for i, (r, s) in enumerate(TRI):
        if i < 14:
            blocks[r, s] = gram[i * 128 : i * 128 + 128, :]
            if r != s:
                blocks[s, r] = blocks[r, s].T
    edge = gram[1792:1856, :]
    lines = []
    for r in range(4):
        lines.append(jnp.concatenate([blocks[r, s] for s in range(5)], axis=1)[:, :KV])
    bottom = [blocks[4, s][:64] for s in range(4)] + [edge]
    lines.append(jnp.concatenate(bottom, axis=1)[:, :KV])
    full = jnp.concatenate(lines, axis=0)
    row = lax.broadcasted_iota(jnp.int32, (KV, KV), 0)
    col = lax.broadcasted_iota(jnp.int32, (KV, KV), 1)
    diagonal = row == col
    squares = jnp.sum(jnp.where(diagonal, full, 0.0))
    norm = jnp.sqrt(jnp.full((1, 1), squares, f32)) + 1e-07
    inv = 1.0 / norm
    a_scr[...] = full * inv * inv

    @pl.when(moving)
    def _():
        move.wait_recv()

    out[...] = rows_in[...] * inv

    def lay_left(ref, value, terms):
        parts = split(value, 3 if terms == 6 else 2)
        for t, (i, _) in enumerate(PAIRS[terms]):
            ref[:, t * LAT : (t + 1) * LAT] = parts[i][:, :LAT]
            at = terms * LAT + t * ROPE
            ref[:, at : at + ROPE] = parts[i][:, LAT:]

    def lay_right(value, terms):
        parts = split(value, 3 if terms == 6 else 2)
        for t, (_, j) in enumerate(PAIRS[terms]):
            right_scr[t * LAT : (t + 1) * LAT, :] = parts[j][:LAT]
            at = terms * LAT + t * ROPE
            right_scr[at : at + ROPE, :] = parts[j][LAT:]

    def symmetric(terms):
        size = terms * KV
        wide = nn(left_scr[:, :size], right_scr[:size, :LAT])
        corner = nn(left_scr[LAT:, :size], right_scr[:size, LAT:])
        return jnp.concatenate([wide, jnp.concatenate([wide[LAT:].T, corner], axis=0)], axis=1)

    def mix(terms):
        a = a_scr[...]
        lay_left(left_scr, a, terms)
        lay_right(a, terms)
        mixing = quintic_b * a + quintic_c * symmetric(terms)
        lay_right(mixing, terms)
        lay_left(thin_scr, out[...], terms)
        size = terms * KV
        out[...] = quintic_a * out[...] + nn(thin_scr[:, :size], right_scr[:size, :])

    def advance(terms):
        b = quintic_a * a_scr[...] + symmetric(terms)
        lay_left(left_scr, b, terms)
        a_scr[...] = quintic_a * b + symmetric(terms)

    mix(6)
    advance(6)

    def iteration(step, _):
        mix(3)
        advance(3)
        return 0

    lax.fori_loop(1, NS_ITERS - 1, iteration, 0)
    mix(3)
    iterate = out[...]
    out[...] = iterate * (0.2 * math.sqrt(D))

    @pl.when(moving)
    def _():
        move.wait_send()

    for copy in copies:
        copy.wait_send()


def muon(g):
    half = PACKED // 2
    sems = [1, 1, 16, 16, 4, 4, 4, 4, 16, 16, 1, 1]
    return pl.pallas_call(
        muon_kernel,
        out_shape=jax.ShapeDtypeStruct((PIECE, KV), f32),
        in_specs=[VMEM],
        out_specs=VMEM,
        scratch_shapes=[
            pltpu.VMEM((PACKED, 128), f32),
            pltpu.VMEM((half, 128), f32),
            pltpu.VMEM((16, half // 16, 128), f32),
            pltpu.VMEM((4, half // 64, 128), f32),
            pltpu.VMEM((half, 128), f32),
            pltpu.VMEM((PACKED, 128), f32),
            pltpu.VMEM((PIECE, KV), f32),
            pltpu.VMEM((KV, KV), f32),
            pltpu.VMEM((KV, 6 * KV), bf16),
            pltpu.VMEM((PIECE, 6 * KV), bf16),
            pltpu.VMEM((6 * KV, KV), bf16),
            pltpu.SemaphoreType.DMA((1,)),
            pltpu.SemaphoreType.DMA((1,)),
        ]
        + [pltpu.SemaphoreType.DMA((n,)) for n in sems],
        compiler_params=pltpu.CompilerParams(
            collective_id=2, has_side_effects=True, vmem_limit_bytes=32 * MiB
        ),
        name="muon",
    )(g)


def per_device(tokens, kv_weight, latent_gain, queries, out_grad, segment_ids):
    tok = tokens[0]
    c = lax.axis_index("ctx")
    positions = c * BLOCK + jnp.arange(BLOCK, dtype=jnp.int32)
    cos, sin = rope_tables(positions)
    gain = latent_gain[None]
    docs = segment_ids[0]
    lanes = jnp.arange(ROPE, dtype=jnp.int32)
    hot = (docs[:, None] == lanes[None]).astype(f32)
    heads = jnp.pad(docs[::TILE_Q].astype(f32), (0, 128 - TILES))[None]
    qt = jnp.transpose(queries[0], (1, 2, 0))
    keys, proj, low, q = make_keys(tok, kv_weight.T, gain, hot, cos, sin, heads, qt)
    keys = keys.reshape(WINDOW, PAD)
    dout = out_grad[0].reshape(BLOCK * HEADS, LAT)
    attended, kg, peak = attention(low.reshape(128), q, dout, hot, keys)
    rows, top = weight_grad(
        kg.reshape(SLOTS, BLOCK, KV), proj, gain, cos, sin, tok, peak
    )
    update = muon(rows)
    return (attended.reshape(1, BLOCK, HEADS, LAT), jnp.max(top.reshape(TILE_Q, HEADS), axis=0), update)


def solution(mesh):
    return jax.shard_map(
        per_device,
        mesh=mesh,
        in_specs=(
            P("fsdp", "ctx", None),
            P("fsdp", None),
            P(),
            P("fsdp", "ctx", None, None),
            P("fsdp", "ctx", None, None),
            P("fsdp", "ctx"),
        ),
        out_specs=(P("fsdp", "ctx", None, None), P(), P(("ctx", "fsdp"), None)),
        check_vma=False,
    )
```

```python
import functools
import math

import jax
import jax.numpy as jnp
from jax import lax
from jax.experimental import pallas as pl
from jax.experimental.pallas import tpu as pltpu
from jax.sharding import PartitionSpec as P

D = 7168
LAT = 512
ROPE = 64
HEADS = 32
NS_ITERS = 5
KV = LAT + ROPE
PAD = 640
HALF = ROPE // 2
BLOCK = 128
REACH = 8
SLOTS = REACH + 1
WINDOW = SLOTS * BLOCK
CTX = 16
FSDP = 8
SHARD = D // FSDP
PIECE = SHARD // CTX
TILE_Q = 16
ROWS = TILE_Q * HEADS
TILES = BLOCK // TILE_Q

attn_scale = 192.0 ** (-0.5)
rope_base = 50000.0
quintic_a = 3.4445
quintic_b = -4.775
quintic_c = 2.0315
BIG = -1e30
MiB = 1 << 20

MESH = pl.DeviceIdType.MESH
VMEM = pl.BlockSpec(memory_space=pltpu.VMEM)
ANY = pl.BlockSpec(memory_space=pl.ANY)
f32, bf16 = jnp.float32, jnp.bfloat16


def rope_tables(positions):
    ladder = jnp.arange(HALF, dtype=f32)
    freqs = jnp.power(rope_base, -2.0 * ladder / ROPE)
    angles = positions.astype(f32)[:, None] * freqs[None, :]
    return (jnp.cos(angles), jnp.sin(angles))


def nn(a, b, **kw):
    return lax.dot_general(a, b, (((1,), (0,)), ((), ())), preferred_element_type=f32, **kw)


def nt(a, b, **kw):
    return lax.dot_general(a, b, (((1,), (1,)), ((), ())), preferred_element_type=f32, **kw)


def tn(a, b, **kw):
    return lax.dot_general(a, b, (((0,), (0,)), ((), ())), preferred_element_type=f32, **kw)


class Place:
    def __init__(self):
        self.c, self.f = lax.axis_index("ctx"), lax.axis_index("fsdp")
        self.y, self.zh, self.k = self.c // 4, (self.c // 2) % 2, self.c % 2
        self.x, self.zl = self.f // 2, self.f % 2

    def at(self, x=None, y=None, zh=None, zl=None, k=None):
        x = self.x if x is None else x
        y = self.y if y is None else y
        zh = self.zh if zh is None else zh
        zl = self.zl if zl is None else zl
        k = self.k if k is None else k
        return ((y * 2 + zh) * 2 + k, x * 2 + zl)

    def ctx(self, c):
        return (c, self.f)

    def fsdp(self, f):
        return (self.c, f)


def greet(devices, others=0):
    barrier = pltpu.get_barrier_semaphore()
    for device in devices:
        pl.semaphore_signal(barrier, inc=1, device_id=device, device_id_type=MESH)
    pl.semaphore_wait(barrier, len(devices) + others)


def send(src, dst, send_sem, recv_sem, device):
    return pltpu.make_async_remote_copy(
        src_ref=src,
        dst_ref=dst,
        send_sem=send_sem,
        recv_sem=recv_sem,
        device_id=device,
        device_id_type=MESH,
    )


def keys_kernel(
    tok_hbm, w, gain, hot, cos, sin, qt, keys_out, proj_out, q_out, wall, win, tok, qin, qrow, qs, ws, wr, ks, kr
):
    me = Place()
    c, k, x = me.c, me.k, me.x
    sibling = me.at(k=1 - k)
    z_same, z_other = me.at(zl=1 - me.zl), me.at(zl=1 - me.zl, zh=1 - me.zh)
    x_up, x_down = me.at(x=(x + 1) % 4), me.at(x=(x + 3) % 4)
    later = [me.ctx((c + 2 * j) % CTX) for j in range(1, 5)]
    earlier = [me.ctx((c - 2 * j + CTX) % CTX) for j in range(1, 5)]
    greet([sibling, z_same, z_other, x_up, x_down] + later + earlier[:3])

    half = KV // 2
    quarter = half // 2
    counter = [0]

    def rows(core, q=None):
        if q is None:
            return pl.ds(pl.multiple_of(core * half, 16), half)
        return pl.ds(pl.multiple_of(core * half + q * quarter, 16), quarter)

    def post(src_f, src, core, q, device):
        i = counter[0]
        counter[0] += 1
        where = rows(core, q)
        source = w.at[where] if src is None else src.at[src_f, where]
        copy = send(source, wall.at[src_f, where], ws.at[i], wr.at[i], device)
        copy.start()
        return copy

    def shard_of(xx, zl):
        return (xx % 4) * 2 + zl

    own = me.f
    up = [post(own, None, k, 0, x_up), post(own, None, k, 1, x_up)]
    down = [post(own, None, k, 1, x_down), post(own, None, k, 0, x_down)]
    own_z = [post(own, None, k, 0, z_same), post(own, None, k, 1, z_other)]
    fetch = pltpu.make_async_copy(qt, qin, qs.at[0])
    fetch.start()
    fetch_w = pltpu.make_async_copy(w, wall.at[own], qs.at[1])
    fetch_w.start()
    fetch_tok = pltpu.make_async_copy(tok_hbm, tok, qs.at[2])
    fetch_tok.start()
    posted = up + down + own_z

    def forward(copy, shard, q):
        copy.wait_recv()
        z = post(shard, wall, k, q, (z_same, z_other)[q])
        s = post(shard, wall, k, q, sibling)
        posted.extend([z, s])
        return z, s

    def pass_on(copy, shard, q):
        copy.wait_recv()
        s = post(shard, wall, k, q, sibling)
        posted.append(s)
        return s

    other = 1 - me.zl
    f_prev, f_next, f_far = shard_of(x + 3, me.zl), shard_of(x + 1, me.zl), shard_of(x + 2, me.zl)
    o_own, o_prev, o_next, o_far = (shard_of(x + i, other) for i in (0, 3, 1, 2))

    def add(total, shard):
        return total + nt(
            tok[:, pl.ds(pl.multiple_of(shard * SHARD, 128), SHARD)], wall[shard]
        )

    fetch.wait()

    def turn(h, _):
        for lanes in range(PAD // 128):
            width = min(128, KV - lanes * 128)
            block = qin[h, lanes * 128 : lanes * 128 + width, :].astype(f32)
            if width < 128:
                block = jnp.concatenate([block, jnp.zeros((128 - width, BLOCK), f32)], axis=0)
            qrow[lanes, pl.ds(h, BLOCK, stride=HEADS), :] = block.T
        return 0

    lax.fori_loop(0, HEADS // 2, turn, 0)

    prev0 = forward(up[0], f_prev, 0)
    relay_up = post(f_prev, wall, k, 0, x_up)
    next1 = forward(down[0], f_next, 1)
    relay_down = post(f_next, wall, k, 1, x_down)
    posted.extend([relay_up, relay_down])
    s_own = [pass_on(own_z[q], o_own, q) for q in range(2)]
    lax.fori_loop(HEADS // 2, HEADS, turn, 0)
    fetch_w.wait()
    fetch_tok.wait()
    acc = nt(tok[:, pl.ds(pl.multiple_of(own * SHARD, 128), SHARD)], wall[own])
    prev1 = forward(up[1], f_prev, 1)
    next0 = forward(down[1], f_next, 0)
    s_prev0 = pass_on(prev0[0], o_prev, 0)
    s_next1 = pass_on(next1[0], o_next, 1)

    def narrow(i, _):
        rows = pl.ds(pl.multiple_of(i * ROWS, ROWS), ROWS)
        for lanes in range(PAD // 128):
            width = min(128, KV - lanes * 128)
            q_out[rows, lanes * 128 : lanes * 128 + width] = qrow[lanes, rows, :width].astype(bf16)
        return 0

    lax.fori_loop(0, TILES, narrow, 0)
    for copy in s_own:
        copy.wait_recv()
    acc = add(acc, o_own)
    far0 = forward(relay_up, f_far, 0)
    far1 = forward(relay_down, f_far, 1)
    prev0[1].wait_recv()
    prev1[1].wait_recv()
    acc = add(acc, f_prev)
    next0[1].wait_recv()
    next1[1].wait_recv()
    acc = add(acc, f_next)
    s_prev1 = pass_on(prev1[0], o_prev, 1)
    s_next0 = pass_on(next0[0], o_next, 0)
    far0[1].wait_recv()
    far1[1].wait_recv()
    acc = add(acc, f_far)
    s_far0 = pass_on(far0[0], o_far, 0)
    s_far1 = pass_on(far1[0], o_far, 1)
    for shard, pair in ((o_prev, (s_prev0, s_prev1)), (o_next, (s_next0, s_next1)), (o_far, (s_far0, s_far1))):
        for copy in pair:
            copy.wait_recv()
        acc = add(acc, shard)

    compressed = acc[:, :LAT]
    inverse = lax.rsqrt(jnp.mean(compressed * compressed, axis=1, keepdims=True) + 1e-06)
    latent = compressed * inverse * gain[...]
    first, second = acc[:, LAT : LAT + HALF], acc[:, LAT + HALF :]
    mine = win.at[SLOTS - 1]
    mine[:, :LAT] = latent.astype(bf16)
    tail = jnp.concatenate(
        [
            first * cos[...] - second * sin[...],
            second * cos[...] + first * sin[...],
            hot[...],
        ],
        axis=1,
    )
    mine[:, LAT:] = tail.astype(bf16)
    proj_out[...] = acc

    def slot(distance):
        return SLOTS - 1 - distance

    spread = []
    for j in range(1, 5):
        copy = send(mine, win.at[slot(2 * j)], ks.at[j - 1], kr.at[j - 1], later[j - 1])
        copy.start()
        spread.append(copy)
    to_sibling = []

    def give(n):
        copy = send(
            win.at[slot(2 * n + 2 * k)], win.at[slot(2 * n + 1)], ks.at[4 + n], kr.at[4 + n], sibling
        )
        copy.start()
        to_sibling.append(copy)

    spread[0].wait_recv()
    give(0)
    give_next = 1
    for j in range(1, 4):
        spread[j].wait_recv()
        give(give_next)
        give_next += 1
    for copy in to_sibling:
        copy.wait_recv()
    lane = lax.broadcasted_iota(jnp.int32, (BLOCK, 128), 1)
    flag = jnp.where(lane == ROPE + 8, 1.0, 0.0)
    for d in range(REACH + 1):
        keys_out[slot(d)] = win[slot(d)]
        if d > 0:

            @pl.when(c < d)
            def _(d=d):
                keys_out[slot(d), :, LAT:] = flag.astype(bf16)

    for copy in posted + spread + to_sibling:
        copy.wait_send()


N_W = 6 + 2 + 6 * 2 + 8


def make_keys(tok, w, gain, hot, cos, sin, qt):
    return pl.pallas_call(
        keys_kernel,
        out_shape=(
            jax.ShapeDtypeStruct((SLOTS, BLOCK, PAD), bf16),
            jax.ShapeDtypeStruct((BLOCK, KV), f32),
            jax.ShapeDtypeStruct((BLOCK * HEADS, KV), bf16),
        ),
        in_specs=[ANY, ANY] + [VMEM] * 4 + [ANY],
        out_specs=(VMEM,) * 3,
        scratch_shapes=[
            pltpu.VMEM((FSDP, KV, SHARD), bf16),
            pltpu.VMEM((SLOTS, BLOCK, PAD), bf16),
            pltpu.VMEM((BLOCK, D), bf16),
            pltpu.VMEM((HEADS, KV, BLOCK), bf16),
            pltpu.VMEM((PAD // 128, BLOCK * HEADS, 128), f32),
            pltpu.SemaphoreType.DMA((3,)),
            pltpu.SemaphoreType.DMA((N_W,)),
            pltpu.SemaphoreType.DMA((N_W,)),
            pltpu.SemaphoreType.DMA((8,)),
            pltpu.SemaphoreType.DMA((8,)),
        ],
        compiler_params=pltpu.CompilerParams(
            collective_id=0, has_side_effects=True, vmem_limit_bytes=48 * MiB
        ),
        name="keys",
    )(tok, w, gain, hot, cos, sin, qt)


def attention_kernel(
    q, dout, hot, keys, att_out, grad_out, peak_out, vt, qr, s_scr, d_scr, p_scr
):
    t = pl.program_id(0)

    @pl.when(t == 0)
    def _():
        grad_out[...] = jnp.zeros_like(grad_out)
        peak_out[...] = jnp.full_like(peak_out, BIG)
        for j in range(SLOTS):
            vt[:, j * BLOCK : (j + 1) * BLOCK] = keys[j * BLOCK : (j + 1) * BLOCK, :LAT].T

    qr[:, :ROPE] = q[:, LAT:]
    lane = lax.broadcasted_iota(jnp.int32, (TILE_Q, ROPE), 1)
    qmask = jnp.where((lane < 9) & (hot[...] == 0.0), BIG, 0.0)
    spread = jnp.broadcast_to(qmask[:, None, :], (TILE_Q, HEADS, ROPE))
    qr[:, ROPE:] = spread.reshape(ROWS, ROPE).astype(bf16)

    own = slice(WINDOW - BLOCK, WINDOW)
    s_scr[...] = nt(keys[:, :LAT], q[:, :LAT]) + nt(keys[:, LAT:], qr[...])
    d_scr[...] = nt(keys[:, :LAT], dout[...])
    key = lax.broadcasted_iota(jnp.int32, (BLOCK, ROWS), 0)
    query = t * TILE_Q + lax.broadcasted_iota(jnp.int32, (BLOCK, ROWS), 1) // HEADS
    s_scr[own, :] = jnp.where(key <= query, s_scr[own, :], BIG)
    peak = jnp.max(s_scr[...], axis=0, keepdims=True)
    peak_out[...] = jnp.maximum(peak_out[...], peak * attn_scale)
    total = jnp.zeros((1, ROWS), f32)
    for j in range(SLOTS):
        at = slice(j * BLOCK, (j + 1) * BLOCK)
        e = jnp.exp((s_scr[at, :] - peak) * attn_scale)
        s_scr[at, :] = e
        total = total + jnp.sum(e, axis=0, keepdims=True)
    share = 1.0 / total
    for j in range(SLOTS):
        at = slice(j * BLOCK, (j + 1) * BLOCK)
        p_scr[at, :] = (s_scr[at, :] * share).astype(bf16)
    attended = nn(vt[...], p_scr[...]).T.astype(bf16)
    grad_out[:, :LAT] += nn(p_scr[...], dout[...])
    att_out[...] = attended
    delta = jnp.sum(dout[...].astype(f32) * attended.astype(f32), axis=1, keepdims=True)
    delta = jnp.broadcast_to(delta, (ROWS, 128)).T[:1, :]
    share = share * attn_scale
    for j in range(SLOTS):
        at = slice(j * BLOCK, (j + 1) * BLOCK)
        p_scr[at, :] = (s_scr[at, :] * share * (d_scr[at, :] - delta)).astype(bf16)
    grad_out[...] += nn(p_scr[...], q[...])


def attention(q, dout, hot, keys):
    per_tile = lambda width: pl.BlockSpec((ROWS, width), lambda t: (t, 0))
    whole = lambda *shape: pl.BlockSpec(shape, lambda t: (0, 0))
    flops = 2 * BLOCK * HEADS * WINDOW // 2 * (2 * KV + 3 * LAT)
    return pl.pallas_call(
        attention_kernel,
        grid=(TILES,),
        in_specs=[
            per_tile(KV),
            per_tile(LAT),
            pl.BlockSpec((TILE_Q, ROPE), lambda t: (t, 0)),
            whole(WINDOW, PAD),
        ],
        out_specs=[per_tile(LAT), whole(WINDOW, KV), whole(8, ROWS)],
        scratch_shapes=[
            pltpu.VMEM((LAT, WINDOW), bf16),
            pltpu.VMEM((ROWS, 128), bf16),
            pltpu.VMEM((WINDOW, ROWS), f32),
            pltpu.VMEM((WINDOW, ROWS), f32),
            pltpu.VMEM((WINDOW, ROWS), bf16),
        ],
        out_shape=(
            jax.ShapeDtypeStruct((BLOCK * HEADS, LAT), bf16),
            jax.ShapeDtypeStruct((WINDOW, KV), f32),
            jax.ShapeDtypeStruct((8, ROWS), f32),
        ),
        compiler_params=pltpu.CompilerParams(
            dimension_semantics=("arbitrary",), vmem_limit_bytes=32 * MiB
        ),
        cost_estimate=pl.CostEstimate(
            flops=flops, bytes_accessed=16 << 20, transcendentals=BLOCK * HEADS * WINDOW
        ),
        name="attention",
    )(q, dout, hot, keys)


def grads_kernel(
    kg, proj, gain, cos, sin, tok, peak, rows_out, peak_out,
    near, outbox, far, kvg, peaks, tok_in, tok_t, part, part_in, sums, sums_in,
    ns, nr, fs, fr, gs, gr, ps, pr, ss, sr, ts, tr, as_, ar,
):
    me = Place()
    c, k, f = me.c, me.k, me.f
    sibling = me.at(k=1 - k)
    back = [me.ctx((c - 2 * j + CTX) % CTX) for j in range(1, 8)]
    peers = [me.fsdp((f + s) % FSDP) for s in range(1, FSDP)]
    greet([sibling] + back + peers)

    def slot(distance):
        return SLOTS - 1 - distance

    swaps = []
    for n in range(4):
        copy = send(kg.at[slot(2 * n + 1)], near.at[n], ns.at[n], nr.at[n], sibling)
        copy.start()
        swaps.append(copy)
    tokens = []
    for s in range(1, FSDP):
        columns = pl.ds(pl.multiple_of(((f + s) % FSDP) * SHARD, 128), SHARD)
        copy = send(tok.at[:, columns], tok_in.at[s], as_.at[s - 1], ar.at[s - 1], peers[s - 1])
        copy.start()
        tokens.append(copy)
    gathers = []
    for s in range(1, FSDP):
        copy = send(peak, peaks.at[s], ps.at[s - 1], pr.at[s - 1], peers[s - 1])
        copy.start()
        gathers.append(copy)
    sends = []
    own = kg[slot(0)]
    for copy in swaps:
        copy.wait_recv()

    @pl.when(k == 1)
    def _():
        for n in range(4):
            outbox[n] = near[n] + kg[slot(2 * n + 2)]

    @pl.when(k == 0)
    def _():
        for n in range(3):
            outbox[n] = near[n + 1] + kg[slot(2 * n + 2)]
        outbox[3] = kg[slot(8)]

    own = own + jnp.where(k == 0, near[0], jnp.zeros_like(own))
    for n in range(4):
        copy = send(outbox.at[n], far.at[n], fs.at[n], fr.at[n], back[n])
        copy.start()
        sends.append(copy)
    tok_t[:, :BLOCK] = tok[:, pl.ds(pl.multiple_of(f * SHARD, 128), SHARD)].T
    for s in range(1, FSDP):
        tokens[s - 1].wait_recv()
        tok_t[:, s * BLOCK : (s + 1) * BLOCK] = tok_in[s].T
    for copy in sends:
        copy.wait_recv()
    key_grad = own
    for n in range(4):
        key_grad = key_grad + far[n]

    compressed = proj[:, :LAT]
    inverse = lax.rsqrt(jnp.mean(compressed * compressed, axis=1, keepdims=True) + 1e-06)
    first, second = key_grad[:, LAT : LAT + HALF], key_grad[:, LAT + HALF :]
    d_first = first * cos[...] + second * sin[...]
    d_second = -first * sin[...] + second * cos[...]
    scaled = key_grad[:, :LAT] * gain[...]
    inner = jnp.mean(compressed * scaled, axis=1, keepdims=True)
    d_comp = inverse * (scaled - compressed * (inverse * inverse * inner))
    kvg[0, :, :LAT] = d_comp.astype(bf16)
    kvg[0, :, LAT:] = jnp.concatenate([d_first, d_second], axis=1).astype(bf16)
    spread = []
    for s in range(1, FSDP):
        copy = send(kvg.at[0], kvg.at[s], gs.at[s - 1], gr.at[s - 1], peers[s - 1])
        copy.start()
        spread.append(copy)
    top = peak[...]
    for s in range(1, FSDP):
        gathers[s - 1].wait_recv()
        top = jnp.maximum(top, peaks[s])
    for copy in spread:
        copy.wait_recv()

    everything = kvg[...].reshape(FSDP * BLOCK, KV)

    def multiply(n, core):
        p = 2 * n + core
        rows = pl.ds(pl.multiple_of(p * PIECE, 8), PIECE)
        return nn(tok_t[rows, :], everything)

    whole = nn(tok_t[...], everything)
    for p in range(CTX):
        part[p, :, :KV] = whole[p * PIECE : (p + 1) * PIECE]
        for r in range(8):
            part[p, r : r + 1, KV:] = top[r : r + 1, r * ROPE : (r + 1) * ROPE]
    halves = []
    for n in range(CTX // 2):
        copy = send(part.at[2 * n + 1 - k], part_in.at[n], ss.at[n], sr.at[n], sibling)
        copy.start()
        halves.append(copy)
    totals = []
    me_n = c // 2
    for n in range(CTX // 2):
        halves[n].wait_recv()
        here = part.at[2 * n + k]
        sums[n, :, :KV] = here[:, :KV] + part_in[n, :, :KV]
        sums[n, :8, KV:] = jnp.maximum(here[:8, KV:], part_in[n, :8, KV:])
    for s in range(1, CTX // 2):
        to = (me_n - s + 8) % 8
        copy = send(sums.at[to], sums_in.at[s], ts.at[s], tr.at[s], back[s - 1])
        copy.start()
        totals.append(copy)
    rows = sums[me_n, :, :KV]
    top = sums[me_n, :8, KV:]
    for s in range(1, CTX // 2):
        totals[s - 1].wait_recv()
        rows = rows + sums_in[s, :, :KV]
        top = jnp.maximum(top, sums_in[s, :8, KV:])
    rows_out[...] = rows
    peak_out[...] = top
    for copy in swaps + tokens + gathers + sends + spread + halves + totals:
        copy.wait_send()


def weight_grad(kg, proj, gain, cos, sin, tok, peak):
    sems = [4, 4, 4, 4, 7, 7, 7, 7, 8, 8, 8, 8, 7, 7]
    return pl.pallas_call(
        grads_kernel,
        out_shape=(
            jax.ShapeDtypeStruct((PIECE, KV), f32),
            jax.ShapeDtypeStruct((8, ROPE), f32),
        ),
        in_specs=[VMEM] * 7,
        out_specs=(VMEM, VMEM),
        scratch_shapes=[
            pltpu.VMEM((4, BLOCK, KV), f32),
            pltpu.VMEM((4, BLOCK, KV), f32),
            pltpu.VMEM((4, BLOCK, KV), f32),
            pltpu.VMEM((FSDP, BLOCK, KV), bf16),
            pltpu.VMEM((FSDP, 8, ROWS), f32),
            pltpu.VMEM((FSDP, BLOCK, SHARD), bf16),
            pltpu.VMEM((SHARD, FSDP * BLOCK), bf16),
            pltpu.VMEM((CTX, PIECE, PAD), f32),
            pltpu.VMEM((CTX // 2, PIECE, PAD), f32),
            pltpu.VMEM((CTX // 2, PIECE, PAD), f32),
            pltpu.VMEM((CTX // 2, PIECE, PAD), f32),
        ]
        + [pltpu.SemaphoreType.DMA((n,)) for n in sems],
        compiler_params=pltpu.CompilerParams(
            collective_id=1, has_side_effects=True, vmem_limit_bytes=32 * MiB
        ),
        name="weight_grad",
    )(kg, proj, gain, cos, sin, tok, peak)


TRI = [(r, s) for r in range(5) for s in range(r, 5)]
PACKED = 2048
PAIRS = {3: [(0, 0), (0, 1), (1, 0)], 6: [(0, 0), (0, 1), (1, 0), (0, 2), (2, 0), (1, 1)]}


def split(value, count):
    parts = []
    for _ in range(count):
        part = value.astype(bf16)
        parts.append(part)
        value = value - part.astype(f32)
    return parts


def muon_kernel(
    g, out, pack, core_in, yz_in, x_in, acc, gram, rows_in, a_scr, left_scr, thin_scr, right_scr, ms, mr, cs, cr, ys, yr, xs, xr, xs2, xr2, ys2, yr2, cs2, cr2
):
    me = Place()
    k, x, y = me.k, me.x, me.y
    z = me.zh * 2 + me.zl
    sibling = me.at(k=1 - k)

    def plane(n):
        yy, zz = (y + n // 4) % 4, (z + n % 4) % 4
        return me.at(y=yy, zh=zz // 2, zl=zz % 2), yy * 4 + zz

    planes = [plane(n) for n in range(16)]
    line = [me.at(x=(x + s) % 4) for s in range(4)]
    give = me.f * CTX + me.c
    take = me.c * FSDP + me.f
    moving = give != take
    barrier = pltpu.get_barrier_semaphore()

    @pl.when(moving)
    def _():
        pl.semaphore_signal(
            barrier, inc=1, device_id=(take % CTX, take // CTX), device_id_type=MESH
        )

    friends = [sibling] + [p[0] for p in planes[1:]] + line[1:]
    greet(friends, jnp.where(moving, 1, 0))
    move = send(g, rows_in, ms.at[0], mr.at[0], (give // FSDP, give % FSDP))

    grad = g[...]
    parts = [
        jnp.concatenate([p.astype(f32), jnp.zeros((8, KV), f32)], axis=0).astype(bf16)
        for p in split(grad, 3)
    ]
    left = jnp.concatenate([parts[i] for i, _ in PAIRS[6]], axis=0)
    right = jnp.concatenate([parts[j] for _, j in PAIRS[6]], axis=0)
    local = tn(left, right)
    for i, (r, s) in enumerate(TRI[:14]):
        width = min(128, KV - s * 128)
        pack[i * 128 : i * 128 + 128, :width] = local[r * 128 : r * 128 + 128, s * 128 : s * 128 + width]
    pack[1792:1856, :64] = local[512:, 512:]
    pack[1856:, :] = jnp.zeros((PACKED - 1856, 128), f32)

    half = PACKED // 2
    unit = half // 16
    small = unit // 4

    def rows(start, size):
        return pl.ds(pl.multiple_of(start, 8), size)

    copies = []
    swap = send(pack.at[rows((1 - k) * half, half)], core_in, cs.at[0], cr.at[0], sibling)
    swap.start()

    @pl.when(moving)
    def _():
        move.start()

    @pl.when(jnp.logical_not(moving))
    def _():
        rows_in[...] = grad

    swap.wait_recv()
    acc[...] = pack[rows(k * half, half), :] + core_in[...]
    copies.append(swap)
    mine = y * 4 + z
    first = []
    for n in range(1, 16):
        device, index = planes[n]
        copy = send(acc.at[rows(index * unit, unit)], yz_in.at[n], ys.at[n], yr.at[n], device)
        copy.start()
        first.append(copy)
    total = acc[rows(mine * unit, unit), :]
    for n in range(1, 16):
        first[n - 1].wait_recv()
        total = total + yz_in[n]
    yz_in[0] = total
    second = []
    for s in range(1, 4):
        to = (x + s) % 4
        copy = send(yz_in.at[0, rows(to * small, small)], x_in.at[s], xs.at[s], xr.at[s], line[s])
        copy.start()
        second.append(copy)
    total = yz_in[0, rows(x * small, small), :]
    for s in range(1, 4):
        second[s - 1].wait_recv()
        total = total + x_in[s]
    base = k * half + mine * unit
    gram[rows(base + x * small, small), :] = total
    third = []
    for s in range(1, 4):
        there = gram.at[rows(base + x * small, small)]
        copy = send(there, there, xs2.at[s], xr2.at[s], line[s])
        copy.start()
        third.append(copy)
    for copy in third:
        copy.wait_recv()
    fourth = []
    for n in range(1, 16):
        there = gram.at[rows(base, unit)]
        copy = send(there, there, ys2.at[n], yr2.at[n], planes[n][0])
        copy.start()
        fourth.append(copy)
    for copy in fourth:
        copy.wait_recv()
    there = gram.at[rows(k * half, half)]
    last = send(there, there, cs2.at[0], cr2.at[0], sibling)
    last.start()
    last.wait_recv()
    copies += first + second + third + fourth + [last]

    blocks = {}
    for i, (r, s) in enumerate(TRI):
        if i < 14:
            blocks[r, s] = gram[i * 128 : i * 128 + 128, :]
            if r != s:
                blocks[s, r] = blocks[r, s].T
    edge = gram[1792:1856, :]
    lines = []
    for r in range(4):
        lines.append(jnp.concatenate([blocks[r, s] for s in range(5)], axis=1)[:, :KV])
    bottom = [blocks[4, s][:64] for s in range(4)] + [edge]
    lines.append(jnp.concatenate(bottom, axis=1)[:, :KV])
    full = jnp.concatenate(lines, axis=0)
    row = lax.broadcasted_iota(jnp.int32, (KV, KV), 0)
    col = lax.broadcasted_iota(jnp.int32, (KV, KV), 1)
    diagonal = row == col
    squares = jnp.sum(jnp.where(diagonal, full, 0.0))
    norm = jnp.sqrt(jnp.full((1, 1), squares, f32)) + 1e-07
    inv = 1.0 / norm
    a_scr[...] = full * inv * inv

    @pl.when(moving)
    def _():
        move.wait_recv()

    out[...] = rows_in[...] * inv

    def lay_left(ref, value, terms):
        parts = split(value, 3 if terms == 6 else 2)
        for t, (i, _) in enumerate(PAIRS[terms]):
            ref[:, t * LAT : (t + 1) * LAT] = parts[i][:, :LAT]
            at = terms * LAT + t * ROPE
            ref[:, at : at + ROPE] = parts[i][:, LAT:]

    def lay_right(value, terms):
        parts = split(value, 3 if terms == 6 else 2)
        for t, (_, j) in enumerate(PAIRS[terms]):
            right_scr[t * LAT : (t + 1) * LAT, :] = parts[j][:LAT]
            at = terms * LAT + t * ROPE
            right_scr[at : at + ROPE, :] = parts[j][LAT:]

    def symmetric(terms):
        size = terms * KV
        wide = nn(left_scr[:, :size], right_scr[:size, :LAT])
        corner = nn(left_scr[LAT:, :size], right_scr[:size, LAT:])
        return jnp.concatenate([wide, jnp.concatenate([wide[LAT:].T, corner], axis=0)], axis=1)

    def mix(terms):
        a = a_scr[...]
        lay_left(left_scr, a, terms)
        lay_right(a, terms)
        mixing = quintic_b * a + quintic_c * symmetric(terms)
        lay_right(mixing, terms)
        lay_left(thin_scr, out[...], terms)
        size = terms * KV
        out[...] = quintic_a * out[...] + nn(thin_scr[:, :size], right_scr[:size, :])

    def advance(terms):
        b = quintic_a * a_scr[...] + symmetric(terms)
        lay_left(left_scr, b, terms)
        a_scr[...] = quintic_a * b + symmetric(terms)

    mix(6)
    advance(6)

    def iteration(step, _):
        mix(3)

        @pl.when(step < NS_ITERS - 1)
        def _():
            advance(3)

        return 0

    lax.fori_loop(1, NS_ITERS, iteration, 0)
    iterate = out[...]
    out[...] = iterate * (0.2 * math.sqrt(D))

    @pl.when(moving)
    def _():
        move.wait_send()

    for copy in copies:
        copy.wait_send()


def muon(g):
    half = PACKED // 2
    sems = [1, 1, 16, 16, 4, 4, 4, 4, 16, 16, 1, 1]
    return pl.pallas_call(
        muon_kernel,
        out_shape=jax.ShapeDtypeStruct((PIECE, KV), f32),
        in_specs=[VMEM],
        out_specs=VMEM,
        scratch_shapes=[
            pltpu.VMEM((PACKED, 128), f32),
            pltpu.VMEM((half, 128), f32),
            pltpu.VMEM((16, half // 16, 128), f32),
            pltpu.VMEM((4, half // 64, 128), f32),
            pltpu.VMEM((half, 128), f32),
            pltpu.VMEM((PACKED, 128), f32),
            pltpu.VMEM((PIECE, KV), f32),
            pltpu.VMEM((KV, KV), f32),
            pltpu.VMEM((KV, 6 * KV), bf16),
            pltpu.VMEM((PIECE, 6 * KV), bf16),
            pltpu.VMEM((6 * KV, KV), bf16),
            pltpu.SemaphoreType.DMA((1,)),
            pltpu.SemaphoreType.DMA((1,)),
        ]
        + [pltpu.SemaphoreType.DMA((n,)) for n in sems],
        compiler_params=pltpu.CompilerParams(
            collective_id=2, has_side_effects=True, vmem_limit_bytes=32 * MiB
        ),
        name="muon",
    )(g)


def per_device(tokens, kv_weight, latent_gain, queries, out_grad, segment_ids):
    tok = tokens[0]
    c = lax.axis_index("ctx")
    positions = c * BLOCK + jnp.arange(BLOCK, dtype=jnp.int32)
    cos, sin = rope_tables(positions)
    gain = latent_gain[None]
    docs = segment_ids[0]
    lanes = jnp.arange(ROPE, dtype=jnp.int32)
    hot = (docs[:, None] == lanes[None]).astype(f32)
    qt = jnp.transpose(queries[0], (1, 2, 0))
    keys, proj, q = make_keys(tok, kv_weight.T, gain, hot, cos, sin, qt)
    keys = keys.reshape(WINDOW, PAD)
    dout = out_grad[0].reshape(BLOCK * HEADS, LAT)
    attended, kg, peak = attention(q, dout, hot, keys)
    rows, top = weight_grad(
        kg.reshape(SLOTS, BLOCK, KV), proj, gain, cos, sin, tok, peak
    )
    update = muon(rows)
    return (attended.reshape(1, BLOCK, HEADS, LAT), jnp.max(top.reshape(TILE_Q, HEADS), axis=0), update)


def solution(mesh):
    return jax.shard_map(
        per_device,
        mesh=mesh,
        in_specs=(
            P("fsdp", "ctx", None),
            P("fsdp", None),
            P(),
            P("fsdp", "ctx", None, None),
            P("fsdp", "ctx", None, None),
            P("fsdp", "ctx"),
        ),
        out_specs=(P("fsdp", "ctx", None, None), P(), P(("ctx", "fsdp"), None)),
        check_vma=False,
    )
```

```python
import functools
import math

import jax
import jax.numpy as jnp
from jax import lax
from jax.experimental import pallas as pl
from jax.experimental.pallas import tpu as pltpu
from jax.sharding import PartitionSpec as P

D = 7168
LAT = 512
ROPE = 64
HEADS = 32
NS_ITERS = 5
KV = LAT + ROPE
PAD = 640
HALF = ROPE // 2
BLOCK = 128
REACH = 8
SLOTS = REACH + 1
WINDOW = SLOTS * BLOCK
CTX = 16
FSDP = 8
SHARD = D // FSDP
PIECE = SHARD // CTX
TILE_Q = 16
ROWS = TILE_Q * HEADS
TILES = BLOCK // TILE_Q

attn_scale = 192.0 ** (-0.5)
rope_base = 50000.0
quintic_a = 3.4445
quintic_b = -4.775
quintic_c = 2.0315
BIG = -1e30
MiB = 1 << 20

MESH = pl.DeviceIdType.MESH
VMEM = pl.BlockSpec(memory_space=pltpu.VMEM)
HBM = pl.BlockSpec(memory_space=pltpu.HBM)
f32, bf16 = jnp.float32, jnp.bfloat16


def rope_tables(positions):
    ladder = jnp.arange(HALF, dtype=f32)
    freqs = jnp.power(rope_base, -2.0 * ladder / ROPE)
    angles = positions.astype(f32)[:, None] * freqs[None, :]
    return (jnp.cos(angles), jnp.sin(angles))


def nn(a, b, **kw):
    return lax.dot_general(a, b, (((1,), (0,)), ((), ())), preferred_element_type=f32, **kw)


def nt(a, b, **kw):
    return lax.dot_general(a, b, (((1,), (1,)), ((), ())), preferred_element_type=f32, **kw)


def tn(a, b, **kw):
    return lax.dot_general(a, b, (((0,), (0,)), ((), ())), preferred_element_type=f32, **kw)


class Place:
    def __init__(self):
        self.c, self.f = lax.axis_index("ctx"), lax.axis_index("fsdp")
        self.y, self.zh, self.k = self.c // 4, (self.c // 2) % 2, self.c % 2
        self.x, self.zl = self.f // 2, self.f % 2

    def at(self, x=None, y=None, zh=None, zl=None, k=None):
        x = self.x if x is None else x
        y = self.y if y is None else y
        zh = self.zh if zh is None else zh
        zl = self.zl if zl is None else zl
        k = self.k if k is None else k
        return ((y * 2 + zh) * 2 + k, x * 2 + zl)

    def ctx(self, c):
        return (c, self.f)

    def fsdp(self, f):
        return (self.c, f)


def greet(devices, others=0):
    barrier = pltpu.get_barrier_semaphore()
    for device in devices:
        pl.semaphore_signal(barrier, inc=1, device_id=device, device_id_type=MESH)
    pl.semaphore_wait(barrier, len(devices) + others)


def send(src, dst, send_sem, recv_sem, device):
    return pltpu.make_async_remote_copy(
        src_ref=src,
        dst_ref=dst,
        send_sem=send_sem,
        recv_sem=recv_sem,
        device_id=device,
        device_id_type=MESH,
    )


def keys_kernel(
    tok_hbm, w, gain, hot, cos, sin, qt, keys_out, proj_out, q_out, wall, win, tok, qin, qrow, qs, ws, wr, ks, kr
):
    me = Place()
    c, k, x = me.c, me.k, me.x
    sibling = me.at(k=1 - k)
    z_same, z_other = me.at(zl=1 - me.zl), me.at(zl=1 - me.zl, zh=1 - me.zh)
    x_up, x_down = me.at(x=(x + 1) % 4), me.at(x=(x + 3) % 4)
    later = [me.ctx((c + 2 * j) % CTX) for j in range(1, 5)]
    earlier = [me.ctx((c - 2 * j + CTX) % CTX) for j in range(1, 5)]
    greet([sibling, z_same, z_other, x_up, x_down] + later + earlier[:3])

    half = KV // 2
    quarter = half // 2
    counter = [0]

    def rows(core, q=None):
        if q is None:
            return pl.ds(pl.multiple_of(core * half, 16), half)
        return pl.ds(pl.multiple_of(core * half + q * quarter, 16), quarter)

    def post(src_f, src, core, q, device):
        i = counter[0]
        counter[0] += 1
        where = rows(core, q)
        source = w.at[where] if src is None else src.at[src_f, where]
        copy = send(source, wall.at[src_f, where], ws.at[i], wr.at[i], device)
        copy.start()
        return copy

    def shard_of(xx, zl):
        return (xx % 4) * 2 + zl

    own = me.f
    up = [post(own, None, k, 0, x_up), post(own, None, k, 1, x_up)]
    down = [post(own, None, k, 1, x_down), post(own, None, k, 0, x_down)]
    own_z = [post(own, None, k, 0, z_same), post(own, None, k, 1, z_other)]
    fetch = pltpu.make_async_copy(qt, qin, qs.at[0])
    fetch.start()
    fetch_w = pltpu.make_async_copy(w, wall.at[own], qs.at[1])
    fetch_w.start()
    fetch_tok = pltpu.make_async_copy(tok_hbm, tok, qs.at[2])
    fetch_tok.start()
    posted = up + down + own_z

    def forward(copy, shard, q):
        copy.wait_recv()
        z = post(shard, wall, k, q, (z_same, z_other)[q])
        s = post(shard, wall, k, q, sibling)
        posted.extend([z, s])
        return z, s

    def pass_on(copy, shard, q):
        copy.wait_recv()
        s = post(shard, wall, k, q, sibling)
        posted.append(s)
        return s

    other = 1 - me.zl
    f_prev, f_next, f_far = shard_of(x + 3, me.zl), shard_of(x + 1, me.zl), shard_of(x + 2, me.zl)
    o_own, o_prev, o_next, o_far = (shard_of(x + i, other) for i in (0, 3, 1, 2))

    def add(total, shard):
        return total + nt(
            tok[:, pl.ds(pl.multiple_of(shard * SHARD, 128), SHARD)], wall[shard]
        )

    fetch.wait()

    def turn(h, _):
        for lanes in range(PAD // 128):
            width = min(128, KV - lanes * 128)
            block = qin[h, lanes * 128 : lanes * 128 + width, :].astype(f32)
            if width < 128:
                block = jnp.concatenate([block, jnp.zeros((128 - width, BLOCK), f32)], axis=0)
            qrow[lanes, pl.ds(h, BLOCK, stride=HEADS), :] = block.T
        return 0

    lax.fori_loop(0, HEADS // 2, turn, 0)

    prev0 = forward(up[0], f_prev, 0)
    relay_up = post(f_prev, wall, k, 0, x_up)
    next1 = forward(down[0], f_next, 1)
    relay_down = post(f_next, wall, k, 1, x_down)
    posted.extend([relay_up, relay_down])
    s_own = [pass_on(own_z[q], o_own, q) for q in range(2)]
    lax.fori_loop(HEADS // 2, HEADS, turn, 0)
    fetch_w.wait()
    fetch_tok.wait()
    acc = nt(tok[:, pl.ds(pl.multiple_of(own * SHARD, 128), SHARD)], wall[own])
    prev1 = forward(up[1], f_prev, 1)
    next0 = forward(down[1], f_next, 0)
    s_prev0 = pass_on(prev0[0], o_prev, 0)
    s_next1 = pass_on(next1[0], o_next, 1)

    def narrow(i, _):
        rows = pl.ds(pl.multiple_of(i * ROWS, ROWS), ROWS)
        for lanes in range(PAD // 128):
            width = min(128, KV - lanes * 128)
            q_out[rows, lanes * 128 : lanes * 128 + width] = qrow[lanes, rows, :width].astype(bf16)
        return 0

    lax.fori_loop(0, TILES, narrow, 0)
    for copy in s_own:
        copy.wait_recv()
    acc = add(acc, o_own)
    far0 = forward(relay_up, f_far, 0)
    far1 = forward(relay_down, f_far, 1)
    prev0[1].wait_recv()
    prev1[1].wait_recv()
    acc = add(acc, f_prev)
    next0[1].wait_recv()
    next1[1].wait_recv()
    acc = add(acc, f_next)
    s_prev1 = pass_on(prev1[0], o_prev, 1)
    s_next0 = pass_on(next0[0], o_next, 0)
    far0[1].wait_recv()
    far1[1].wait_recv()
    acc = add(acc, f_far)
    s_far0 = pass_on(far0[0], o_far, 0)
    s_far1 = pass_on(far1[0], o_far, 1)
    for shard, pair in ((o_prev, (s_prev0, s_prev1)), (o_next, (s_next0, s_next1)), (o_far, (s_far0, s_far1))):
        for copy in pair:
            copy.wait_recv()
        acc = add(acc, shard)

    compressed = acc[:, :LAT]
    inverse = lax.rsqrt(jnp.mean(compressed * compressed, axis=1, keepdims=True) + 1e-06)
    latent = compressed * inverse * gain[...]
    first, second = acc[:, LAT : LAT + HALF], acc[:, LAT + HALF :]
    mine = win.at[SLOTS - 1]
    mine[:, :LAT] = latent.astype(bf16)
    tail = jnp.concatenate(
        [
            first * cos[...] - second * sin[...],
            second * cos[...] + first * sin[...],
            hot[...],
        ],
        axis=1,
    )
    mine[:, LAT:] = tail.astype(bf16)
    proj_out[...] = acc

    def slot(distance):
        return SLOTS - 1 - distance

    spread = []
    for j in range(1, 5):
        copy = send(mine, win.at[slot(2 * j)], ks.at[j - 1], kr.at[j - 1], later[j - 1])
        copy.start()
        spread.append(copy)
    to_sibling = []

    def give(n):
        copy = send(
            win.at[slot(2 * n + 2 * k)], win.at[slot(2 * n + 1)], ks.at[4 + n], kr.at[4 + n], sibling
        )
        copy.start()
        to_sibling.append(copy)

    spread[0].wait_recv()
    give(0)
    give_next = 1
    for j in range(1, 4):
        spread[j].wait_recv()
        give(give_next)
        give_next += 1
    for copy in to_sibling:
        copy.wait_recv()
    lane = lax.broadcasted_iota(jnp.int32, (BLOCK, 128), 1)
    flag = jnp.where(lane == ROPE + 8, 1.0, 0.0)
    for d in range(REACH + 1):
        keys_out[slot(d)] = win[slot(d)]
        if d > 0:

            @pl.when(c < d)
            def _(d=d):
                keys_out[slot(d), :, LAT:] = flag.astype(bf16)

    for copy in posted + spread + to_sibling:
        copy.wait_send()


N_W = 6 + 2 + 6 * 2 + 8


def make_keys(tok, w, gain, hot, cos, sin, qt):
    return pl.pallas_call(
        keys_kernel,
        out_shape=(
            jax.ShapeDtypeStruct((SLOTS, BLOCK, PAD), bf16),
            jax.ShapeDtypeStruct((BLOCK, KV), f32),
            jax.ShapeDtypeStruct((BLOCK * HEADS, KV), bf16),
        ),
        in_specs=[HBM, HBM] + [VMEM] * 4 + [HBM],
        out_specs=(VMEM,) * 3,
        scratch_shapes=[
            pltpu.VMEM((FSDP, KV, SHARD), bf16),
            pltpu.VMEM((SLOTS, BLOCK, PAD), bf16),
            pltpu.VMEM((BLOCK, D), bf16),
            pltpu.VMEM((HEADS, KV, BLOCK), bf16),
            pltpu.VMEM((PAD // 128, BLOCK * HEADS, 128), f32),
            pltpu.SemaphoreType.DMA((3,)),
            pltpu.SemaphoreType.DMA((N_W,)),
            pltpu.SemaphoreType.DMA((N_W,)),
            pltpu.SemaphoreType.DMA((8,)),
            pltpu.SemaphoreType.DMA((8,)),
        ],
        compiler_params=pltpu.CompilerParams(
            collective_id=0, has_side_effects=True, vmem_limit_bytes=58 * MiB
        ),
        name="keys",
    )(tok, w, gain, hot, cos, sin, qt)


def attention_kernel(
    q, dout, hot, keys, att_out, grad_out, peak_out, vt, qr, s_scr, d_scr, p_scr
):
    t = pl.program_id(0)

    @pl.when(t == 0)
    def _():
        grad_out[...] = jnp.zeros_like(grad_out)
        peak_out[...] = jnp.full_like(peak_out, BIG)
        for j in range(SLOTS):
            vt[:, j * BLOCK : (j + 1) * BLOCK] = keys[j * BLOCK : (j + 1) * BLOCK, :LAT].T

    qr[:, :ROPE] = q[:, LAT:]
    lane = lax.broadcasted_iota(jnp.int32, (TILE_Q, ROPE), 1)
    qmask = jnp.where((lane < 9) & (hot[...] == 0.0), BIG, 0.0)
    spread = jnp.broadcast_to(qmask[:, None, :], (TILE_Q, HEADS, ROPE))
    qr[:, ROPE:] = spread.reshape(ROWS, ROPE).astype(bf16)

    own = slice(WINDOW - BLOCK, WINDOW)
    s_scr[...] = nt(keys[:, :LAT], q[:, :LAT]) + nt(keys[:, LAT:], qr[...])
    d_scr[...] = nt(keys[:, :LAT], dout[...])
    key = lax.broadcasted_iota(jnp.int32, (BLOCK, ROWS), 0)
    query = t * TILE_Q + lax.broadcasted_iota(jnp.int32, (BLOCK, ROWS), 1) // HEADS
    s_scr[own, :] = jnp.where(key <= query, s_scr[own, :], BIG)
    peak = jnp.max(s_scr[...], axis=0, keepdims=True)
    peak_out[...] = jnp.maximum(peak_out[...], peak * attn_scale)
    total = jnp.zeros((1, ROWS), f32)
    for j in range(SLOTS):
        at = slice(j * BLOCK, (j + 1) * BLOCK)
        e = jnp.exp((s_scr[at, :] - peak) * attn_scale)
        s_scr[at, :] = e
        total = total + jnp.sum(e, axis=0, keepdims=True)
    share = 1.0 / total
    for j in range(SLOTS):
        at = slice(j * BLOCK, (j + 1) * BLOCK)
        p_scr[at, :] = (s_scr[at, :] * share).astype(bf16)
    attended = nn(vt[...], p_scr[...]).T.astype(bf16)
    grad_out[:, :LAT] += nn(p_scr[...], dout[...])
    att_out[...] = attended
    delta = jnp.sum(dout[...].astype(f32) * attended.astype(f32), axis=1, keepdims=True)
    delta = jnp.broadcast_to(delta, (ROWS, 128)).T[:1, :]
    share = share * attn_scale
    for j in range(SLOTS):
        at = slice(j * BLOCK, (j + 1) * BLOCK)
        p_scr[at, :] = (s_scr[at, :] * share * (d_scr[at, :] - delta)).astype(bf16)
    grad_out[...] += nn(p_scr[...], q[...])


def attention(q, dout, hot, keys):
    per_tile = lambda width: pl.BlockSpec((ROWS, width), lambda t: (t, 0))
    whole = lambda *shape: pl.BlockSpec(shape, lambda t: (0, 0))
    flops = 2 * BLOCK * HEADS * WINDOW // 2 * (2 * KV + 3 * LAT)
    return pl.pallas_call(
        attention_kernel,
        grid=(TILES,),
        in_specs=[
            per_tile(KV),
            per_tile(LAT),
            pl.BlockSpec((TILE_Q, ROPE), lambda t: (t, 0)),
            whole(WINDOW, PAD),
        ],
        out_specs=[per_tile(LAT), whole(WINDOW, KV), whole(8, ROWS)],
        scratch_shapes=[
            pltpu.VMEM((LAT, WINDOW), bf16),
            pltpu.VMEM((ROWS, 128), bf16),
            pltpu.VMEM((WINDOW, ROWS), f32),
            pltpu.VMEM((WINDOW, ROWS), f32),
            pltpu.VMEM((WINDOW, ROWS), bf16),
        ],
        out_shape=(
            jax.ShapeDtypeStruct((BLOCK * HEADS, LAT), bf16),
            jax.ShapeDtypeStruct((WINDOW, KV), f32),
            jax.ShapeDtypeStruct((8, ROWS), f32),
        ),
        compiler_params=pltpu.CompilerParams(
            dimension_semantics=("arbitrary",), vmem_limit_bytes=50 * MiB
        ),
        cost_estimate=pl.CostEstimate(
            flops=flops, bytes_accessed=16 << 20, transcendentals=BLOCK * HEADS * WINDOW
        ),
        name="attention",
    )(q, dout, hot, keys)


def grads_kernel(
    kg, proj, gain, cos, sin, tok, peak, rows_out, peak_out,
    near, outbox, far, kvg, peaks, tok_in, tok_t, part, part_in, sums, sums_in,
    ns, nr, fs, fr, gs, gr, ps, pr, ss, sr, ts, tr, as_, ar,
):
    me = Place()
    c, k, f = me.c, me.k, me.f
    sibling = me.at(k=1 - k)
    back = [me.ctx((c - 2 * j + CTX) % CTX) for j in range(1, 8)]
    peers = [me.fsdp((f + s) % FSDP) for s in range(1, FSDP)]

    def slot(distance):
        return SLOTS - 1 - distance

    swaps = []
    for n in range(4):
        copy = send(kg.at[slot(2 * n + 1)], near.at[n], ns.at[n], nr.at[n], sibling)
        copy.start()
        swaps.append(copy)
    tokens = []
    for s in range(1, FSDP):
        columns = pl.ds(pl.multiple_of(((f + s) % FSDP) * SHARD, 128), SHARD)
        copy = send(tok.at[:, columns], tok_in.at[s], as_.at[s - 1], ar.at[s - 1], peers[s - 1])
        copy.start()
        tokens.append(copy)
    gathers = []
    for s in range(1, FSDP):
        copy = send(peak, peaks.at[s], ps.at[s - 1], pr.at[s - 1], peers[s - 1])
        copy.start()
        gathers.append(copy)
    sends = []
    own = kg[slot(0)]
    for copy in swaps:
        copy.wait_recv()

    @pl.when(k == 1)
    def _():
        for n in range(4):
            outbox[n] = near[n] + kg[slot(2 * n + 2)]

    @pl.when(k == 0)
    def _():
        for n in range(3):
            outbox[n] = near[n + 1] + kg[slot(2 * n + 2)]
        outbox[3] = kg[slot(8)]

    own = own + jnp.where(k == 0, near[0], jnp.zeros_like(own))
    for n in range(4):
        copy = send(outbox.at[n], far.at[n], fs.at[n], fr.at[n], back[n])
        copy.start()
        sends.append(copy)
    tok_t[:, :BLOCK] = tok[:, pl.ds(pl.multiple_of(f * SHARD, 128), SHARD)].T
    for s in range(1, FSDP):
        tokens[s - 1].wait_recv()
        tok_t[:, s * BLOCK : (s + 1) * BLOCK] = tok_in[s].T
    for copy in sends:
        copy.wait_recv()
    key_grad = own
    for n in range(4):
        key_grad = key_grad + far[n]

    compressed = proj[:, :LAT]
    inverse = lax.rsqrt(jnp.mean(compressed * compressed, axis=1, keepdims=True) + 1e-06)
    first, second = key_grad[:, LAT : LAT + HALF], key_grad[:, LAT + HALF :]
    d_first = first * cos[...] + second * sin[...]
    d_second = -first * sin[...] + second * cos[...]
    scaled = key_grad[:, :LAT] * gain[...]
    inner = jnp.mean(compressed * scaled, axis=1, keepdims=True)
    d_comp = inverse * (scaled - compressed * (inverse * inverse * inner))
    kvg[0, :, :LAT] = d_comp.astype(bf16)
    kvg[0, :, LAT:] = jnp.concatenate([d_first, d_second], axis=1).astype(bf16)
    spread = []
    for s in range(1, FSDP):
        copy = send(kvg.at[0], kvg.at[s], gs.at[s - 1], gr.at[s - 1], peers[s - 1])
        copy.start()
        spread.append(copy)
    top = peak[...]
    for s in range(1, FSDP):
        gathers[s - 1].wait_recv()
        top = jnp.maximum(top, peaks[s])
    for copy in spread:
        copy.wait_recv()

    everything = kvg[...].reshape(FSDP * BLOCK, KV)

    def multiply(n, core):
        p = 2 * n + core
        rows = pl.ds(pl.multiple_of(p * PIECE, 8), PIECE)
        return nn(tok_t[rows, :], everything)

    whole = nn(tok_t[...], everything)
    for p in range(CTX):
        part[p, :, :KV] = whole[p * PIECE : (p + 1) * PIECE]
        for r in range(8):
            part[p, r : r + 1, KV:] = top[r : r + 1, r * ROPE : (r + 1) * ROPE]
    halves = []
    for n in range(CTX // 2):
        copy = send(part.at[2 * n + 1 - k], part_in.at[n], ss.at[n], sr.at[n], sibling)
        copy.start()
        halves.append(copy)
    totals = []
    me_n = c // 2
    for n in range(CTX // 2):
        halves[n].wait_recv()
        here = part.at[2 * n + k]
        sums[n, :, :KV] = here[:, :KV] + part_in[n, :, :KV]
        sums[n, :8, KV:] = jnp.maximum(here[:8, KV:], part_in[n, :8, KV:])
    for s in range(1, CTX // 2):
        to = (me_n - s + 8) % 8
        copy = send(sums.at[to], sums_in.at[s], ts.at[s], tr.at[s], back[s - 1])
        copy.start()
        totals.append(copy)
    rows = sums[me_n, :, :KV]
    top = sums[me_n, :8, KV:]
    for s in range(1, CTX // 2):
        totals[s - 1].wait_recv()
        rows = rows + sums_in[s, :, :KV]
        top = jnp.maximum(top, sums_in[s, :8, KV:])
    rows_out[...] = rows
    peak_out[...] = top
    for copy in swaps + tokens + gathers + sends + spread + halves + totals:
        copy.wait_send()


GRADS = 25
TRI = [(r, s) for r in range(5) for s in range(r, 5)]
PACKED = 2048
PAIRS = {3: [(0, 0), (0, 1), (1, 0)], 6: [(0, 0), (0, 1), (1, 0), (0, 2), (2, 0), (1, 1)]}


def split(value, count):
    parts = []
    for _ in range(count):
        part = value.astype(bf16)
        parts.append(part)
        value = value - part.astype(f32)
    return parts


def muon_kernel(
    g, out, pack, core_in, yz_in, x_in, acc, gram, rows_in, a_scr, left_scr, thin_scr, right_scr, ms, mr, cs, cr, ys, yr, xs, xr, xs2, xr2, ys2, yr2, cs2, cr2
):
    me = Place()
    k, x, y = me.k, me.x, me.y
    z = me.zh * 2 + me.zl
    sibling = me.at(k=1 - k)

    def plane(n):
        yy, zz = (y + n // 4) % 4, (z + n % 4) % 4
        return me.at(y=yy, zh=zz // 2, zl=zz % 2), yy * 4 + zz

    planes = [plane(n) for n in range(16)]
    line = [me.at(x=(x + s) % 4) for s in range(4)]
    give = me.f * CTX + me.c
    take = me.c * FSDP + me.f
    moving = give != take
    move = send(g, rows_in, ms.at[0], mr.at[0], (give // FSDP, give % FSDP))

    grad = g[...]
    parts = [
        jnp.concatenate([p.astype(f32), jnp.zeros((8, KV), f32)], axis=0).astype(bf16)
        for p in split(grad, 3)
    ]
    left = jnp.concatenate([parts[i] for i, _ in PAIRS[6]], axis=0)
    right = jnp.concatenate([parts[j] for _, j in PAIRS[6]], axis=0)
    local = tn(left, right)
    for i, (r, s) in enumerate(TRI[:14]):
        width = min(128, KV - s * 128)
        pack[i * 128 : i * 128 + 128, :width] = local[r * 128 : r * 128 + 128, s * 128 : s * 128 + width]
    pack[1792:1856, :64] = local[512:, 512:]
    pack[1856:, :] = jnp.zeros((PACKED - 1856, 128), f32)

    half = PACKED // 2
    unit = half // 16
    small = unit // 4

    def rows(start, size):
        return pl.ds(pl.multiple_of(start, 8), size)

    copies = []
    swap = send(pack.at[rows((1 - k) * half, half)], core_in, cs.at[0], cr.at[0], sibling)
    swap.start()

    @pl.when(moving)
    def _():
        move.start()

    @pl.when(jnp.logical_not(moving))
    def _():
        rows_in[...] = grad

    swap.wait_recv()
    acc[...] = pack[rows(k * half, half), :] + core_in[...]
    copies.append(swap)
    mine = y * 4 + z
    first = []
    for n in range(1, 16):
        device, index = planes[n]
        copy = send(acc.at[rows(index * unit, unit)], yz_in.at[n], ys.at[n], yr.at[n], device)
        copy.start()
        first.append(copy)
    total = acc[rows(mine * unit, unit), :]
    for n in range(1, 16):
        first[n - 1].wait_recv()
        total = total + yz_in[n]
    yz_in[0] = total
    second = []
    for s in range(1, 4):
        to = (x + s) % 4
        copy = send(yz_in.at[0, rows(to * small, small)], x_in.at[s], xs.at[s], xr.at[s], line[s])
        copy.start()
        second.append(copy)
    total = yz_in[0, rows(x * small, small), :]
    for s in range(1, 4):
        second[s - 1].wait_recv()
        total = total + x_in[s]
    base = k * half + mine * unit
    gram[rows(base + x * small, small), :] = total
    third = []
    for s in range(1, 4):
        there = gram.at[rows(base + x * small, small)]
        copy = send(there, there, xs2.at[s], xr2.at[s], line[s])
        copy.start()
        third.append(copy)
    for copy in third:
        copy.wait_recv()
    fourth = []
    for n in range(1, 16):
        there = gram.at[rows(base, unit)]
        copy = send(there, there, ys2.at[n], yr2.at[n], planes[n][0])
        copy.start()
        fourth.append(copy)
    for copy in fourth:
        copy.wait_recv()
    there = gram.at[rows(k * half, half)]
    last = send(there, there, cs2.at[0], cr2.at[0], sibling)
    last.start()
    last.wait_recv()
    copies += first + second + third + fourth + [last]

    blocks = {}
    for i, (r, s) in enumerate(TRI):
        if i < 14:
            blocks[r, s] = gram[i * 128 : i * 128 + 128, :]
            if r != s:
                blocks[s, r] = blocks[r, s].T
    edge = gram[1792:1856, :]
    lines = []
    for r in range(4):
        lines.append(jnp.concatenate([blocks[r, s] for s in range(5)], axis=1)[:, :KV])
    bottom = [blocks[4, s][:64] for s in range(4)] + [edge]
    lines.append(jnp.concatenate(bottom, axis=1)[:, :KV])
    full = jnp.concatenate(lines, axis=0)
    row = lax.broadcasted_iota(jnp.int32, (KV, KV), 0)
    col = lax.broadcasted_iota(jnp.int32, (KV, KV), 1)
    diagonal = row == col
    squares = jnp.sum(jnp.where(diagonal, full, 0.0))
    norm = jnp.sqrt(jnp.full((1, 1), squares, f32)) + 1e-07
    inv = 1.0 / norm
    a_scr[...] = full * inv * inv

    @pl.when(moving)
    def _():
        move.wait_recv()

    out[...] = rows_in[...] * inv

    def lay_left(ref, value, terms):
        parts = split(value, 3 if terms == 6 else 2)
        for t, (i, _) in enumerate(PAIRS[terms]):
            ref[:, t * LAT : (t + 1) * LAT] = parts[i][:, :LAT]
            at = terms * LAT + t * ROPE
            ref[:, at : at + ROPE] = parts[i][:, LAT:]

    def lay_right(value, terms):
        parts = split(value, 3 if terms == 6 else 2)
        for t, (_, j) in enumerate(PAIRS[terms]):
            right_scr[t * LAT : (t + 1) * LAT, :] = parts[j][:LAT]
            at = terms * LAT + t * ROPE
            right_scr[at : at + ROPE, :] = parts[j][LAT:]

    def symmetric(terms):
        size = terms * KV
        wide = nn(left_scr[:, :size], right_scr[:size, :LAT])
        corner = nn(left_scr[LAT:, :size], right_scr[:size, LAT:])
        return jnp.concatenate([wide, jnp.concatenate([wide[LAT:].T, corner], axis=0)], axis=1)

    def mix(terms):
        a = a_scr[...]
        lay_left(left_scr, a, terms)
        lay_right(a, terms)
        mixing = quintic_b * a + quintic_c * symmetric(terms)
        lay_right(mixing, terms)
        lay_left(thin_scr, out[...], terms)
        size = terms * KV
        out[...] = quintic_a * out[...] + nn(thin_scr[:, :size], right_scr[:size, :])

    def advance(terms):
        b = quintic_a * a_scr[...] + symmetric(terms)
        lay_left(left_scr, b, terms)
        a_scr[...] = quintic_a * b + symmetric(terms)

    mix(6)
    advance(6)

    def iteration(step, _):
        mix(3)

        @pl.when(step < NS_ITERS - 1)
        def _():
            advance(3)

        return 0

    lax.fori_loop(1, NS_ITERS, iteration, 0)
    iterate = out[...]
    out[...] = iterate * (0.2 * math.sqrt(D))

    @pl.when(moving)
    def _():
        move.wait_send()

    for copy in copies:
        copy.wait_send()


def update_kernel(kg, proj, gain, cos, sin, tok, peak, out, peak_out, rows, *scratch):
    me = Place()
    give, take = me.f * CTX + me.c, me.c * FSDP + me.f
    moving = give != take

    @pl.when(moving)
    def _():
        pl.semaphore_signal(
            pltpu.get_barrier_semaphore(),
            inc=1,
            device_id=(take % CTX, take // CTX),
            device_id_type=MESH,
        )

    c, x, y, z = me.c, me.x, me.y, me.zh * 2 + me.zl
    friends = [me.at(k=1 - me.k)]
    friends += [me.ctx((c - 2 * j + CTX) % CTX) for j in range(1, 8)]
    friends += [me.fsdp((me.f + s) % FSDP) for s in range(1, FSDP)]
    for n in range(1, 16):
        zz = (z + n % 4) % 4
        friends.append(me.at(y=(y + n // 4) % 4, zh=zz // 2, zl=zz % 2))
    friends += [me.at(x=(x + s) % 4) for s in range(1, 4)]
    greet(friends, jnp.where(moving, 1, 0))
    grads_kernel(kg, proj, gain, cos, sin, tok, peak, rows, peak_out, *scratch[:GRADS])
    muon_kernel(rows, out, *scratch[GRADS:])


def weight_update(kg, proj, gain, cos, sin, tok, peak):
    half = PACKED // 2
    dma = lambda sizes: [pltpu.SemaphoreType.DMA((n,)) for n in sizes]
    grads = [
        pltpu.VMEM((4, BLOCK, KV), f32),
        pltpu.VMEM((4, BLOCK, KV), f32),
        pltpu.VMEM((4, BLOCK, KV), f32),
        pltpu.VMEM((FSDP, BLOCK, KV), bf16),
        pltpu.VMEM((FSDP, 8, ROWS), f32),
        pltpu.VMEM((FSDP, BLOCK, SHARD), bf16),
        pltpu.VMEM((SHARD, FSDP * BLOCK), bf16),
        pltpu.VMEM((CTX, PIECE, PAD), f32),
        pltpu.VMEM((CTX // 2, PIECE, PAD), f32),
        pltpu.VMEM((CTX // 2, PIECE, PAD), f32),
        pltpu.VMEM((CTX // 2, PIECE, PAD), f32),
    ] + dma([4, 4, 4, 4, 7, 7, 7, 7, 8, 8, 8, 8, 7, 7])
    assert len(grads) == GRADS
    newton = [
        pltpu.VMEM((PACKED, 128), f32),
        pltpu.VMEM((half, 128), f32),
        pltpu.VMEM((16, half // 16, 128), f32),
        pltpu.VMEM((4, half // 64, 128), f32),
        pltpu.VMEM((half, 128), f32),
        pltpu.VMEM((PACKED, 128), f32),
        pltpu.VMEM((PIECE, KV), f32),
        pltpu.VMEM((KV, KV), f32),
        pltpu.VMEM((KV, 6 * KV), bf16),
        pltpu.VMEM((PIECE, 6 * KV), bf16),
        pltpu.VMEM((6 * KV, KV), bf16),
    ] + dma([1, 1, 1, 1, 16, 16, 4, 4, 4, 4, 16, 16, 1, 1])
    return pl.pallas_call(
        update_kernel,
        out_shape=(
            jax.ShapeDtypeStruct((PIECE, KV), f32),
            jax.ShapeDtypeStruct((8, ROPE), f32),
        ),
        in_specs=[VMEM] * 7,
        out_specs=(VMEM, VMEM),
        scratch_shapes=[pltpu.VMEM((PIECE, KV), f32)] + grads + newton,
        compiler_params=pltpu.CompilerParams(
            collective_id=1, has_side_effects=True, vmem_limit_bytes=48 * MiB
        ),
        name="weight_grad",
    )(kg, proj, gain, cos, sin, tok, peak)


def per_device(tokens, kv_weight, latent_gain, queries, out_grad, segment_ids):
    tok = tokens[0]
    c = lax.axis_index("ctx")
    positions = c * BLOCK + jnp.arange(BLOCK, dtype=jnp.int32)
    cos, sin = rope_tables(positions)
    gain = latent_gain[None]
    docs = segment_ids[0]
    lanes = jnp.arange(ROPE, dtype=jnp.int32)
    hot = (docs[:, None] == lanes[None]).astype(f32)
    qt = jnp.transpose(queries[0], (1, 2, 0))
    keys, proj, q = make_keys(tok, kv_weight.T, gain, hot, cos, sin, qt)
    keys = keys.reshape(WINDOW, PAD)
    dout = out_grad[0].reshape(BLOCK * HEADS, LAT)
    attended, kg, peak = attention(q, dout, hot, keys)
    update, top = weight_update(
        kg.reshape(SLOTS, BLOCK, KV), proj, gain, cos, sin, tok, peak
    )
    return (attended.reshape(1, BLOCK, HEADS, LAT), jnp.max(top.reshape(TILE_Q, HEADS), axis=0), update)


def solution(mesh):
    return jax.shard_map(
        per_device,
        mesh=mesh,
        in_specs=(
            P("fsdp", "ctx", None),
            P("fsdp", None),
            P(),
            P("fsdp", "ctx", None, None),
            P("fsdp", "ctx", None, None),
            P("fsdp", "ctx"),
        ),
        out_specs=(P("fsdp", "ctx", None, None), P(), P(("ctx", "fsdp"), None)),
        check_vma=False,
    )
```

```python
import functools
import math

import jax
import jax.numpy as jnp
from jax import lax
from jax.experimental import pallas as pl
from jax.experimental.pallas import tpu as pltpu
from jax.sharding import PartitionSpec as P

D = 7168
LAT = 512
ROPE = 64
HEADS = 32
NS_ITERS = 5
KV = LAT + ROPE
PAD = 640
HALF = ROPE // 2
BLOCK = 128
REACH = 8
SLOTS = REACH + 1
WINDOW = SLOTS * BLOCK
CTX = 16
FSDP = 8
SHARD = D // FSDP
PIECE = SHARD // CTX
TILE_Q = 16
ROWS = TILE_Q * HEADS
TILES = BLOCK // TILE_Q

attn_scale = 192.0 ** (-0.5)
rope_base = 50000.0
quintic_a = 3.4445
quintic_b = -4.775
quintic_c = 2.0315
BIG = -1e30
MiB = 1 << 20

MESH = pl.DeviceIdType.MESH
VMEM = pl.BlockSpec(memory_space=pltpu.VMEM)
HBM = pl.BlockSpec(memory_space=pltpu.HBM)
f32, bf16 = jnp.float32, jnp.bfloat16


def rope_tables(positions):
    ladder = jnp.arange(HALF, dtype=f32)
    freqs = jnp.power(rope_base, -2.0 * ladder / ROPE)
    angles = positions.astype(f32)[:, None] * freqs[None, :]
    return (jnp.cos(angles), jnp.sin(angles))


def nn(a, b, **kw):
    return lax.dot_general(a, b, (((1,), (0,)), ((), ())), preferred_element_type=f32, **kw)


def nt(a, b, **kw):
    return lax.dot_general(a, b, (((1,), (1,)), ((), ())), preferred_element_type=f32, **kw)


def tn(a, b, **kw):
    return lax.dot_general(a, b, (((0,), (0,)), ((), ())), preferred_element_type=f32, **kw)


class Place:
    def __init__(self):
        self.c, self.f = lax.axis_index("ctx"), lax.axis_index("fsdp")
        self.y, self.zh, self.k = self.c // 4, (self.c // 2) % 2, self.c % 2
        self.x, self.zl = self.f // 2, self.f % 2

    def at(self, x=None, y=None, zh=None, zl=None, k=None):
        x = self.x if x is None else x
        y = self.y if y is None else y
        zh = self.zh if zh is None else zh
        zl = self.zl if zl is None else zl
        k = self.k if k is None else k
        return ((y * 2 + zh) * 2 + k, x * 2 + zl)

    def ctx(self, c):
        return (c, self.f)

    def fsdp(self, f):
        return (self.c, f)


def greet(devices, others=0):
    barrier = pltpu.get_barrier_semaphore()
    for device in devices:
        pl.semaphore_signal(barrier, inc=1, device_id=device, device_id_type=MESH)
    pl.semaphore_wait(barrier, len(devices) + others)


def send(src, dst, send_sem, recv_sem, device):
    return pltpu.make_async_remote_copy(
        src_ref=src,
        dst_ref=dst,
        send_sem=send_sem,
        recv_sem=recv_sem,
        device_id=device,
        device_id_type=MESH,
    )


def keys_kernel(
    tok_hbm, w, gain, hot, cos, sin, qt, keys_out, proj_out, q_out, wall, win, tok, qin, qrow, qs, ws, wr, ks, kr
):
    me = Place()
    c, k, x = me.c, me.k, me.x
    sibling = me.at(k=1 - k)
    z_same, z_other = me.at(zl=1 - me.zl), me.at(zl=1 - me.zl, zh=1 - me.zh)
    x_up, x_down = me.at(x=(x + 1) % 4), me.at(x=(x + 3) % 4)
    later = [me.ctx((c + 2 * j) % CTX) for j in range(1, 5)]
    earlier = [me.ctx((c - 2 * j + CTX) % CTX) for j in range(1, 5)]
    greet([sibling, z_same, z_other, x_up, x_down] + later + earlier[:3])

    half = KV // 2
    quarter = half // 2
    counter = [0]

    def rows(core, q=None):
        if q is None:
            return pl.ds(pl.multiple_of(core * half, 16), half)
        return pl.ds(pl.multiple_of(core * half + q * quarter, 16), quarter)

    def post(src_f, src, core, q, device):
        i = counter[0]
        counter[0] += 1
        where = rows(core, q)
        source = w.at[where] if src is None else src.at[src_f, where]
        copy = send(source, wall.at[src_f, where], ws.at[i], wr.at[i], device)
        copy.start()
        return copy

    def shard_of(xx, zl):
        return (xx % 4) * 2 + zl

    own = me.f
    up = [post(own, None, k, 0, x_up), post(own, None, k, 1, x_up)]
    down = [post(own, None, k, 1, x_down), post(own, None, k, 0, x_down)]
    own_z = [post(own, None, k, 0, z_same), post(own, None, k, 1, z_other)]
    fetch = pltpu.make_async_copy(qt, qin, qs.at[0])
    fetch.start()
    fetch_w = pltpu.make_async_copy(w, wall.at[own], qs.at[1])
    fetch_w.start()
    fetch_tok = pltpu.make_async_copy(tok_hbm, tok, qs.at[2])
    fetch_tok.start()
    posted = up + down + own_z

    def forward(copy, shard, q):
        copy.wait_recv()
        z = post(shard, wall, k, q, (z_same, z_other)[q])
        s = post(shard, wall, k, q, sibling)
        posted.extend([z, s])
        return z, s

    def pass_on(copy, shard, q):
        copy.wait_recv()
        s = post(shard, wall, k, q, sibling)
        posted.append(s)
        return s

    other = 1 - me.zl
    f_prev, f_next, f_far = shard_of(x + 3, me.zl), shard_of(x + 1, me.zl), shard_of(x + 2, me.zl)
    o_own, o_prev, o_next, o_far = (shard_of(x + i, other) for i in (0, 3, 1, 2))

    def add(total, shard):
        return total + nt(
            tok[:, pl.ds(pl.multiple_of(shard * SHARD, 128), SHARD)], wall[shard]
        )

    fetch.wait()

    def turn(h, _):
        for lanes in range(PAD // 128):
            width = min(128, KV - lanes * 128)
            block = qin[h, lanes * 128 : lanes * 128 + width, :].astype(f32)
            if width < 128:
                block = jnp.concatenate([block, jnp.zeros((128 - width, BLOCK), f32)], axis=0)
            qrow[lanes, pl.ds(h, BLOCK, stride=HEADS), :] = block.T
        return 0

    lax.fori_loop(0, 10, turn, 0)

    prev0 = forward(up[0], f_prev, 0)
    relay_up = post(f_prev, wall, k, 0, x_up)
    next1 = forward(down[0], f_next, 1)
    relay_down = post(f_next, wall, k, 1, x_down)
    posted.extend([relay_up, relay_down])
    s_own = [pass_on(own_z[q], o_own, q) for q in range(2)]
    lax.fori_loop(10, 22, turn, 0)
    prev1 = forward(up[1], f_prev, 1)
    next0 = forward(down[1], f_next, 0)
    lax.fori_loop(22, HEADS, turn, 0)
    far0 = forward(relay_up, f_far, 0)
    far1 = forward(relay_down, f_far, 1)
    s_prev0 = pass_on(prev0[0], o_prev, 0)
    s_next1 = pass_on(next1[0], o_next, 1)
    fetch_w.wait()
    fetch_tok.wait()
    acc = nt(tok[:, pl.ds(pl.multiple_of(own * SHARD, 128), SHARD)], wall[own])

    def narrow(i, _):
        rows = pl.ds(pl.multiple_of(i * ROWS, ROWS), ROWS)
        for lanes in range(PAD // 128):
            width = min(128, KV - lanes * 128)
            q_out[rows, lanes * 128 : lanes * 128 + width] = qrow[lanes, rows, :width].astype(bf16)
        return 0

    lax.fori_loop(0, TILES, narrow, 0)
    for copy in s_own:
        copy.wait_recv()
    acc = add(acc, o_own)
    prev0[1].wait_recv()
    prev1[1].wait_recv()
    acc = add(acc, f_prev)
    next0[1].wait_recv()
    next1[1].wait_recv()
    acc = add(acc, f_next)
    s_prev1 = pass_on(prev1[0], o_prev, 1)
    s_next0 = pass_on(next0[0], o_next, 0)
    far0[1].wait_recv()
    far1[1].wait_recv()
    acc = add(acc, f_far)
    s_far0 = pass_on(far0[0], o_far, 0)
    s_far1 = pass_on(far1[0], o_far, 1)
    for shard, pair in ((o_prev, (s_prev0, s_prev1)), (o_next, (s_next0, s_next1)), (o_far, (s_far0, s_far1))):
        for copy in pair:
            copy.wait_recv()
        acc = add(acc, shard)

    compressed = acc[:, :LAT]
    inverse = lax.rsqrt(jnp.mean(compressed * compressed, axis=1, keepdims=True) + 1e-06)
    latent = compressed * inverse * gain[...]
    first, second = acc[:, LAT : LAT + HALF], acc[:, LAT + HALF :]
    mine = win.at[SLOTS - 1]
    mine[:, :LAT] = latent.astype(bf16)
    tail = jnp.concatenate(
        [
            first * cos[...] - second * sin[...],
            second * cos[...] + first * sin[...],
            hot[...],
        ],
        axis=1,
    )
    mine[:, LAT:] = tail.astype(bf16)
    proj_out[...] = acc

    def slot(distance):
        return SLOTS - 1 - distance

    spread = []
    for j in range(1, 5):
        copy = send(mine, win.at[slot(2 * j)], ks.at[j - 1], kr.at[j - 1], later[j - 1])
        copy.start()
        spread.append(copy)
    to_sibling = []

    def give(n):
        copy = send(
            win.at[slot(2 * n + 2 * k)], win.at[slot(2 * n + 1)], ks.at[4 + n], kr.at[4 + n], sibling
        )
        copy.start()
        to_sibling.append(copy)

    spread[0].wait_recv()
    give(0)
    give_next = 1
    for j in range(1, 4):
        spread[j].wait_recv()
        give(give_next)
        give_next += 1
    for copy in to_sibling:
        copy.wait_recv()
    lane = lax.broadcasted_iota(jnp.int32, (BLOCK, 128), 1)
    flag = jnp.where(lane == ROPE + 8, 1.0, 0.0)
    for d in range(REACH + 1):
        keys_out[slot(d)] = win[slot(d)]
        if d > 0:

            @pl.when(c < d)
            def _(d=d):
                keys_out[slot(d), :, LAT:] = flag.astype(bf16)

    for copy in posted + spread + to_sibling:
        copy.wait_send()


N_W = 6 + 2 + 6 * 2 + 8


def make_keys(tok, w, gain, hot, cos, sin, qt):
    return pl.pallas_call(
        keys_kernel,
        out_shape=(
            jax.ShapeDtypeStruct((SLOTS, BLOCK, PAD), bf16),
            jax.ShapeDtypeStruct((BLOCK, KV), f32),
            jax.ShapeDtypeStruct((BLOCK * HEADS, KV), bf16),
        ),
        in_specs=[HBM, HBM] + [VMEM] * 4 + [HBM],
        out_specs=(VMEM,) * 3,
        scratch_shapes=[
            pltpu.VMEM((FSDP, KV, SHARD), bf16),
            pltpu.VMEM((SLOTS, BLOCK, PAD), bf16),
            pltpu.VMEM((BLOCK, D), bf16),
            pltpu.VMEM((HEADS, KV, BLOCK), bf16),
            pltpu.VMEM((PAD // 128, BLOCK * HEADS, 128), f32),
            pltpu.SemaphoreType.DMA((3,)),
            pltpu.SemaphoreType.DMA((N_W,)),
            pltpu.SemaphoreType.DMA((N_W,)),
            pltpu.SemaphoreType.DMA((8,)),
            pltpu.SemaphoreType.DMA((8,)),
        ],
        compiler_params=pltpu.CompilerParams(
            collective_id=0, has_side_effects=True, vmem_limit_bytes=58 * MiB
        ),
        name="keys",
    )(tok, w, gain, hot, cos, sin, qt)


def attention_kernel(
    q, dout, hot, keys, att_out, grad_out, peak_out, vt, qr, s_scr, d_scr, p_scr
):
    t = pl.program_id(0)

    @pl.when(t == 0)
    def _():
        grad_out[...] = jnp.zeros_like(grad_out)
        peak_out[...] = jnp.full_like(peak_out, BIG)
        for j in range(SLOTS):
            vt[:, j * BLOCK : (j + 1) * BLOCK] = keys[j * BLOCK : (j + 1) * BLOCK, :LAT].T

    qr[:, :ROPE] = q[:, LAT:]
    lane = lax.broadcasted_iota(jnp.int32, (TILE_Q, ROPE), 1)
    qmask = jnp.where((lane < 9) & (hot[...] == 0.0), BIG, 0.0)
    spread = jnp.broadcast_to(qmask[:, None, :], (TILE_Q, HEADS, ROPE))
    qr[:, ROPE:] = spread.reshape(ROWS, ROPE).astype(bf16)

    own = slice(WINDOW - BLOCK, WINDOW)
    s_scr[...] = nt(keys[:, :LAT], q[:, :LAT]) + nt(keys[:, LAT:], qr[...])
    d_scr[...] = nt(keys[:, :LAT], dout[...])
    key = lax.broadcasted_iota(jnp.int32, (BLOCK, ROWS), 0)
    query = t * TILE_Q + lax.broadcasted_iota(jnp.int32, (BLOCK, ROWS), 1) // HEADS
    s_scr[own, :] = jnp.where(key <= query, s_scr[own, :], BIG)
    peak = jnp.max(s_scr[...], axis=0, keepdims=True)
    peak_out[...] = jnp.maximum(peak_out[...], peak * attn_scale)
    total = jnp.zeros((1, ROWS), f32)
    for j in range(SLOTS):
        at = slice(j * BLOCK, (j + 1) * BLOCK)
        e = jnp.exp((s_scr[at, :] - peak) * attn_scale)
        s_scr[at, :] = e
        total = total + jnp.sum(e, axis=0, keepdims=True)
    share = 1.0 / total
    for j in range(SLOTS):
        at = slice(j * BLOCK, (j + 1) * BLOCK)
        p_scr[at, :] = (s_scr[at, :] * share).astype(bf16)
    attended = nn(vt[...], p_scr[...]).T.astype(bf16)
    grad_out[:, :LAT] += nn(p_scr[...], dout[...])
    att_out[...] = attended
    delta = jnp.sum(dout[...].astype(f32) * attended.astype(f32), axis=1, keepdims=True)
    delta = jnp.broadcast_to(delta, (ROWS, 128)).T[:1, :]
    share = share * attn_scale
    for j in range(SLOTS):
        at = slice(j * BLOCK, (j + 1) * BLOCK)
        p_scr[at, :] = (s_scr[at, :] * share * (d_scr[at, :] - delta)).astype(bf16)
    grad_out[...] += nn(p_scr[...], q[...])


def attention(q, dout, hot, keys):
    per_tile = lambda width: pl.BlockSpec((ROWS, width), lambda t: (t, 0))
    whole = lambda *shape: pl.BlockSpec(shape, lambda t: (0, 0))
    flops = 2 * BLOCK * HEADS * WINDOW // 2 * (2 * KV + 3 * LAT)
    return pl.pallas_call(
        attention_kernel,
        grid=(TILES,),
        in_specs=[
            per_tile(KV),
            per_tile(LAT),
            pl.BlockSpec((TILE_Q, ROPE), lambda t: (t, 0)),
            whole(WINDOW, PAD),
        ],
        out_specs=[per_tile(LAT), whole(WINDOW, KV), whole(8, ROWS)],
        scratch_shapes=[
            pltpu.VMEM((LAT, WINDOW), bf16),
            pltpu.VMEM((ROWS, 128), bf16),
            pltpu.VMEM((WINDOW, ROWS), f32),
            pltpu.VMEM((WINDOW, ROWS), f32),
            pltpu.VMEM((WINDOW, ROWS), bf16),
        ],
        out_shape=(
            jax.ShapeDtypeStruct((BLOCK * HEADS, LAT), bf16),
            jax.ShapeDtypeStruct((WINDOW, KV), f32),
            jax.ShapeDtypeStruct((8, ROWS), f32),
        ),
        compiler_params=pltpu.CompilerParams(
            dimension_semantics=("arbitrary",), vmem_limit_bytes=50 * MiB
        ),
        cost_estimate=pl.CostEstimate(
            flops=flops, bytes_accessed=16 << 20, transcendentals=BLOCK * HEADS * WINDOW
        ),
        name="attention",
    )(q, dout, hot, keys)


def grads_kernel(
    kg, proj, gain, cos, sin, tok, peak, rows_out, peak_out,
    near, outbox, far, kvg, peaks, tok_in, tok_t, part, part_in, sums, sums_in,
    ns, nr, fs, fr, gs, gr, ps, pr, ss, sr, ts, tr, as_, ar,
):
    me = Place()
    c, k, f = me.c, me.k, me.f
    sibling = me.at(k=1 - k)
    back = [me.ctx((c - 2 * j + CTX) % CTX) for j in range(1, 8)]
    peers = [me.fsdp((f + s) % FSDP) for s in range(1, FSDP)]

    def slot(distance):
        return SLOTS - 1 - distance

    swaps = []
    for n in range(4):
        copy = send(kg.at[slot(2 * n + 1)], near.at[n], ns.at[n], nr.at[n], sibling)
        copy.start()
        swaps.append(copy)
    gathers = []
    for s in range(1, FSDP):
        copy = send(peak, peaks.at[s], ps.at[s - 1], pr.at[s - 1], peers[s - 1])
        copy.start()
        gathers.append(copy)
    sends = []
    own = kg[slot(0)]
    for copy in swaps:
        copy.wait_recv()

    @pl.when(k == 1)
    def _():
        for n in range(4):
            outbox[n] = near[n] + kg[slot(2 * n + 2)]

    @pl.when(k == 0)
    def _():
        for n in range(3):
            outbox[n] = near[n + 1] + kg[slot(2 * n + 2)]
        outbox[3] = kg[slot(8)]

    own = own + jnp.where(k == 0, near[0], jnp.zeros_like(own))
    for n in range(4):
        copy = send(outbox.at[n], far.at[n], fs.at[n], fr.at[n], back[n])
        copy.start()
        sends.append(copy)
    tokens = []
    for s in range(1, FSDP):
        columns = pl.ds(pl.multiple_of(((f + s) % FSDP) * SHARD, 128), SHARD)
        copy = send(tok.at[:, columns], tok_in.at[s], as_.at[s - 1], ar.at[s - 1], peers[s - 1])
        copy.start()
        tokens.append(copy)
    for copy in sends:
        copy.wait_recv()
    key_grad = own
    for n in range(4):
        key_grad = key_grad + far[n]

    compressed = proj[:, :LAT]
    inverse = lax.rsqrt(jnp.mean(compressed * compressed, axis=1, keepdims=True) + 1e-06)
    first, second = key_grad[:, LAT : LAT + HALF], key_grad[:, LAT + HALF :]
    d_first = first * cos[...] + second * sin[...]
    d_second = -first * sin[...] + second * cos[...]
    scaled = key_grad[:, :LAT] * gain[...]
    inner = jnp.mean(compressed * scaled, axis=1, keepdims=True)
    d_comp = inverse * (scaled - compressed * (inverse * inverse * inner))
    kvg[0, :, :LAT] = d_comp.astype(bf16)
    kvg[0, :, LAT:] = jnp.concatenate([d_first, d_second], axis=1).astype(bf16)
    spread = []
    for s in range(1, FSDP):
        copy = send(kvg.at[0], kvg.at[s], gs.at[s - 1], gr.at[s - 1], peers[s - 1])
        copy.start()
        spread.append(copy)
    tok_t[:, :BLOCK] = tok[:, pl.ds(pl.multiple_of(f * SHARD, 128), SHARD)].T
    for s in range(1, FSDP):
        tokens[s - 1].wait_recv()
        tok_t[:, s * BLOCK : (s + 1) * BLOCK] = tok_in[s].T
    top = peak[...]
    for s in range(1, FSDP):
        gathers[s - 1].wait_recv()
        top = jnp.maximum(top, peaks[s])
    for copy in spread:
        copy.wait_recv()

    everything = kvg[...].reshape(FSDP * BLOCK, KV)

    def multiply(n, core):
        p = 2 * n + core
        rows = pl.ds(pl.multiple_of(p * PIECE, 8), PIECE)
        return nn(tok_t[rows, :], everything)

    whole = nn(tok_t[...], everything)
    for p in range(CTX):
        part[p, :, :KV] = whole[p * PIECE : (p + 1) * PIECE]
        for r in range(8):
            part[p, r : r + 1, KV:] = top[r : r + 1, r * ROPE : (r + 1) * ROPE]
    halves = []
    for n in range(CTX // 2):
        copy = send(part.at[2 * n + 1 - k], part_in.at[n], ss.at[n], sr.at[n], sibling)
        copy.start()
        halves.append(copy)
    totals = []
    me_n = c // 2
    for n in range(CTX // 2):
        halves[n].wait_recv()
        here = part.at[2 * n + k]
        sums[n, :, :KV] = here[:, :KV] + part_in[n, :, :KV]
        sums[n, :8, KV:] = jnp.maximum(here[:8, KV:], part_in[n, :8, KV:])
    for s in range(1, CTX // 2):
        to = (me_n - s + 8) % 8
        copy = send(sums.at[to], sums_in.at[s], ts.at[s], tr.at[s], back[s - 1])
        copy.start()
        totals.append(copy)
    rows = sums[me_n, :, :KV]
    top = sums[me_n, :8, KV:]
    for s in range(1, CTX // 2):
        totals[s - 1].wait_recv()
        rows = rows + sums_in[s, :, :KV]
        top = jnp.maximum(top, sums_in[s, :8, KV:])
    rows_out[...] = rows
    peak_out[...] = top
    for copy in swaps + tokens + gathers + sends + spread + halves + totals:
        copy.wait_send()


GRADS = 25
TRI = [(r, s) for r in range(5) for s in range(r, 5)]
PACKED = 2048
PAIRS = {3: [(0, 0), (0, 1), (1, 0)], 6: [(0, 0), (0, 1), (1, 0), (0, 2), (2, 0), (1, 1)]}


def split(value, count):
    parts = []
    for _ in range(count):
        part = value.astype(bf16)
        parts.append(part)
        value = value - part.astype(f32)
    return parts


def muon_kernel(
    g, out, pack, core_in, yz_in, x_in, acc, gram, rows_in, a_scr, left_scr, thin_scr, right_scr, ms, mr, cs, cr, ys, yr, xs, xr, xs2, xr2, ys2, yr2, cs2, cr2
):
    me = Place()
    k, x, y = me.k, me.x, me.y
    z = me.zh * 2 + me.zl
    sibling = me.at(k=1 - k)

    def plane(n):
        yy, zz = (y + n // 4) % 4, (z + n % 4) % 4
        return me.at(y=yy, zh=zz // 2, zl=zz % 2), yy * 4 + zz

    planes = [plane(n) for n in range(16)]
    line = [me.at(x=(x + s) % 4) for s in range(4)]
    give = me.f * CTX + me.c
    take = me.c * FSDP + me.f
    moving = give != take
    move = send(g, rows_in, ms.at[0], mr.at[0], (give // FSDP, give % FSDP))

    grad = g[...]
    parts = [
        jnp.concatenate([p.astype(f32), jnp.zeros((8, KV), f32)], axis=0).astype(bf16)
        for p in split(grad, 3)
    ]
    left = jnp.concatenate([parts[i] for i, _ in PAIRS[6]], axis=0)
    right = jnp.concatenate([parts[j] for _, j in PAIRS[6]], axis=0)
    local = tn(left, right)
    for i, (r, s) in enumerate(TRI[:14]):
        width = min(128, KV - s * 128)
        pack[i * 128 : i * 128 + 128, :width] = local[r * 128 : r * 128 + 128, s * 128 : s * 128 + width]
    pack[1792:1856, :64] = local[512:, 512:]
    pack[1856:, :] = jnp.zeros((PACKED - 1856, 128), f32)

    half = PACKED // 2
    unit = half // 16
    small = unit // 4

    def rows(start, size):
        return pl.ds(pl.multiple_of(start, 8), size)

    copies = []
    swap = send(pack.at[rows((1 - k) * half, half)], core_in, cs.at[0], cr.at[0], sibling)
    swap.start()

    @pl.when(moving)
    def _():
        move.start()

    @pl.when(jnp.logical_not(moving))
    def _():
        rows_in[...] = grad

    swap.wait_recv()
    acc[...] = pack[rows(k * half, half), :] + core_in[...]
    copies.append(swap)
    mine = y * 4 + z
    first = []
    for n in range(1, 16):
        device, index = planes[n]
        copy = send(acc.at[rows(index * unit, unit)], yz_in.at[n], ys.at[n], yr.at[n], device)
        copy.start()
        first.append(copy)
    total = acc[rows(mine * unit, unit), :]
    for n in range(1, 16):
        first[n - 1].wait_recv()
        total = total + yz_in[n]
    yz_in[0] = total
    second = []
    for s in range(1, 4):
        to = (x + s) % 4
        copy = send(yz_in.at[0, rows(to * small, small)], x_in.at[s], xs.at[s], xr.at[s], line[s])
        copy.start()
        second.append(copy)
    total = yz_in[0, rows(x * small, small), :]
    for s in range(1, 4):
        second[s - 1].wait_recv()
        total = total + x_in[s]
    base = k * half + mine * unit
    gram[rows(base + x * small, small), :] = total
    third = []
    for s in range(1, 4):
        there = gram.at[rows(base + x * small, small)]
        copy = send(there, there, xs2.at[s], xr2.at[s], line[s])
        copy.start()
        third.append(copy)
    for copy in third:
        copy.wait_recv()
    fourth = []
    for n in range(1, 16):
        there = gram.at[rows(base, unit)]
        copy = send(there, there, ys2.at[n], yr2.at[n], planes[n][0])
        copy.start()
        fourth.append(copy)
    for copy in fourth:
        copy.wait_recv()
    there = gram.at[rows(k * half, half)]
    last = send(there, there, cs2.at[0], cr2.at[0], sibling)
    last.start()
    last.wait_recv()
    copies += first + second + third + fourth + [last]

    blocks = {}
    for i, (r, s) in enumerate(TRI):
        if i < 14:
            blocks[r, s] = gram[i * 128 : i * 128 + 128, :]
            if r != s:
                blocks[s, r] = blocks[r, s].T
    edge = gram[1792:1856, :]
    lines = []
    for r in range(4):
        lines.append(jnp.concatenate([blocks[r, s] for s in range(5)], axis=1)[:, :KV])
    bottom = [blocks[4, s][:64] for s in range(4)] + [edge]
    lines.append(jnp.concatenate(bottom, axis=1)[:, :KV])
    full = jnp.concatenate(lines, axis=0)
    row = lax.broadcasted_iota(jnp.int32, (KV, KV), 0)
    col = lax.broadcasted_iota(jnp.int32, (KV, KV), 1)
    diagonal = row == col
    squares = jnp.sum(jnp.where(diagonal, full, 0.0))
    norm = jnp.sqrt(jnp.full((1, 1), squares, f32)) + 1e-07
    inv = 1.0 / norm
    a_scr[...] = full * inv * inv

    @pl.when(moving)
    def _():
        move.wait_recv()

    out[...] = rows_in[...] * inv

    def lay_left(ref, value, terms):
        parts = split(value, 3 if terms == 6 else 2)
        for t, (i, _) in enumerate(PAIRS[terms]):
            ref[:, t * LAT : (t + 1) * LAT] = parts[i][:, :LAT]
            at = terms * LAT + t * ROPE
            ref[:, at : at + ROPE] = parts[i][:, LAT:]

    def lay_right(value, terms):
        parts = split(value, 3 if terms == 6 else 2)
        for t, (_, j) in enumerate(PAIRS[terms]):
            right_scr[t * LAT : (t + 1) * LAT, :] = parts[j][:LAT]
            at = terms * LAT + t * ROPE
            right_scr[at : at + ROPE, :] = parts[j][LAT:]

    def symmetric(terms):
        size = terms * KV
        wide = nn(left_scr[:, :size], right_scr[:size, :LAT])
        corner = nn(left_scr[LAT:, :size], right_scr[:size, LAT:])
        return jnp.concatenate([wide, jnp.concatenate([wide[LAT:].T, corner], axis=0)], axis=1)

    def mix(terms):
        a = a_scr[...]
        lay_left(left_scr, a, terms)
        lay_right(a, terms)
        mixing = quintic_b * a + quintic_c * symmetric(terms)
        lay_right(mixing, terms)
        lay_left(thin_scr, out[...], terms)
        size = terms * KV
        out[...] = quintic_a * out[...] + nn(thin_scr[:, :size], right_scr[:size, :])

    def advance(terms):
        b = quintic_a * a_scr[...] + symmetric(terms)
        lay_left(left_scr, b, terms)
        a_scr[...] = quintic_a * b + symmetric(terms)

    mix(6)
    advance(6)

    def iteration(step, _):
        mix(3)

        @pl.when(step < NS_ITERS - 1)
        def _():
            advance(3)

        return 0

    lax.fori_loop(1, NS_ITERS, iteration, 0)
    iterate = out[...]
    out[...] = iterate * (0.2 * math.sqrt(D))

    @pl.when(moving)
    def _():
        move.wait_send()

    for copy in copies:
        copy.wait_send()


def update_kernel(kg, proj, gain, cos, sin, tok, peak, out, peak_out, rows, *scratch):
    me = Place()
    give, take = me.f * CTX + me.c, me.c * FSDP + me.f
    moving = give != take

    @pl.when(moving)
    def _():
        pl.semaphore_signal(
            pltpu.get_barrier_semaphore(),
            inc=1,
            device_id=(take % CTX, take // CTX),
            device_id_type=MESH,
        )

    c, x, y, z = me.c, me.x, me.y, me.zh * 2 + me.zl
    friends = [me.at(k=1 - me.k)]
    friends += [me.ctx((c - 2 * j + CTX) % CTX) for j in range(1, 8)]
    friends += [me.fsdp((me.f + s) % FSDP) for s in range(1, FSDP)]
    for n in range(1, 16):
        zz = (z + n % 4) % 4
        friends.append(me.at(y=(y + n // 4) % 4, zh=zz // 2, zl=zz % 2))
    friends += [me.at(x=(x + s) % 4) for s in range(1, 4)]
    greet(friends, jnp.where(moving, 1, 0))
    grads_kernel(kg, proj, gain, cos, sin, tok, peak, rows, peak_out, *scratch[:GRADS])
    muon_kernel(rows, out, *scratch[GRADS:])


def weight_update(kg, proj, gain, cos, sin, tok, peak):
    half = PACKED // 2
    dma = lambda sizes: [pltpu.SemaphoreType.DMA((n,)) for n in sizes]
    grads = [
        pltpu.VMEM((4, BLOCK, KV), f32),
        pltpu.VMEM((4, BLOCK, KV), f32),
        pltpu.VMEM((4, BLOCK, KV), f32),
        pltpu.VMEM((FSDP, BLOCK, KV), bf16),
        pltpu.VMEM((FSDP, 8, ROWS), f32),
        pltpu.VMEM((FSDP, BLOCK, SHARD), bf16),
        pltpu.VMEM((SHARD, FSDP * BLOCK), bf16),
        pltpu.VMEM((CTX, PIECE, PAD), f32),
        pltpu.VMEM((CTX // 2, PIECE, PAD), f32),
        pltpu.VMEM((CTX // 2, PIECE, PAD), f32),
        pltpu.VMEM((CTX // 2, PIECE, PAD), f32),
    ] + dma([4, 4, 4, 4, 7, 7, 7, 7, 8, 8, 8, 8, 7, 7])
    assert len(grads) == GRADS
    newton = [
        pltpu.VMEM((PACKED, 128), f32),
        pltpu.VMEM((half, 128), f32),
        pltpu.VMEM((16, half // 16, 128), f32),
        pltpu.VMEM((4, half // 64, 128), f32),
        pltpu.VMEM((half, 128), f32),
        pltpu.VMEM((PACKED, 128), f32),
        pltpu.VMEM((PIECE, KV), f32),
        pltpu.VMEM((KV, KV), f32),
        pltpu.VMEM((KV, 6 * KV), bf16),
        pltpu.VMEM((PIECE, 6 * KV), bf16),
        pltpu.VMEM((6 * KV, KV), bf16),
    ] + dma([1, 1, 1, 1, 16, 16, 4, 4, 4, 4, 16, 16, 1, 1])
    return pl.pallas_call(
        update_kernel,
        out_shape=(
            jax.ShapeDtypeStruct((PIECE, KV), f32),
            jax.ShapeDtypeStruct((8, ROPE), f32),
        ),
        in_specs=[VMEM] * 7,
        out_specs=(VMEM, VMEM),
        scratch_shapes=[pltpu.VMEM((PIECE, KV), f32)] + grads + newton,
        compiler_params=pltpu.CompilerParams(
            collective_id=1, has_side_effects=True, vmem_limit_bytes=48 * MiB
        ),
        name="weight_grad",
    )(kg, proj, gain, cos, sin, tok, peak)


def per_device(tokens, kv_weight, latent_gain, queries, out_grad, segment_ids):
    tok = tokens[0]
    c = lax.axis_index("ctx")
    positions = c * BLOCK + jnp.arange(BLOCK, dtype=jnp.int32)
    cos, sin = rope_tables(positions)
    gain = latent_gain[None]
    docs = segment_ids[0]
    lanes = jnp.arange(ROPE, dtype=jnp.int32)
    hot = (docs[:, None] == lanes[None]).astype(f32)
    qt = jnp.transpose(queries[0], (1, 2, 0))
    keys, proj, q = make_keys(tok, kv_weight.T, gain, hot, cos, sin, qt)
    keys = keys.reshape(WINDOW, PAD)
    dout = out_grad[0].reshape(BLOCK * HEADS, LAT)
    attended, kg, peak = attention(q, dout, hot, keys)
    update, top = weight_update(
        kg.reshape(SLOTS, BLOCK, KV), proj, gain, cos, sin, tok, peak
    )
    return (attended.reshape(1, BLOCK, HEADS, LAT), jnp.max(top.reshape(TILE_Q, HEADS), axis=0), update)


def solution(mesh):
    return jax.shard_map(
        per_device,
        mesh=mesh,
        in_specs=(
            P("fsdp", "ctx", None),
            P("fsdp", None),
            P(),
            P("fsdp", "ctx", None, None),
            P("fsdp", "ctx", None, None),
            P("fsdp", "ctx"),
        ),
        out_specs=(P("fsdp", "ctx", None, None), P(), P(("ctx", "fsdp"), None)),
        check_vma=False,
    )
```

```python
import functools
import math

import jax
import jax.numpy as jnp
from jax import lax
from jax.experimental import pallas as pl
from jax.experimental.pallas import tpu as pltpu
from jax.sharding import PartitionSpec as P

D = 7168
LAT = 512
ROPE = 64
HEADS = 32
NS_ITERS = 5
KV = LAT + ROPE
PAD = 640
HALF = ROPE // 2
BLOCK = 128
REACH = 8
SLOTS = REACH + 1
WINDOW = SLOTS * BLOCK
CTX = 16
FSDP = 8
SHARD = D // FSDP
PIECE = SHARD // CTX
TILE_Q = 16
ROWS = TILE_Q * HEADS
TILES = BLOCK // TILE_Q

attn_scale = 192.0 ** (-0.5)
rope_base = 50000.0
quintic_a = 3.4445
quintic_b = -4.775
quintic_c = 2.0315
BIG = -1e30
MiB = 1 << 20

MESH = pl.DeviceIdType.MESH
VMEM = pl.BlockSpec(memory_space=pltpu.VMEM)
HBM = pl.BlockSpec(memory_space=pltpu.HBM)
f32, bf16 = jnp.float32, jnp.bfloat16


def rope_tables(positions):
    ladder = jnp.arange(HALF, dtype=f32)
    freqs = jnp.power(rope_base, -2.0 * ladder / ROPE)
    angles = positions.astype(f32)[:, None] * freqs[None, :]
    return (jnp.cos(angles), jnp.sin(angles))


def nn(a, b, **kw):
    return lax.dot_general(a, b, (((1,), (0,)), ((), ())), preferred_element_type=f32, **kw)


def nt(a, b, **kw):
    return lax.dot_general(a, b, (((1,), (1,)), ((), ())), preferred_element_type=f32, **kw)


def tn(a, b, **kw):
    return lax.dot_general(a, b, (((0,), (0,)), ((), ())), preferred_element_type=f32, **kw)


class Place:
    def __init__(self):
        self.c, self.f = lax.axis_index("ctx"), lax.axis_index("fsdp")
        self.y, self.zh, self.k = self.c // 4, (self.c // 2) % 2, self.c % 2
        self.x, self.zl = self.f // 2, self.f % 2

    def at(self, x=None, y=None, zh=None, zl=None, k=None):
        x = self.x if x is None else x
        y = self.y if y is None else y
        zh = self.zh if zh is None else zh
        zl = self.zl if zl is None else zl
        k = self.k if k is None else k
        return ((y * 2 + zh) * 2 + k, x * 2 + zl)

    def ctx(self, c):
        return (c, self.f)

    def fsdp(self, f):
        return (self.c, f)


def greet(devices, others=0):
    barrier = pltpu.get_barrier_semaphore()
    for device in devices:
        pl.semaphore_signal(barrier, inc=1, device_id=device, device_id_type=MESH)
    pl.semaphore_wait(barrier, len(devices) + others)


def send(src, dst, send_sem, recv_sem, device):
    return pltpu.make_async_remote_copy(
        src_ref=src,
        dst_ref=dst,
        send_sem=send_sem,
        recv_sem=recv_sem,
        device_id=device,
        device_id_type=MESH,
    )


def keys_kernel(
    tok_hbm, w, gain, hot, cos, sin, qt, keys_out, proj_out, q_out, wall, win, tok, qin, qrow, qs, ws, wr, ks, kr
):
    me = Place()
    c, k, x = me.c, me.k, me.x
    sibling = me.at(k=1 - k)
    z_same, z_other = me.at(zl=1 - me.zl), me.at(zl=1 - me.zl, zh=1 - me.zh)
    x_up, x_down = me.at(x=(x + 1) % 4), me.at(x=(x + 3) % 4)
    later = [me.ctx((c + 2 * j) % CTX) for j in range(1, 5)]
    earlier = [me.ctx((c - 2 * j + CTX) % CTX) for j in range(1, 5)]
    greet([sibling, z_same, z_other, x_up, x_down] + later + earlier[:3])

    half = KV // 2
    quarter = half // 2
    counter = [0]

    def rows(core, q=None):
        if q is None:
            return pl.ds(pl.multiple_of(core * half, 16), half)
        return pl.ds(pl.multiple_of(core * half + q * quarter, 16), quarter)

    def post(src_f, src, core, q, device):
        i = counter[0]
        counter[0] += 1
        where = rows(core, q)
        source = w.at[where] if src is None else src.at[src_f, where]
        copy = send(source, wall.at[src_f, where], ws.at[i], wr.at[i], device)
        copy.start()
        return copy

    def shard_of(xx, zl):
        return (xx % 4) * 2 + zl

    own = me.f
    up = [post(own, None, k, 0, x_up), post(own, None, k, 1, x_up)]
    down = [post(own, None, k, 1, x_down), post(own, None, k, 0, x_down)]
    own_z = [post(own, None, k, 0, z_same), post(own, None, k, 1, z_other)]
    fetch = pltpu.make_async_copy(qt, qin, qs.at[0])
    fetch.start()
    fetch_w = pltpu.make_async_copy(w, wall.at[own], qs.at[1])
    fetch_w.start()
    fetch_tok = pltpu.make_async_copy(tok_hbm, tok, qs.at[2])
    fetch_tok.start()
    posted = up + down + own_z

    def forward(copy, shard, q):
        copy.wait_recv()
        z = post(shard, wall, k, q, (z_same, z_other)[q])
        s = post(shard, wall, k, q, sibling)
        posted.extend([z, s])
        return z, s

    def pass_on(copy, shard, q):
        copy.wait_recv()
        s = post(shard, wall, k, q, sibling)
        posted.append(s)
        return s

    other = 1 - me.zl
    f_prev, f_next, f_far = shard_of(x + 3, me.zl), shard_of(x + 1, me.zl), shard_of(x + 2, me.zl)
    o_own, o_prev, o_next, o_far = (shard_of(x + i, other) for i in (0, 3, 1, 2))

    def add(total, shard):
        return total + nt(
            tok[:, pl.ds(pl.multiple_of(shard * SHARD, 128), SHARD)], wall[shard]
        )

    fetch.wait()

    def turn(h, _):
        for lanes in range(PAD // 128):
            width = min(128, KV - lanes * 128)
            block = qin[h, lanes * 128 : lanes * 128 + width, :].astype(f32)
            if width < 128:
                block = jnp.concatenate([block, jnp.zeros((128 - width, BLOCK), f32)], axis=0)
            qrow[lanes, pl.ds(h, BLOCK, stride=HEADS), :] = block.T
        return 0

    lax.fori_loop(0, 10, turn, 0)

    prev0 = forward(up[0], f_prev, 0)
    relay_up = post(f_prev, wall, k, 0, x_up)
    next1 = forward(down[0], f_next, 1)
    relay_down = post(f_next, wall, k, 1, x_down)
    posted.extend([relay_up, relay_down])
    s_own = [pass_on(own_z[q], o_own, q) for q in range(2)]
    lax.fori_loop(10, 22, turn, 0)
    prev1 = forward(up[1], f_prev, 1)
    next0 = forward(down[1], f_next, 0)
    lax.fori_loop(22, HEADS, turn, 0)
    far0 = forward(relay_up, f_far, 0)
    far1 = forward(relay_down, f_far, 1)
    s_prev0 = pass_on(prev0[0], o_prev, 0)
    s_next1 = pass_on(next1[0], o_next, 1)
    fetch_w.wait()
    fetch_tok.wait()
    acc = nt(tok[:, pl.ds(pl.multiple_of(own * SHARD, 128), SHARD)], wall[own])

    def narrow(i, _):
        rows = pl.ds(pl.multiple_of(i * ROWS, ROWS), ROWS)
        for lanes in range(PAD // 128):
            width = min(128, KV - lanes * 128)
            q_out[rows, lanes * 128 : lanes * 128 + width] = qrow[lanes, rows, :width].astype(bf16)
        return 0

    lax.fori_loop(0, TILES, narrow, 0)
    for copy in s_own:
        copy.wait_recv()
    acc = add(acc, o_own)
    prev0[1].wait_recv()
    prev1[1].wait_recv()
    acc = add(acc, f_prev)
    next0[1].wait_recv()
    next1[1].wait_recv()
    acc = add(acc, f_next)
    s_prev1 = pass_on(prev1[0], o_prev, 1)
    s_next0 = pass_on(next0[0], o_next, 0)
    far0[1].wait_recv()
    far1[1].wait_recv()
    acc = add(acc, f_far)
    s_far0 = pass_on(far0[0], o_far, 0)
    s_far1 = pass_on(far1[0], o_far, 1)
    for shard, pair in ((o_prev, (s_prev0, s_prev1)), (o_next, (s_next0, s_next1)), (o_far, (s_far0, s_far1))):
        for copy in pair:
            copy.wait_recv()
        acc = add(acc, shard)

    compressed = acc[:, :LAT]
    inverse = lax.rsqrt(jnp.mean(compressed * compressed, axis=1, keepdims=True) + 1e-06)
    latent = compressed * inverse * gain[...]
    first, second = acc[:, LAT : LAT + HALF], acc[:, LAT + HALF :]
    mine = win.at[SLOTS - 1]
    mine[:, :LAT] = latent.astype(bf16)
    tail = jnp.concatenate(
        [
            first * cos[...] - second * sin[...],
            second * cos[...] + first * sin[...],
            hot[...],
        ],
        axis=1,
    )
    mine[:, LAT:] = tail.astype(bf16)
    proj_out[...] = acc

    def slot(distance):
        return SLOTS - 1 - distance

    spread = []
    for j in range(1, 5):
        copy = send(mine, win.at[slot(2 * j)], ks.at[j - 1], kr.at[j - 1], later[j - 1])
        copy.start()
        spread.append(copy)
    to_sibling = []

    def give(n):
        copy = send(
            win.at[slot(2 * n + 2 * k)], win.at[slot(2 * n + 1)], ks.at[4 + n], kr.at[4 + n], sibling
        )
        copy.start()
        to_sibling.append(copy)

    spread[0].wait_recv()
    give(0)
    give_next = 1
    for j in range(1, 4):
        spread[j].wait_recv()
        give(give_next)
        give_next += 1
    for copy in to_sibling:
        copy.wait_recv()
    lane = lax.broadcasted_iota(jnp.int32, (BLOCK, 128), 1)
    flag = jnp.where(lane == ROPE + 8, 1.0, 0.0)
    for d in range(REACH + 1):
        keys_out[slot(d)] = win[slot(d)]
        if d > 0:

            @pl.when(c < d)
            def _(d=d):
                keys_out[slot(d), :, LAT:] = flag.astype(bf16)

    for copy in posted + spread + to_sibling:
        copy.wait_send()


N_W = 6 + 2 + 6 * 2 + 8


def make_keys(tok, w, gain, hot, cos, sin, qt):
    return pl.pallas_call(
        keys_kernel,
        out_shape=(
            jax.ShapeDtypeStruct((SLOTS, BLOCK, PAD), bf16),
            jax.ShapeDtypeStruct((BLOCK, KV), f32),
            jax.ShapeDtypeStruct((BLOCK * HEADS, KV), bf16),
        ),
        in_specs=[HBM, HBM] + [VMEM] * 4 + [HBM],
        out_specs=(VMEM,) * 3,
        scratch_shapes=[
            pltpu.VMEM((FSDP, KV, SHARD), bf16),
            pltpu.VMEM((SLOTS, BLOCK, PAD), bf16),
            pltpu.VMEM((BLOCK, D), bf16),
            pltpu.VMEM((HEADS, KV, BLOCK), bf16),
            pltpu.VMEM((PAD // 128, BLOCK * HEADS, 128), f32),
            pltpu.SemaphoreType.DMA((3,)),
            pltpu.SemaphoreType.DMA((N_W,)),
            pltpu.SemaphoreType.DMA((N_W,)),
            pltpu.SemaphoreType.DMA((8,)),
            pltpu.SemaphoreType.DMA((8,)),
        ],
        compiler_params=pltpu.CompilerParams(
            collective_id=0, has_side_effects=True, vmem_limit_bytes=58 * MiB
        ),
        name="keys",
    )(tok, w, gain, hot, cos, sin, qt)


def attention_kernel(
    q, dout, hot, keys, att_out, grad_out, peak_out, vt, qr, s_scr, d_scr, p_scr
):
    t = pl.program_id(0)

    @pl.when(t == 0)
    def _():
        grad_out[...] = jnp.zeros_like(grad_out)
        peak_out[...] = jnp.full_like(peak_out, BIG)
        for j in range(SLOTS):
            vt[:, j * BLOCK : (j + 1) * BLOCK] = keys[j * BLOCK : (j + 1) * BLOCK, :LAT].T

    qr[:, :ROPE] = q[:, LAT:]
    lane = lax.broadcasted_iota(jnp.int32, (TILE_Q, ROPE), 1)
    qmask = jnp.where((lane < 9) & (hot[...] == 0.0), BIG, 0.0)
    spread = jnp.broadcast_to(qmask[:, None, :], (TILE_Q, HEADS, ROPE))
    qr[:, ROPE:] = spread.reshape(ROWS, ROPE).astype(bf16)

    own = slice(WINDOW - BLOCK, WINDOW)
    s_scr[...] = nt(keys[:, :LAT], q[:, :LAT]) + nt(keys[:, LAT:], qr[...])
    d_scr[...] = nt(keys[:, :LAT], dout[...])
    key = lax.broadcasted_iota(jnp.int32, (BLOCK, ROWS), 0)
    query = t * TILE_Q + lax.broadcasted_iota(jnp.int32, (BLOCK, ROWS), 1) // HEADS
    s_scr[own, :] = jnp.where(key <= query, s_scr[own, :], BIG)
    peak = jnp.max(s_scr[...], axis=0, keepdims=True)
    peak_out[...] = jnp.maximum(peak_out[...], peak * attn_scale)
    total = jnp.zeros((1, ROWS), f32)
    for j in range(SLOTS):
        at = slice(j * BLOCK, (j + 1) * BLOCK)
        e = jnp.exp((s_scr[at, :] - peak) * attn_scale)
        s_scr[at, :] = e
        total = total + jnp.sum(e, axis=0, keepdims=True)
    share = 1.0 / total
    for j in range(SLOTS):
        at = slice(j * BLOCK, (j + 1) * BLOCK)
        p_scr[at, :] = (s_scr[at, :] * share).astype(bf16)
    attended = nn(vt[...], p_scr[...]).T.astype(bf16)
    grad_out[:, :LAT] += nn(p_scr[...], dout[...])
    att_out[...] = attended
    delta = jnp.sum(dout[...].astype(f32) * attended.astype(f32), axis=1, keepdims=True)
    delta = jnp.broadcast_to(delta, (ROWS, 128)).T[:1, :]
    share = share * attn_scale
    for j in range(SLOTS):
        at = slice(j * BLOCK, (j + 1) * BLOCK)
        p_scr[at, :] = (s_scr[at, :] * share * (d_scr[at, :] - delta)).astype(bf16)
    grad_out[...] += nn(p_scr[...], q[...])


def attention(q, dout, hot, keys):
    per_tile = lambda width: pl.BlockSpec((ROWS, width), lambda t: (t, 0))
    whole = lambda *shape: pl.BlockSpec(shape, lambda t: (0, 0))
    flops = 2 * BLOCK * HEADS * WINDOW // 2 * (2 * KV + 3 * LAT)
    return pl.pallas_call(
        attention_kernel,
        grid=(TILES,),
        in_specs=[
            per_tile(KV),
            per_tile(LAT),
            pl.BlockSpec((TILE_Q, ROPE), lambda t: (t, 0)),
            whole(WINDOW, PAD),
        ],
        out_specs=[per_tile(LAT), whole(WINDOW, KV), whole(8, ROWS)],
        scratch_shapes=[
            pltpu.VMEM((LAT, WINDOW), bf16),
            pltpu.VMEM((ROWS, 128), bf16),
            pltpu.VMEM((WINDOW, ROWS), f32),
            pltpu.VMEM((WINDOW, ROWS), f32),
            pltpu.VMEM((WINDOW, ROWS), bf16),
        ],
        out_shape=(
            jax.ShapeDtypeStruct((BLOCK * HEADS, LAT), bf16),
            jax.ShapeDtypeStruct((WINDOW, KV), f32),
            jax.ShapeDtypeStruct((8, ROWS), f32),
        ),
        compiler_params=pltpu.CompilerParams(
            dimension_semantics=("arbitrary",), vmem_limit_bytes=50 * MiB
        ),
        cost_estimate=pl.CostEstimate(
            flops=flops, bytes_accessed=16 << 20, transcendentals=BLOCK * HEADS * WINDOW
        ),
        name="attention",
    )(q, dout, hot, keys)


def grads_kernel(
    kg, proj, gain, cos, sin, tok, peak, rows_out, peak_out,
    near, outbox, far, kvg, peaks, tok_in, tok_t, part, part_in, sums, sums_in,
    ns, nr, fs, fr, gs, gr, ps, pr, ss, sr, ts, tr, as_, ar,
):
    me = Place()
    c, k, f = me.c, me.k, me.f
    sibling = me.at(k=1 - k)
    back = [me.ctx((c - 2 * j + CTX) % CTX) for j in range(1, 8)]
    peers = [me.fsdp((f + s) % FSDP) for s in range(1, FSDP)]

    def slot(distance):
        return SLOTS - 1 - distance

    swaps = []
    for n in range(4):
        copy = send(kg.at[slot(2 * n + 1)], near.at[n], ns.at[n], nr.at[n], sibling)
        copy.start()
        swaps.append(copy)
    gathers = []
    for s in range(1, FSDP):
        copy = send(peak, peaks.at[s], ps.at[s - 1], pr.at[s - 1], peers[s - 1])
        copy.start()
        gathers.append(copy)
    sends = []
    own = kg[slot(0)]
    for copy in swaps:
        copy.wait_recv()

    @pl.when(k == 1)
    def _():
        for n in range(4):
            outbox[n] = near[n] + kg[slot(2 * n + 2)]

    @pl.when(k == 0)
    def _():
        for n in range(3):
            outbox[n] = near[n + 1] + kg[slot(2 * n + 2)]
        outbox[3] = kg[slot(8)]

    own = own + jnp.where(k == 0, near[0], jnp.zeros_like(own))
    for n in range(4):
        copy = send(outbox.at[n], far.at[n], fs.at[n], fr.at[n], back[n])
        copy.start()
        sends.append(copy)
    tokens = []
    for s in range(1, FSDP):
        columns = pl.ds(pl.multiple_of(((f + s) % FSDP) * SHARD, 128), SHARD)
        copy = send(tok.at[:, columns], tok_in.at[s], as_.at[s - 1], ar.at[s - 1], peers[s - 1])
        copy.start()
        tokens.append(copy)
    for copy in sends:
        copy.wait_recv()
    key_grad = own
    for n in range(4):
        key_grad = key_grad + far[n]

    compressed = proj[:, :LAT]
    inverse = lax.rsqrt(jnp.mean(compressed * compressed, axis=1, keepdims=True) + 1e-06)
    first, second = key_grad[:, LAT : LAT + HALF], key_grad[:, LAT + HALF :]
    d_first = first * cos[...] + second * sin[...]
    d_second = -first * sin[...] + second * cos[...]
    scaled = key_grad[:, :LAT] * gain[...]
    inner = jnp.mean(compressed * scaled, axis=1, keepdims=True)
    d_comp = inverse * (scaled - compressed * (inverse * inverse * inner))
    kvg[0, :, :LAT] = d_comp.astype(bf16)
    kvg[0, :, LAT:] = jnp.concatenate([d_first, d_second], axis=1).astype(bf16)
    spread = []
    for s in range(1, FSDP):
        copy = send(kvg.at[0], kvg.at[s], gs.at[s - 1], gr.at[s - 1], peers[s - 1])
        copy.start()
        spread.append(copy)
    tok_t[:, :BLOCK] = tok[:, pl.ds(pl.multiple_of(f * SHARD, 128), SHARD)].T
    for s in range(1, FSDP):
        tokens[s - 1].wait_recv()
        tok_t[:, s * BLOCK : (s + 1) * BLOCK] = tok_in[s].T
    top = peak[...]
    for s in range(1, FSDP):
        gathers[s - 1].wait_recv()
        top = jnp.maximum(top, peaks[s])
    for copy in spread:
        copy.wait_recv()

    everything = kvg[...].reshape(FSDP * BLOCK, KV)

    def multiply(n, core):
        p = 2 * n + core
        rows = pl.ds(pl.multiple_of(p * PIECE, 8), PIECE)
        return nn(tok_t[rows, :], everything)

    whole = nn(tok_t[...], everything)
    for p in range(CTX):
        part[p, :, :KV] = whole[p * PIECE : (p + 1) * PIECE]
        for r in range(8):
            part[p, r : r + 1, KV:] = top[r : r + 1, r * ROPE : (r + 1) * ROPE]
    me_n = c // 2
    order = [*range(1, CTX // 2), 0]
    piece = [(me_n - s + 8) % 8 for s in range(CTX // 2)]
    halves = {}
    for s in order:
        copy = send(part.at[2 * piece[s] + 1 - k], part_in.at[s], ss.at[s], sr.at[s], sibling)
        copy.start()
        halves[s] = copy
    totals = []
    for s in order:
        halves[s].wait_recv()
        here = part.at[2 * piece[s] + k]
        sums[s, :, :KV] = here[:, :KV] + part_in[s, :, :KV]
        sums[s, :8, KV:] = jnp.maximum(here[:8, KV:], part_in[s, :8, KV:])
        if s > 0:
            copy = send(sums.at[s], sums_in.at[s], ts.at[s], tr.at[s], back[s - 1])
            copy.start()
            totals.append(copy)
    rows = sums[0, :, :KV]
    top = sums[0, :8, KV:]
    for s in range(1, CTX // 2):
        totals[s - 1].wait_recv()
        rows = rows + sums_in[s, :, :KV]
        top = jnp.maximum(top, sums_in[s, :8, KV:])
    rows_out[...] = rows
    peak_out[...] = top
    for copy in swaps + tokens + gathers + sends + spread + list(halves.values()) + totals:
        copy.wait_send()


GRADS = 25
TRI = [(r, s) for r in range(5) for s in range(r, 5)]
PACKED = 2048
PAIRS = {3: [(0, 0), (0, 1), (1, 0)], 6: [(0, 0), (0, 1), (1, 0), (0, 2), (2, 0), (1, 1)]}


def split(value, count):
    parts = []
    for _ in range(count):
        part = value.astype(bf16)
        parts.append(part)
        value = value - part.astype(f32)
    return parts


def muon_kernel(
    g, out, pack, core_in, yz_in, x_in, acc, gram, rows_in, a_scr, left_scr, thin_scr, right_scr, ms, mr, cs, cr, ys, yr, xs, xr, xs2, xr2, ys2, yr2, cs2, cr2
):
    me = Place()
    k, x, y = me.k, me.x, me.y
    z = me.zh * 2 + me.zl
    sibling = me.at(k=1 - k)

    def plane(n):
        yy, zz = (y + n // 4) % 4, (z + n % 4) % 4
        return me.at(y=yy, zh=zz // 2, zl=zz % 2), yy * 4 + zz

    planes = [plane(n) for n in range(16)]
    line = [me.at(x=(x + s) % 4) for s in range(4)]
    give = me.f * CTX + me.c
    take = me.c * FSDP + me.f
    moving = give != take
    move = send(g, rows_in, ms.at[0], mr.at[0], (give // FSDP, give % FSDP))

    grad = g[...]
    parts = [
        jnp.concatenate([p.astype(f32), jnp.zeros((8, KV), f32)], axis=0).astype(bf16)
        for p in split(grad, 3)
    ]
    left = jnp.concatenate([parts[i] for i, _ in PAIRS[6]], axis=0)
    right = jnp.concatenate([parts[j] for _, j in PAIRS[6]], axis=0)
    local = tn(left, right)
    for i, (r, s) in enumerate(TRI[:14]):
        width = min(128, KV - s * 128)
        pack[i * 128 : i * 128 + 128, :width] = local[r * 128 : r * 128 + 128, s * 128 : s * 128 + width]
    pack[1792:1856, :64] = local[512:, 512:]
    pack[1856:, :] = jnp.zeros((PACKED - 1856, 128), f32)

    half = PACKED // 2
    unit = half // 16
    small = unit // 4

    def rows(start, size):
        return pl.ds(pl.multiple_of(start, 8), size)

    copies = []
    swap = send(pack.at[rows((1 - k) * half, half)], core_in, cs.at[0], cr.at[0], sibling)
    swap.start()

    @pl.when(moving)
    def _():
        move.start()

    @pl.when(jnp.logical_not(moving))
    def _():
        rows_in[...] = grad

    swap.wait_recv()
    acc[...] = pack[rows(k * half, half), :] + core_in[...]
    copies.append(swap)
    mine = y * 4 + z
    first = []
    for n in range(1, 16):
        device, index = planes[n]
        copy = send(acc.at[rows(index * unit, unit)], yz_in.at[n], ys.at[n], yr.at[n], device)
        copy.start()
        first.append(copy)
    total = acc[rows(mine * unit, unit), :]
    for n in range(1, 16):
        first[n - 1].wait_recv()
        total = total + yz_in[n]
    yz_in[0] = total
    second = []
    for s in range(1, 4):
        to = (x + s) % 4
        copy = send(yz_in.at[0, rows(to * small, small)], x_in.at[s], xs.at[s], xr.at[s], line[s])
        copy.start()
        second.append(copy)
    total = yz_in[0, rows(x * small, small), :]
    for s in range(1, 4):
        second[s - 1].wait_recv()
        total = total + x_in[s]
    base = k * half + mine * unit
    gram[rows(base + x * small, small), :] = total
    third = []
    for s in range(1, 4):
        there = gram.at[rows(base + x * small, small)]
        copy = send(there, there, xs2.at[s], xr2.at[s], line[s])
        copy.start()
        third.append(copy)
    for copy in third:
        copy.wait_recv()
    fourth = []
    for n in range(1, 16):
        there = gram.at[rows(base, unit)]
        copy = send(there, there, ys2.at[n], yr2.at[n], planes[n][0])
        copy.start()
        fourth.append(copy)
    for copy in fourth:
        copy.wait_recv()
    there = gram.at[rows(k * half, half)]
    last = send(there, there, cs2.at[0], cr2.at[0], sibling)
    last.start()
    last.wait_recv()
    copies += first + second + third + fourth + [last]

    blocks = {}
    for i, (r, s) in enumerate(TRI):
        if i < 14:
            blocks[r, s] = gram[i * 128 : i * 128 + 128, :]
            if r != s:
                blocks[s, r] = blocks[r, s].T
    edge = gram[1792:1856, :]
    lines = []
    for r in range(4):
        lines.append(jnp.concatenate([blocks[r, s] for s in range(5)], axis=1)[:, :KV])
    bottom = [blocks[4, s][:64] for s in range(4)] + [edge]
    lines.append(jnp.concatenate(bottom, axis=1)[:, :KV])
    full = jnp.concatenate(lines, axis=0)
    row = lax.broadcasted_iota(jnp.int32, (KV, KV), 0)
    col = lax.broadcasted_iota(jnp.int32, (KV, KV), 1)
    diagonal = row == col
    squares = jnp.sum(jnp.where(diagonal, full, 0.0))
    norm = jnp.sqrt(jnp.full((1, 1), squares, f32)) + 1e-07
    inv = 1.0 / norm
    a_scr[...] = full * inv * inv

    @pl.when(moving)
    def _():
        move.wait_recv()

    out[...] = rows_in[...] * inv

    def lay_left(ref, value, terms):
        parts = split(value, 3 if terms == 6 else 2)
        for t, (i, _) in enumerate(PAIRS[terms]):
            ref[:, t * LAT : (t + 1) * LAT] = parts[i][:, :LAT]
            at = terms * LAT + t * ROPE
            ref[:, at : at + ROPE] = parts[i][:, LAT:]

    def lay_right(value, terms):
        parts = split(value, 3 if terms == 6 else 2)
        for t, (_, j) in enumerate(PAIRS[terms]):
            right_scr[t * LAT : (t + 1) * LAT, :] = parts[j][:LAT]
            at = terms * LAT + t * ROPE
            right_scr[at : at + ROPE, :] = parts[j][LAT:]

    def symmetric(terms):
        size = terms * KV
        wide = nn(left_scr[:, :size], right_scr[:size, :LAT])
        corner = nn(left_scr[LAT:, :size], right_scr[:size, LAT:])
        return jnp.concatenate([wide, jnp.concatenate([wide[LAT:].T, corner], axis=0)], axis=1)

    def mix(terms):
        a = a_scr[...]
        lay_left(left_scr, a, terms)
        lay_right(a, terms)
        mixing = quintic_b * a + quintic_c * symmetric(terms)
        lay_right(mixing, terms)
        lay_left(thin_scr, out[...], terms)
        size = terms * KV
        out[...] = quintic_a * out[...] + nn(thin_scr[:, :size], right_scr[:size, :])

    def advance(terms):
        b = quintic_a * a_scr[...] + symmetric(terms)
        lay_left(left_scr, b, terms)
        a_scr[...] = quintic_a * b + symmetric(terms)

    mix(6)
    advance(6)

    def iteration(step, _):
        mix(3)

        @pl.when(step < NS_ITERS - 1)
        def _():
            advance(3)

        return 0

    lax.fori_loop(1, NS_ITERS, iteration, 0)
    iterate = out[...]
    out[...] = iterate * (0.2 * math.sqrt(D))

    @pl.when(moving)
    def _():
        move.wait_send()

    for copy in copies:
        copy.wait_send()


def update_kernel(kg, proj, gain, cos, sin, tok, peak, out, peak_out, rows, *scratch):
    me = Place()
    give, take = me.f * CTX + me.c, me.c * FSDP + me.f
    moving = give != take

    @pl.when(moving)
    def _():
        pl.semaphore_signal(
            pltpu.get_barrier_semaphore(),
            inc=1,
            device_id=(take % CTX, take // CTX),
            device_id_type=MESH,
        )

    c, x, y, z = me.c, me.x, me.y, me.zh * 2 + me.zl
    friends = [me.at(k=1 - me.k)]
    friends += [me.ctx((c - 2 * j + CTX) % CTX) for j in range(1, 8)]
    friends += [me.fsdp((me.f + s) % FSDP) for s in range(1, FSDP)]
    for n in range(1, 16):
        zz = (z + n % 4) % 4
        friends.append(me.at(y=(y + n // 4) % 4, zh=zz // 2, zl=zz % 2))
    friends += [me.at(x=(x + s) % 4) for s in range(1, 4)]
    greet(friends, jnp.where(moving, 1, 0))
    grads_kernel(kg, proj, gain, cos, sin, tok, peak, rows, peak_out, *scratch[:GRADS])
    muon_kernel(rows, out, *scratch[GRADS:])


def weight_update(kg, proj, gain, cos, sin, tok, peak):
    half = PACKED // 2
    dma = lambda sizes: [pltpu.SemaphoreType.DMA((n,)) for n in sizes]
    grads = [
        pltpu.VMEM((4, BLOCK, KV), f32),
        pltpu.VMEM((4, BLOCK, KV), f32),
        pltpu.VMEM((4, BLOCK, KV), f32),
        pltpu.VMEM((FSDP, BLOCK, KV), bf16),
        pltpu.VMEM((FSDP, 8, ROWS), f32),
        pltpu.VMEM((FSDP, BLOCK, SHARD), bf16),
        pltpu.VMEM((SHARD, FSDP * BLOCK), bf16),
        pltpu.VMEM((CTX, PIECE, PAD), f32),
        pltpu.VMEM((CTX // 2, PIECE, PAD), f32),
        pltpu.VMEM((CTX // 2, PIECE, PAD), f32),
        pltpu.VMEM((CTX // 2, PIECE, PAD), f32),
    ] + dma([4, 4, 4, 4, 7, 7, 7, 7, 8, 8, 8, 8, 7, 7])
    assert len(grads) == GRADS
    newton = [
        pltpu.VMEM((PACKED, 128), f32),
        pltpu.VMEM((half, 128), f32),
        pltpu.VMEM((16, half // 16, 128), f32),
        pltpu.VMEM((4, half // 64, 128), f32),
        pltpu.VMEM((half, 128), f32),
        pltpu.VMEM((PACKED, 128), f32),
        pltpu.VMEM((PIECE, KV), f32),
        pltpu.VMEM((KV, KV), f32),
        pltpu.VMEM((KV, 6 * KV), bf16),
        pltpu.VMEM((PIECE, 6 * KV), bf16),
        pltpu.VMEM((6 * KV, KV), bf16),
    ] + dma([1, 1, 1, 1, 16, 16, 4, 4, 4, 4, 16, 16, 1, 1])
    return pl.pallas_call(
        update_kernel,
        out_shape=(
            jax.ShapeDtypeStruct((PIECE, KV), f32),
            jax.ShapeDtypeStruct((8, ROPE), f32),
        ),
        in_specs=[VMEM] * 7,
        out_specs=(VMEM, VMEM),
        scratch_shapes=[pltpu.VMEM((PIECE, KV), f32)] + grads + newton,
        compiler_params=pltpu.CompilerParams(
            collective_id=1, has_side_effects=True, vmem_limit_bytes=48 * MiB
        ),
        name="weight_grad",
    )(kg, proj, gain, cos, sin, tok, peak)


def per_device(tokens, kv_weight, latent_gain, queries, out_grad, segment_ids):
    tok = tokens[0]
    c = lax.axis_index("ctx")
    positions = c * BLOCK + jnp.arange(BLOCK, dtype=jnp.int32)
    cos, sin = rope_tables(positions)
    gain = latent_gain[None]
    docs = segment_ids[0]
    lanes = jnp.arange(ROPE, dtype=jnp.int32)
    hot = (docs[:, None] == lanes[None]).astype(f32)
    qt = jnp.transpose(queries[0], (1, 2, 0))
    keys, proj, q = make_keys(tok, kv_weight.T, gain, hot, cos, sin, qt)
    keys = keys.reshape(WINDOW, PAD)
    dout = out_grad[0].reshape(BLOCK * HEADS, LAT)
    attended, kg, peak = attention(q, dout, hot, keys)
    update, top = weight_update(
        kg.reshape(SLOTS, BLOCK, KV), proj, gain, cos, sin, tok, peak
    )
    return (attended.reshape(1, BLOCK, HEADS, LAT), jnp.max(top.reshape(TILE_Q, HEADS), axis=0), update)


def solution(mesh):
    return jax.shard_map(
        per_device,
        mesh=mesh,
        in_specs=(
            P("fsdp", "ctx", None),
            P("fsdp", None),
            P(),
            P("fsdp", "ctx", None, None),
            P("fsdp", "ctx", None, None),
            P("fsdp", "ctx"),
        ),
        out_specs=(P("fsdp", "ctx", None, None), P(), P(("ctx", "fsdp"), None)),
        check_vma=False,
    )
```
